256 devices in a mesh: wide: 32 (over x, z), narrow: 8 (over y, core).
Axes of the slice: x: 4, y: 4, z: 8, core: 2. Of those that a mesh axis runs over, the one named last changes fastest.
Arguments:
- hidden: bfloat16 [8192, 5120], P('wide', 'narrow'), may hold values from -6 to 6
- resid: bfloat16 [8192, 5120], P('wide'), may hold values from -6 to 6
- w_out: bfloat16 [5120, 5120], P('narrow', 'wide'), may hold values from -0.078125 to 0.078125
- key_gain: bfloat16 [5120], P('narrow'), may hold values from 0.099609375 to 1.8984375
- cluster_ids: int32 [8192], P('wide'), may hold values from 0 to 32767, as said below
- centroids: bfloat16 [32768, 5120], P(('wide', 'narrow')), may hold values from -6 to 6
- rotation: bfloat16 [5120, 5120], P(None, 'narrow'), may hold values from -0.078125 to 0.078125
Outputs:
- rotated: bfloat16 [32768, 5120], P('wide', 'narrow')
The draws below stay inside these ranges and needn't reach their ends.
Inputs may be any that keep to these rules, and one draw needn't show every extreme that they name: `cluster_ids`: in each block of 256 tokens at most 32 tokens have clusters of one owner (owner = id // 1024); one owner, the same for every block, gets exactly 32 tokens from every block; the other 224 tokens of a block are spread as evenly as possible over the other owners, so their counts differ by at most one.
All inputs are finite; a program needn't handle non-finite values.
Results may differ from the reference program's by a relative error of at most 0.0055.
Values may be sent and summed in bfloat16 or wider, within the bound.
No kernel may reach another device: no remote copies, remote signals or barrier semaphores. Data moves between devices by JAX's collectives and lax.ppermute only.
A program may use at most 64 MiB of HBM per device.

```python
import jax
import jax.numpy as jnp
from jax import lax

D = 5120
TOK_DEV = 256
CL_DEV = 1024
TOKENS = 8192
CLUSTERS = 32768
N_WIDE = 32


def draw_cluster_ids(key, part):
    key = jax.random.fold_in(key, 7)
    capacity = 4 * TOK_DEV // N_WIDE
    hot_owner = jax.random.randint(jax.random.fold_in(key, 1), (), 0, N_WIDE)
    offsets = jax.random.randint(jax.random.fold_in(key, 2), (N_WIDE, 1), 0, N_WIDE - 1)
    position = jnp.arange(TOK_DEV, dtype=jnp.int32)[None, :]
    others = (hot_owner + 1 + (position - capacity + offsets) % (N_WIDE - 1)) % N_WIDE
    base = jnp.where(position < capacity, hot_owner, others)
    base = jnp.broadcast_to(base, (N_WIDE, TOK_DEV)).astype(jnp.int32)
    perm_keys = jax.random.split(jax.random.fold_in(key, 3), N_WIDE)
    perms = jax.vmap(lambda k: jax.random.permutation(k, TOK_DEV))(perm_keys)
    owner_of = jnp.take_along_axis(base, perms, axis=1).reshape(-1)
    first = jax.random.randint(jax.random.fold_in(key, 4), (TOKENS,), 0, CL_DEV)
    second = jax.random.randint(jax.random.fold_in(key, 5), (TOKENS,), 0, CL_DEV)
    shift = jax.random.randint(jax.random.fold_in(key, 6), (), 0, CL_DEV)
    local_id = (jnp.minimum(first, second) + shift) % CL_DEV
    return (owner_of * CL_DEV + local_id).astype(jnp.int32)


def steps_of(rng, dims, shards, smallest, high):
    factor_of = 1.0
    for dim, parts in shards:
        steps = jax.random.uniform(jax.random.fold_in(jax.random.fold_in(rng, 6), dim), (parts,), jnp.float32, smallest / len(shards), high / len(shards))
        factor_of = factor_of * jnp.repeat(jnp.exp(steps), dims[dim] // parts).reshape((-1,) + (1,) * (len(dims) - 1 - dim))
    return factor_of


def bell_draw(stream_key, shape, spread, most, cuts=(), held_as=jnp.bfloat16):
    result = spread * jax.random.normal(stream_key, shape, jnp.float32)
    if cuts:
        result = result * steps_of(stream_key, shape, cuts, -0.22, 0.18)
    return jnp.clip(result, -most, most).astype(held_as)


def setup_inputs(seed: int = 0) -> dict:
    streams_of = jax.random.split(jax.random.key(seed), 8)
    hidden = bell_draw(streams_of[0], (TOKENS, D), 1.0, 6.0, ((0, 32), (1, 8)))
    resid = bell_draw(streams_of[1], (TOKENS, D), 1.0, 6.0, ((0, 32),))
    w_out = bell_draw(streams_of[2], (D, D), D ** -0.5, 0.078125, ((0, 8), (1, 32)))
    key_gain = jnp.clip(1.0 + 0.18 * jax.random.normal(streams_of[3], (D,), jnp.float32), 0.099609375, 1.8984375).astype(jnp.bfloat16)
    cluster_ids = draw_cluster_ids(jax.random.fold_in(streams_of[7], 71), 0)
    centroids = bell_draw(streams_of[5], (CLUSTERS, D), 1.0, 6.0, ((0, 256),))
    rotation = bell_draw(streams_of[6], (D, D), D ** -0.5, 0.078125, ((1, 8),))
    return {"hidden": hidden, "resid": resid, "w_out": w_out, "key_gain": key_gain, "cluster_ids": cluster_ids, "centroids": centroids, "rotation": rotation}


EPS = 1e-05

def reference(hidden, resid, w_out, key_gain, cluster_ids, centroids, rotation):
    projected = jnp.dot(hidden, w_out, preferred_element_type=jnp.float32)
    stream = resid.astype(jnp.float32) + projected
    norm_scale = lax.rsqrt(lax.optimization_barrier(jnp.mean(stream * stream, axis=1, keepdims=True)) + EPS)
    key_rows = (stream * norm_scale * key_gain.astype(jnp.float32)).astype(jnp.bfloat16)
    capacity = 4 * TOK_DEV // N_WIDE
    owner_of = cluster_ids // CL_DEV
    blocks = owner_of.reshape(N_WIDE, TOK_DEV)
    owners = jnp.arange(N_WIDE, dtype=jnp.int32)
    onehot = (blocks[:, :, None] == owners[None, None, :]).astype(jnp.int32)
    slot_rank = lax.optimization_barrier(jnp.sum((jnp.cumsum(onehot, axis=1) - onehot) * onehot, axis=2))
    source = owners[:, None]
    target = (blocks * (N_WIDE * capacity) + source * capacity + slot_rank).reshape(-1).astype(jnp.int32)
    total_slots = N_WIDE * N_WIDE * capacity
    packed = jnp.zeros((total_slots, D), jnp.bfloat16).at[target].set(key_rows)
    packed_ids = jnp.full((total_slots,), -1, jnp.int32).at[target].set(cluster_ids.astype(jnp.int32))
    filled = packed_ids >= 0
    centre_rows = jnp.take(centroids, jnp.clip(packed_ids, 0, CLUSTERS - 1), axis=0).astype(jnp.float32)
    residual = (packed.astype(jnp.float32) - jnp.where(filled[:, None], centre_rows, 0.0)).astype(jnp.bfloat16)
    rotated = jnp.dot(residual, rotation, preferred_element_type=jnp.float32)
    return rotated.astype(jnp.bfloat16)
```

```python
import jax
import jax.numpy as jnp
from jax import lax
from jax.sharding import Mesh, PartitionSpec as P

CL_DEV = 1024
EPS = 1e-05
NX, NZ, NY, NC = 4, 8, 4, 2
WIDE = ("x", "z")
NARROW = ("y", "c")
BF = jnp.bfloat16
F32 = jnp.float32


def shifted(a, axis, n, h):
    return lax.ppermute(a, axis, [(i, (i + h) % n) for i in range(n)])


def pick(a, i, axis=0):
    return lax.dynamic_index_in_dim(a, i, axis, keepdims=False)


def per_device(hidden, resid, w_out, key_gain, cluster_ids, centroids, rotation):
    xi, zi, yi, ci = (lax.axis_index(a) for a in ("x", "z", "y", "c"))
    ni = yi * NC + ci
    wi = xi * NZ + zi
    tokens, width = hidden.shape
    n_wide, n_narrow = NX * NZ, NY * NC
    d = width * n_narrow
    cap = 4 * tokens // n_wide
    slots = n_wide * cap
    rows = tokens // n_narrow
    cols = w_out.shape[1]

    owner_of = cluster_ids // CL_DEV
    onehot = (owner_of[:, None] == jnp.arange(n_wide, dtype=jnp.int32)[None, :]).astype(jnp.int32)
    rank = jnp.sum((jnp.cumsum(onehot, axis=0) - onehot) * onehot, axis=1)
    target = owner_of * cap + rank
    slot_of = target[:, None] == jnp.arange(slots, dtype=jnp.int32)[None, :]
    send_ids = jnp.sum(jnp.where(slot_of, cluster_ids[:, None] + 1, 0), axis=0) - 1
    got_ids = lax.all_to_all(send_ids, WIDE, 0, 0, tiled=True)

    w_t = w_out.T
    w_parts = [w_t] + [shifted(w_t, "z", NZ, -h) for h in (1, 2, 3, 4, 5, 6, 7)]
    h_parts = [hidden] + [shifted(hidden, "x", NX, h) for h in (1, 2, 3)]
    w_all = jnp.zeros((NZ * cols, width), BF)
    for h, part in enumerate(w_parts):
        w_all = lax.dynamic_update_slice(w_all, part, (((zi + h) % NZ) * cols, 0))
    wide_cols = NZ * cols

    cent_tile = lax.all_to_all(centroids, NARROW, split_axis=1, concat_axis=0, tiled=True)
    local_id = jnp.where(got_ids >= 0, got_ids - wi * CL_DEV, -1)
    choose = (local_id[:, None] == jnp.arange(CL_DEV, dtype=jnp.int32)[None, :]).astype(BF)
    cent_send = jnp.dot(choose, cent_tile, preferred_element_type=F32).astype(BF)
    cent_slots = lax.all_to_all(cent_send, WIDE, 0, 0, tiled=True)
    cent_tok = jnp.dot(slot_of.astype(BF), cent_slots, preferred_element_type=F32).astype(BF)
    cent_rows = lax.all_to_all(cent_tok.reshape(n_narrow, rows, width), NARROW, 0, 0, tiled=True)
    cent_rows = cent_rows.transpose(1, 0, 2).reshape(rows, d)

    partial = jnp.stack(
        [
            lax.dot_general(p, w_all, (((1,), (1,)), ((), ())), preferred_element_type=F32)
            for p in h_parts
        ]
    ).astype(BF)
    partial = partial.reshape(NX, NY, NC, rows, wide_cols)
    other = shifted(pick(partial, 1 - ci, 2), "c", NC, 1)
    pair = (pick(partial, ci, 2).astype(F32) + other.astype(F32)).astype(BF)
    total = pick(pair, yi, 1).astype(F32)
    for h in (1, 2, 3):
        total = total + shifted(pick(pair, (yi + h) % NY, 1), "y", NY, h).astype(F32)
    total = total.astype(BF)
    back = jnp.stack([total[0]] + [shifted(total[h], "x", NX, -h) for h in (1, 2, 3)])
    projected = jnp.concatenate([pick(back, (j - xi) % NX) for j in range(NX)], axis=1)

    stream = (
        lax.dynamic_slice_in_dim(resid, ni * rows, rows, 0).astype(F32) + projected.astype(F32)
    )
    norm_scale = lax.rsqrt(jnp.mean(stream * stream, axis=1, keepdims=True) + EPS)
    gain = lax.all_gather(key_gain, NARROW, axis=0, tiled=True)
    key_rows = (stream * norm_scale * gain.astype(F32)[None, :]).astype(BF)
    residual = (key_rows.astype(F32) - cent_rows.astype(F32)).astype(BF)

    same = jnp.stack([residual] + [shifted(residual, "y", NY, h) for h in (1, 2, 3)])
    both = [same, shifted(same, "c", NC, 1)]
    k_of = jnp.arange(NC)[:, None, None]
    h_of = jnp.arange(NY)[None, :, None]
    r_of = jnp.arange(rows)[None, None, :]
    token_of = (((yi - h_of) % NY) * NC + (ci + k_of) % NC) * rows + r_of
    rotated = jnp.concatenate(
        [
            jnp.dot(b.reshape(NY * rows, d), rotation, preferred_element_type=F32).astype(BF)
            for b in both
        ]
    )
    place = jnp.take(target, token_of.reshape(-1))
    pack = (jnp.arange(slots, dtype=jnp.int32)[:, None] == place[None, :]).astype(BF)
    packed = jnp.dot(pack, rotated, preferred_element_type=F32).astype(BF)
    return lax.all_to_all(packed, WIDE, 0, 0, tiled=True)


def solution(mesh):
    grid = Mesh(mesh.devices.reshape(NX, NZ, NY, NC), ("x", "z", "y", "c"))
    placed = (
        P(WIDE, NARROW),
        P(WIDE, None),
        P(NARROW, WIDE),
        P(NARROW),
        P(WIDE),
        P(WIDE + NARROW, None),
        P(None, NARROW),
    )
    return jax.shard_map(
        per_device, mesh=grid, in_specs=placed, out_specs=P(WIDE, NARROW), check_vma=False
    )
```

```python
import jax
import jax.numpy as jnp
from jax import lax
from jax.sharding import Mesh, PartitionSpec as P

CL_DEV = 1024
EPS = 1e-05
NX, NZ, NY, NC = 4, 8, 4, 2
WIDE = ("x", "z")
NARROW = ("y", "c")
NN = NY * NC
NW = NX * NZ
BF = jnp.bfloat16
F32 = jnp.float32
I32 = jnp.int32


def shifted(a, axis, n, h):
    return lax.ppermute(a, axis, [(i, (i + h) % n) for i in range(n)])


def pick(a, i, axis=0):
    return lax.dynamic_index_in_dim(a, i, axis, keepdims=False)


def iota(shape, dim):
    return lax.broadcasted_iota(I32, shape, dim)


def choose_rows(onehot, a):
    return jnp.dot(onehot.astype(BF), a, preferred_element_type=F32).astype(BF)


def places(ids, cap, per_owner):
    owner = ids // CL_DEV
    onehot = (owner[:, None] == iota((1, NW), 1)).astype(I32)
    rank = jnp.sum((jnp.cumsum(onehot, axis=0) - onehot) * onehot, axis=1)
    count = jnp.sum(onehot, axis=0)
    hot = jnp.argmax(count).astype(I32)
    short = count < per_owner
    nth = jnp.cumsum(short.astype(I32)) - short.astype(I32)
    gap = jnp.where(short, nth % per_owner, per_owner)
    n_of = rank + (rank >= jnp.sum(onehot * gap[None, :], axis=1)).astype(I32)
    surplus = rank >= per_owner
    j = rank - per_owner
    host = jnp.sum(
        jnp.where(short[None, :] & (nth[None, :] == j[:, None]), iota((1, NW), 1), 0), axis=1
    )
    place = jnp.where(surplus, (j % per_owner) * NW + host, n_of * NW + owner)
    cell = owner * cap + jnp.where(surplus, rank, n_of)
    return place, cell, hot, short, nth


def gather_narrow(a):
    same = jnp.stack([a] + [shifted(a, "y", NY, h) for h in (1, 2, 3)])
    return same, shifted(same, "c", NC, 1)


def per_device(hidden, resid, w_out, key_gain, cluster_ids, centroids, rotation):
    xi, zi, yi, ci = (lax.axis_index(a) for a in ("x", "z", "y", "c"))
    ni = yi * NC + ci
    wi = xi * NZ + zi
    tokens, width = hidden.shape
    d = width * NN
    cap = 4 * tokens // NW
    cols = w_out.shape[1]
    wide_cols = NZ * cols
    extra = cap - NN
    per_n = extra // NN

    w_t = w_out.T
    up, down = [w_t], [w_t]
    for _ in range(3):
        up.append(shifted(up[-1], "z", NZ, 1))
        down.append(shifted(down[-1], "z", NZ, -1))
    far = [
        shifted(up[-1][: cols // 2], "z", NZ, 1),
        shifted(down[-1][cols // 2 :], "z", NZ, -1),
    ]

    place, cell, hot, short, nth = places(cluster_ids, cap, NN)
    hidden_p = choose_rows(iota((tokens, 1), 0) == place[None, :], hidden)
    h_parts = [hidden_p] + [shifted(hidden_p, "x", NX, h) for h in (1, 2, 3)]

    cell_of = cell[:, None] == iota((1, NW * cap), 1)
    send_ids = jnp.sum(jnp.where(cell_of, cluster_ids[:, None] + 1, 0), axis=0) - 1
    got_ids = lax.all_to_all(send_ids, WIDE, 0, 0, tiled=True).reshape(NW, cap)

    cent_tile = lax.all_to_all(centroids, NARROW, split_axis=1, concat_axis=0, tiled=True)
    local = jnp.where(got_ids >= 0, got_ids - wi * CL_DEV, -1)
    clusters = iota((1, CL_DEV), 1)
    cent_own = choose_rows(local[:, :NN].T.reshape(-1, 1) == clusters, cent_tile)
    cent_out = choose_rows(local[:, NN:].reshape(-1, 1) == clusters, cent_tile)
    cent_in = pick(lax.all_to_all(cent_out.reshape(NW, extra, width), WIDE, 0, 0, tiled=True), hot)
    cent_both = jnp.concatenate(
        [
            cent_own.reshape(NN, NW, width),
            cent_in.reshape(per_n, NN, width).transpose(1, 0, 2),
            jnp.broadcast_to(key_gain, (NN, 8 - per_n, width)),
        ],
        axis=1,
    )
    cent_both = lax.all_to_all(cent_both, NARROW, 0, 0, tiled=True)
    cent_both = cent_both.transpose(1, 0, 2).reshape(NW + 8, d)
    cent_rows, cent_extra, gain = cent_both[:NW], cent_both[NW:], cent_both[NW + per_n]

    w_all = jnp.zeros((wide_cols, width), BF)
    for h in range(4):
        w_all = lax.dynamic_update_slice(w_all, up[h], (((zi - h) % NZ) * cols, 0))
        if h:
            w_all = lax.dynamic_update_slice(w_all, down[h], (((zi + h) % NZ) * cols, 0))
    w_all = lax.dynamic_update_slice(
        w_all, jnp.concatenate(far), (((zi + 4) % NZ) * cols, 0)
    )
    partial = jnp.stack(
        [
            lax.dot_general(p, w_all, (((1,), (1,)), ((), ())), preferred_element_type=F32)
            for p in h_parts
        ]
    ).astype(BF)
    partial = partial.reshape(NX, NY, NC, NW, wide_cols)
    other = shifted(pick(partial, 1 - ci, 2), "c", NC, 1)
    pair = (pick(partial, ci, 2).astype(F32) + other.astype(F32)).astype(BF)
    total = pick(pair, yi, 1).astype(F32)
    for h in (1, 2, 3):
        total = total + shifted(pick(pair, (yi + h) % NY, 1), "y", NY, h).astype(F32)
    total = total.astype(BF)
    back = jnp.stack([total[0]] + [shifted(total[h], "x", NX, -h) for h in (1, 2, 3)])
    projected = jnp.concatenate([pick(back, (j - xi) % NX) for j in range(NX)], axis=1)

    own_place = ni * NW + iota((NW, 1), 0) == place[None, :]
    resid_rows = choose_rows(own_place, resid)
    stream = resid_rows.astype(F32) + projected.astype(F32)
    norm_scale = lax.rsqrt(jnp.mean(stream * stream, axis=1, keepdims=True) + EPS)
    key_rows = (stream * norm_scale * gain.astype(F32)[None, :]).astype(BF)

    n_of = ((yi - iota((NC, NY, 1), 1)) % NY) * NC + (ci + iota((NC, NY, 1), 0)) % NC

    q = iota((8, 1), 0)
    from_host = short[None, :] & (nth[None, :] == q * NN + ni) & (q < per_n)
    key_extra = choose_rows(from_host, key_rows)
    res_extra = (key_extra.astype(F32) - cent_extra.astype(F32)).astype(BF)
    ext = jnp.concatenate(gather_narrow(res_extra)).reshape(NN * 8, d)
    ext = jnp.dot(ext, rotation, preferred_element_type=F32).astype(BF)
    ext_j = (iota((NC, NY, 8), 2) * NN + n_of).reshape(1, -1)
    ext = choose_rows(ext_j == iota((extra, 1), 0), ext)
    ext_z = jnp.stack([ext] + [shifted(ext, "z", NZ, -h) for h in range(1, NZ)])
    ext_z = jnp.concatenate([pick(ext_z, (j - zi) % NZ) for j in range(NZ)])
    ext_x = jnp.stack([ext_z] + [shifted(ext_z, "x", NX, -h) for h in range(1, NX)])
    ext_all = jnp.concatenate([pick(ext_x, (j - xi) % NX) for j in range(NX)])
    ext_all = ext_all.reshape(NW, extra, width)

    got = lax.all_to_all(key_rows.reshape(NW, NN, width), WIDE, 0, 0, tiled=True).reshape(NW, d)
    filled = pick(got_ids, ni, 1) >= 0
    residual = jnp.where(filled[:, None], got.astype(F32) - cent_rows.astype(F32), 0.0).astype(BF)
    rotated = jnp.concatenate(
        [
            jnp.dot(b.reshape(NY * NW, d), rotation, preferred_element_type=F32).astype(BF)
            for b in gather_narrow(residual)
        ]
    )
    gap = jnp.min(jnp.where(got_ids[:, :NN] < 0, iota((1, NN), 1), NN), axis=1)
    rank = iota((1, NN), 1)
    from_n = (rank + (rank >= gap[:, None]).astype(I32)).reshape(-1, 1)
    from_s = (iota((NW, NN), 0)).reshape(-1, 1)
    row_n = jnp.broadcast_to(n_of, (NC, NY, NW)).reshape(1, -1)
    row_s = iota((NC, NY, NW), 2).reshape(1, -1)
    ordinary = choose_rows((from_n == row_n) & (from_s == row_s), rotated)
    out = jnp.concatenate(
        [ordinary.reshape(NW, NN, width), jnp.where(wi == hot, ext_all, 0)], axis=1
    )
    return out.reshape(NW * cap, width)


def solution(mesh):
    grid = Mesh(mesh.devices.reshape(NX, NZ, NY, NC), ("x", "z", "y", "c"))
    placed = (
        P(WIDE, NARROW),
        P(WIDE, None),
        P(NARROW, WIDE),
        P(NARROW),
        P(WIDE),
        P(WIDE + NARROW, None),
        P(None, NARROW),
    )
    return jax.shard_map(
        per_device, mesh=grid, in_specs=placed, out_specs=P(WIDE, NARROW), check_vma=False
    )
```

```python
import jax
import jax.numpy as jnp
from jax import lax
from jax.experimental import pallas as pl
from jax.experimental.pallas import tpu as pltpu
from jax.sharding import Mesh, PartitionSpec as P

CL_DEV = 1024
EPS = 1e-05
NX, NZ, NY, NC = 4, 8, 4, 2
WIDE = ("x", "z")
NARROW = ("y", "c")
NN = NY * NC
NW = NX * NZ
BF = jnp.bfloat16
F32 = jnp.float32
I32 = jnp.int32


def shifted(a, axis, n, h):
    return lax.ppermute(a, axis, [(i, (i + h) % n) for i in range(n)])


def pick(a, i, axis=0):
    return lax.dynamic_index_in_dim(a, i, axis, keepdims=False)


def iota(shape, dim):
    return lax.broadcasted_iota(I32, shape, dim)


def choose_rows(onehot, a):
    return jnp.dot(onehot.astype(BF), a, preferred_element_type=F32).astype(BF)


def places(ids, cap, per_owner):
    owner = ids // CL_DEV
    onehot = (owner[:, None] == iota((1, NW), 1)).astype(I32)
    rank = jnp.sum((jnp.cumsum(onehot, axis=0) - onehot) * onehot, axis=1)
    count = jnp.sum(onehot, axis=0)
    hot = jnp.argmax(count).astype(I32)
    short = count < per_owner
    nth = jnp.cumsum(short.astype(I32)) - short.astype(I32)
    gap = jnp.where(short, nth % per_owner, per_owner)
    n_of = rank + (rank >= jnp.sum(onehot * gap[None, :], axis=1)).astype(I32)
    surplus = rank >= per_owner
    j = rank - per_owner
    host = jnp.sum(
        jnp.where(short[None, :] & (nth[None, :] == j[:, None]), iota((1, NW), 1), 0), axis=1
    )
    place = jnp.where(surplus, (j % per_owner) * NW + host, n_of * NW + owner)
    cell = owner * cap + jnp.where(surplus, rank, n_of)
    return place, cell, hot, short, nth


VMEM = pl.BlockSpec(memory_space=pltpu.VMEM)
SMEM = pl.BlockSpec(memory_space=pltpu.SMEM)
ANY = pl.BlockSpec(memory_space=pl.ANY)
PARAMS = pltpu.CompilerParams(vmem_limit_bytes=48 * 1024 * 1024)


def like(shape, dtype=BF):
    return jax.ShapeDtypeStruct(shape, dtype)


def at(i, size, step):
    return pl.ds(pl.multiple_of(i * size, step), size)


def project(at_ref, *refs):
    h_refs, up, down, far = refs[:4], refs[4:8], refs[8:11], refs[11:13]
    keep, send, w_all, acc = refs[15:]
    z, y, c = at_ref[1], at_ref[2], at_ref[3]
    cols = up[0].shape[0]
    for h in range(4):
        w_all[at(lax.rem(z + NZ - h, NZ), cols, 16), :] = up[h][...]
        if h:
            w_all[at(lax.rem(z + h, NZ), cols, 16), :] = down[h - 1][...]
    across = lax.rem(z + 4, NZ) * cols
    w_all[pl.ds(pl.multiple_of(across, 16), cols // 2), :] = far[0][...]
    w_all[pl.ds(pl.multiple_of(across + cols // 2, 16), cols // 2), :] = far[1][...]
    for h in range(NX):
        acc[...] = lax.dot_general(
            h_refs[h][...], w_all[...], (((1,), (1,)), ((), ())), preferred_element_type=F32
        )
        for g in range(NY):
            n = lax.rem(y + g, NY) * NC
            keep[g, h] = acc[at(n + c, NW, 32), :].astype(BF)
            send[g, h] = acc[at(n + 1 - c, NW, 32), :].astype(BF)


def add_pair(keep, other, *outs):
    for g in range(NY):
        outs[g][...] = (keep[g].astype(F32) + other[g].astype(F32)).astype(BF)


def add_four(*refs):
    for h in range(NX):
        total = refs[0][h].astype(F32)
        for g in range(1, NY):
            total = total + refs[g][h].astype(F32)
        refs[NY + 1 + h][...] = total.astype(BF)


def normalize(at_ref, b0, b1, b2, b3, resid, cents, from_host, keys, extra, stream):
    x = at_ref[0]
    span = b0.shape[1]
    width = cents.shape[2]
    for h, b in enumerate((b0, b1, b2, b3)):
        where = at(lax.rem(x + h, NX), span, 128)
        stream[:, where] = resid[:, where].astype(F32) + b[...].astype(F32)
    value = stream[...]
    scale = lax.rsqrt(jnp.mean(value * value, axis=1, keepdims=True) + EPS)
    for n in range(NN):
        part = slice(n * width, (n + 1) * width)
        tail = cents[n, NW:, :].astype(F32)
        key = (stream[:, part] * scale * tail[7:8]).astype(BF)
        keys[:, part] = key
        chosen = jnp.dot(from_host[...], key, preferred_element_type=F32)
        extra[:, part] = (chosen - tail).astype(BF)


def subtract(keys, cents, filled, out):
    width = cents.shape[2]
    for n in range(NN):
        part = slice(n * width, (n + 1) * width)
        diff = keys[:, part].astype(F32) - cents[n, :NW, :].astype(F32)
        out[:, part] = jnp.where(filled[...] > 0, diff, 0.0).astype(BF)


def accumulate(parts, rot, acc):
    lhs = jnp.concatenate([p[...] for p in parts], axis=0)
    new = jnp.dot(lhs, rot[...], preferred_element_type=F32)

    @pl.when(pl.program_id(0) == 0)
    def _():
        acc[...] = new

    @pl.when(pl.program_id(0) > 0)
    def _():
        acc[...] += new


def rotate_extra(same, other, rot, chosen, out, acc):
    accumulate((same, other), rot, acc)

    @pl.when(pl.program_id(0) == pl.num_programs(0) - 1)
    def _():
        rows = acc[...].astype(BF)
        out[...] = jnp.dot(chosen[...], rows, preferred_element_type=F32).astype(BF)


def rotate(at_ref, *refs):
    parts, (rot, chosen), ext = refs[:8], refs[8:10], refs[10:14]
    out, acc = refs[14:]
    accumulate(parts, rot, acc)

    @pl.when(pl.program_id(0) == pl.num_programs(0) - 1)
    def _():
        x, z, hot = at_ref[0], at_ref[1], at_ref[4]
        acc[...] = jnp.dot(chosen[...], acc[...].astype(BF), preferred_element_type=F32)
        extra = ext[0].shape[0] // NZ
        cap = NN + extra
        for h in range(NX):
            block = jnp.where(hot > 0, ext[h][...].astype(F32), 0.0)
            for g in range(NZ):
                s = lax.rem(x + h, NX) * NZ + lax.rem(z + g, NZ)
                rows = jnp.concatenate(
                    [acc[at(s, NN, 8), :], block[g * extra : (g + 1) * extra]], axis=0
                )
                out[at(s, cap, 32), :] = rows.astype(BF)


def per_device(hidden, resid, w_out, key_gain, cluster_ids, centroids, rotation):
    xi, zi, yi, ci = (lax.axis_index(a) for a in ("x", "z", "y", "c"))
    ni = yi * NC + ci
    wi = xi * NZ + zi
    tokens, width = hidden.shape
    d = width * NN
    cap = 4 * tokens // NW
    cols = w_out.shape[1]
    wide_cols = NZ * cols
    extra = cap - NN
    per_n = extra // NN

    w_t = w_out.T
    up, down = [w_t], [w_t]
    for _ in range(3):
        up.append(shifted(up[-1], "z", NZ, 1))
        down.append(shifted(down[-1], "z", NZ, -1))
    far = [
        shifted(up[-1][: cols // 2], "z", NZ, 1),
        shifted(down[-1][cols // 2 :], "z", NZ, -1),
    ]

    place, cell, hot, short, nth = places(cluster_ids, cap, NN)
    where_am_i = jnp.stack([xi, zi, yi, ci, (wi == hot).astype(I32)]).astype(I32)
    hidden_p = choose_rows(iota((tokens, 1), 0) == place[None, :], hidden)
    h_parts = [hidden_p] + [shifted(hidden_p, "x", NX, h) for h in (1, 2, 3)]

    cell_of = cell[:, None] == iota((1, NW * cap), 1)
    send_ids = jnp.sum(jnp.where(cell_of, cluster_ids[:, None] + 1, 0), axis=0) - 1
    got_ids = lax.all_to_all(send_ids, WIDE, 0, 0, tiled=True).reshape(NW, cap)

    cent_tile = lax.all_to_all(centroids, NARROW, split_axis=1, concat_axis=0, tiled=True)
    local = jnp.where(got_ids >= 0, got_ids - wi * CL_DEV, -1)
    clusters = iota((1, CL_DEV), 1)
    cent_own = choose_rows(local[:, :NN].T.reshape(-1, 1) == clusters, cent_tile)
    cent_out = choose_rows(local[:, NN:].reshape(-1, 1) == clusters, cent_tile)
    cent_in = pick(lax.all_to_all(cent_out.reshape(NW, extra, width), WIDE, 0, 0, tiled=True), hot)
    cent_pre = jnp.concatenate(
        [
            cent_own.reshape(NN, NW, width),
            cent_in.reshape(per_n, NN, width).transpose(1, 0, 2),
            jnp.broadcast_to(key_gain, (NN, 8 - per_n, width)),
        ],
        axis=1,
    )
    cents = lax.all_to_all(cent_pre, NARROW, 0, 0, tiled=True)

    own_place = ni * NW + iota((NW, 1), 0) == place[None, :]
    resid_rows = choose_rows(own_place, resid)

    block = like((NY, NX, NW, wide_cols))
    keep, send = pl.pallas_call(
        project,
        out_shape=(block, block),
        in_specs=[SMEM] + [VMEM] * 13 + [ANY] * 2,
        out_specs=(VMEM, VMEM),
        scratch_shapes=[pltpu.VMEM((wide_cols, width), BF), pltpu.VMEM((tokens, wide_cols), F32)],
        compiler_params=PARAMS,
        name="project",
    )(where_am_i, *h_parts, *up, *down[1:], *far, cent_own, cent_out)
    pairs = pl.pallas_call(
        add_pair,
        out_shape=[like((NX, NW, wide_cols))] * NY,
        in_specs=[VMEM] * 2,
        out_specs=[VMEM] * NY,
        compiler_params=PARAMS,
        name="add_pair",
    )(keep, shifted(send, "c", NC, 1))
    sums = pl.pallas_call(
        add_four,
        out_shape=[like((NW, wide_cols))] * NX,
        in_specs=[VMEM] * NY + [ANY],
        out_specs=[VMEM] * NX,
        compiler_params=PARAMS,
        name="add_four",
    )(pairs[0], *[shifted(pairs[g], "y", NY, g) for g in (1, 2, 3)], cent_pre)
    q = iota((8, 1), 0)
    from_host = (short[None, :] & (nth[None, :] == q * NN + ni) & (q < per_n)).astype(BF)
    keys, res_extra = pl.pallas_call(
        normalize,
        out_shape=(like((NW, d)), like((8, d))),
        in_specs=[SMEM] + [VMEM] * 7,
        out_specs=(VMEM, VMEM),
        scratch_shapes=[pltpu.VMEM((NW, d), F32)],
        compiler_params=PARAMS,
        name="normalize",
    )(
        where_am_i,
        sums[0],
        *[shifted(sums[h], "x", NX, -h) for h in (1, 2, 3)],
        resid_rows,
        cents,
        from_host,
    )

    n_of = ((yi - iota((NC, NY, 1), 1)) % NY) * NC + (ci + iota((NC, NY, 1), 0)) % NC

    got = lax.all_to_all(keys.reshape(NW, NN, width), WIDE, 0, 0, tiled=True).reshape(NW, d)
    filled = (pick(got_ids, ni, 1) >= 0).astype(F32)[:, None]
    residual = pl.pallas_call(
        subtract,
        out_shape=like((NW, d)),
        in_specs=[VMEM] * 3,
        out_specs=VMEM,
        compiler_params=PARAMS,
        name="subtract",
    )(got, cents, filled)
    parts = [residual] + [shifted(residual, "y", NY, h) for h in (1, 2, 3)]
    parts = parts + [shifted(p, "c", NC, 1) for p in parts]

    same = jnp.concatenate([res_extra] + [shifted(res_extra, "y", NY, h) for h in (1, 2, 3)])
    other = shifted(same, "c", NC, 1)
    ext_j = (iota((NC, NY, 8), 2) * NN + n_of).reshape(1, -1)
    steps = NN
    rot_spec = pl.BlockSpec((d // steps, width), lambda k: (k, 0))
    half = pl.BlockSpec((NY * 8, d // steps), lambda k: (0, k))
    ext = pl.pallas_call(
        rotate_extra,
        out_shape=like((extra, width)),
        grid=(steps,),
        in_specs=[half, half, rot_spec, VMEM],
        out_specs=VMEM,
        scratch_shapes=[pltpu.VMEM((NN * 8, width), F32)],
        compiler_params=PARAMS,
        name="rotate_extra",
    )(same, other, rotation, (ext_j == iota((extra, 1), 0)).astype(BF))
    ext_z = jnp.concatenate([ext] + [shifted(ext, "z", NZ, -h) for h in range(1, NZ)])
    ext_x = [ext_z] + [shifted(ext_z, "x", NX, -h) for h in range(1, NX)]

    gap = jnp.min(jnp.where(got_ids[:, :NN] < 0, iota((1, NN), 1), NN), axis=1)
    rank = iota((1, NN), 1)
    from_n = (rank + (rank >= gap[:, None]).astype(I32)).reshape(-1, 1)
    from_s = iota((NW, NN), 0).reshape(-1, 1)
    row_n = jnp.broadcast_to(n_of, (NC, NY, NW)).reshape(1, -1)
    row_s = iota((NC, NY, NW), 2).reshape(1, -1)
    chosen = ((from_n == row_n) & (from_s == row_s)).astype(BF)
    return pl.pallas_call(
        rotate,
        out_shape=like((NW * cap, width)),
        grid=(steps,),
        in_specs=[SMEM]
        + [pl.BlockSpec((NW, d // steps), lambda k: (0, k))] * 8
        + [rot_spec]
        + [VMEM] * 5,
        out_specs=VMEM,
        scratch_shapes=[pltpu.VMEM((NN * NW, width), F32)],
        compiler_params=PARAMS,
        name="rotate",
    )(where_am_i, *parts, rotation, chosen, *ext_x)


def solution(mesh):
    grid = Mesh(mesh.devices.reshape(NX, NZ, NY, NC), ("x", "z", "y", "c"))
    placed = (
        P(WIDE, NARROW),
        P(WIDE, None),
        P(NARROW, WIDE),
        P(NARROW),
        P(WIDE),
        P(WIDE + NARROW, None),
        P(None, NARROW),
    )
    return jax.shard_map(
        per_device, mesh=grid, in_specs=placed, out_specs=P(WIDE, NARROW), check_vma=False
    )
```

```python
import jax
import jax.numpy as jnp
from jax import lax
from jax.experimental import pallas as pl
from jax.experimental.pallas import tpu as pltpu
from jax.sharding import Mesh, PartitionSpec as P

CL_DEV = 1024
EPS = 1e-05
NX, NZ, NY, NC = 4, 8, 4, 2
WIDE = ("x", "z")
NARROW = ("y", "c")
NN = NY * NC
NW = NX * NZ
BF = jnp.bfloat16
F32 = jnp.float32
I32 = jnp.int32


def shifted(a, axis, n, h):
    return lax.ppermute(a, axis, [(i, (i + h) % n) for i in range(n)])


def pick(a, i, axis=0):
    return lax.dynamic_index_in_dim(a, i, axis, keepdims=False)


def iota(shape, dim):
    return lax.broadcasted_iota(I32, shape, dim)


def choose_rows(onehot, a):
    return jnp.dot(onehot.astype(BF), a, preferred_element_type=F32).astype(BF)


def places(ids, cap, per_owner):
    owner = ids // CL_DEV
    onehot = (owner[:, None] == iota((1, NW), 1)).astype(I32)
    rank = jnp.sum((jnp.cumsum(onehot, axis=0) - onehot) * onehot, axis=1)
    count = jnp.sum(onehot, axis=0)
    hot = jnp.argmax(count).astype(I32)
    short = count < per_owner
    nth = jnp.cumsum(short.astype(I32)) - short.astype(I32)
    gap = jnp.where(short, nth % per_owner, per_owner)
    n_of = rank + (rank >= jnp.sum(onehot * gap[None, :], axis=1)).astype(I32)
    surplus = rank >= per_owner
    j = rank - per_owner
    host = jnp.sum(
        jnp.where(short[None, :] & (nth[None, :] == j[:, None]), iota((1, NW), 1), 0), axis=1
    )
    place = jnp.where(surplus, (j % per_owner) * NW + host, n_of * NW + owner)
    cell = owner * cap + jnp.where(surplus, rank, n_of)
    return place, cell, hot, short, nth


VMEM = pl.BlockSpec(memory_space=pltpu.VMEM)
SMEM = pl.BlockSpec(memory_space=pltpu.SMEM)
ANY = pl.BlockSpec(memory_space=pl.ANY)
PARAMS = pltpu.CompilerParams(vmem_limit_bytes=28 * 1024 * 1024)


def like(shape, dtype=BF):
    return jax.ShapeDtypeStruct(shape, dtype)


def at(i, size, step):
    return pl.ds(pl.multiple_of(i * size, step), size)


def project(at_ref, *refs):
    h_refs, up, down, far = refs[:4], refs[4:8], refs[8:11], refs[11:13]
    keep, send, w_all, acc = refs[15:]
    z, y, c = at_ref[1], at_ref[2], at_ref[3]
    cols = up[0].shape[0]
    for h in range(4):
        w_all[at(lax.rem(z + NZ - h, NZ), cols, 16), :] = up[h][...]
        if h:
            w_all[at(lax.rem(z + h, NZ), cols, 16), :] = down[h - 1][...]
    across = lax.rem(z + 4, NZ) * cols
    w_all[pl.ds(pl.multiple_of(across, 16), cols // 2), :] = far[0][...]
    w_all[pl.ds(pl.multiple_of(across + cols // 2, 16), cols // 2), :] = far[1][...]
    for h in range(NX):
        acc[...] = lax.dot_general(
            h_refs[h][...], w_all[...], (((1,), (1,)), ((), ())), preferred_element_type=F32
        )
        for g in range(NY):
            n = lax.rem(y + g, NY) * NC
            keep[g, h] = acc[at(n + c, NW, 32), :].astype(BF)
            send[g, h] = acc[at(n + 1 - c, NW, 32), :].astype(BF)


def add_pair(keep, other, own, away, *outs):
    for g in range(NY):
        outs[g][...] = (keep[g].astype(F32) + other[g].astype(F32)).astype(BF)


def add_four(*refs):
    for h in range(NX):
        total = refs[0][h].astype(F32)
        for g in range(1, NY):
            total = total + refs[g][h].astype(F32)
        refs[NY + 1 + h][...] = total.astype(BF)


def normalize(at_ref, b0, b1, b2, b3, resid, cents, from_host, keys, extra, stream):
    x = at_ref[0]
    span = b0.shape[1]
    width = cents.shape[2]
    for h, b in enumerate((b0, b1, b2, b3)):
        where = at(lax.rem(x + h, NX), span, 128)
        stream[:, where] = resid[:, where].astype(F32) + b[...].astype(F32)
    value = stream[...]
    scale = lax.rsqrt(jnp.mean(value * value, axis=1, keepdims=True) + EPS)
    for n in range(NN):
        part = slice(n * width, (n + 1) * width)
        tail = cents[n, NW:, :].astype(F32)
        key = (stream[:, part] * scale * tail[7:8]).astype(BF)
        keys[:, part] = key
        chosen = jnp.dot(from_host[...], key, preferred_element_type=F32)
        extra[:, part] = (chosen - tail).astype(BF)


def subtract(keys, cents, filled, out):
    width = cents.shape[2]
    for n in range(NN):
        part = slice(n * width, (n + 1) * width)
        diff = keys[:, part].astype(F32) - cents[n, :NW, :].astype(F32)
        out[:, part] = jnp.where(filled[...] > 0, diff, 0.0).astype(BF)


def split_rows(cent, *refs):
    out = refs[-1]
    width = out.shape[2]
    for n in range(NN):
        out[n] = cent[:, n * width : (n + 1) * width]


def cells(cell, ids, *refs):
    out = refs[-1]
    hit = cell[...] == lax.broadcasted_iota(I32, (cell.shape[0], out.shape[1]), 1)
    out[...] = jnp.sum(jnp.where(hit, ids[...] + 1, 0), axis=0, keepdims=True) - 1


def product(parts, rot):
    lhs = jnp.concatenate([p[...] for p in parts], axis=0)
    step = rot.shape[0] // 4
    total = None
    for k in range(4):
        part = slice(k * step, (k + 1) * step)
        new = jnp.dot(lhs[:, part], rot[part, :], preferred_element_type=F32)
        total = new if total is None else total + new
    return total


def rotate_extra(same, other, rot, chosen, out):
    rows = product((same, other), rot).astype(BF)
    picked = jnp.dot(chosen[...], rows, preferred_element_type=F32).astype(BF)
    for g in range(NZ):
        out[g] = picked


def rotate(at_ref, *refs):
    parts, (rot, chosen, ext, out) = refs[:8], refs[8:]
    hot = at_ref[4]
    rows = product(parts, rot).astype(BF)
    rows = jnp.dot(chosen[...], rows, preferred_element_type=F32)
    extra = ext.shape[0] // NW
    cap = NN + extra
    for s in range(NW):
        tail = ext[s * extra : (s + 1) * extra, :].astype(F32)
        tail = jnp.where(hot > 0, tail, 0.0)
        both = jnp.concatenate([rows[s * NN : (s + 1) * NN], tail], axis=0)
        out[s * cap : (s + 1) * cap, :] = both.astype(BF)


def per_device(hidden, resid, w_out, key_gain, cluster_ids, centroids, rotation):
    xi, zi, yi, ci = (lax.axis_index(a) for a in ("x", "z", "y", "c"))
    ni = yi * NC + ci
    wi = xi * NZ + zi
    tokens, width = hidden.shape
    d = width * NN
    cap = 4 * tokens // NW
    cols = w_out.shape[1]
    wide_cols = NZ * cols
    extra = cap - NN
    per_n = extra // NN

    w_t = w_out.T
    up, down = [w_t], [w_t]
    for _ in range(3):
        up.append(shifted(up[-1], "z", NZ, 1))
        down.append(shifted(down[-1], "z", NZ, -1))
    far = [
        shifted(up[-1][: cols // 2], "z", NZ, 1),
        shifted(down[-1][cols // 2 :], "z", NZ, -1),
    ]

    place, cell, hot, short, nth = places(cluster_ids, cap, NN)
    where_am_i = jnp.stack([xi, zi, yi, ci, (wi == hot).astype(I32)]).astype(I32)
    hidden_p = choose_rows(iota((tokens, 1), 0) == place[None, :], hidden)
    h_parts = [hidden_p] + [shifted(hidden_p, "x", NX, h) for h in (1, 2, 3)]

    send_ids = pl.pallas_call(
        cells,
        out_shape=like((1, NW * cap), I32),
        in_specs=[VMEM] * 2 + [ANY] * 2,
        out_specs=VMEM,
        compiler_params=PARAMS,
        name="cells",
    )(cell[:, None], cluster_ids[:, None], h_parts[1], h_parts[3])
    got_ids = lax.all_to_all(send_ids.reshape(NW * cap), WIDE, 0, 0, tiled=True).reshape(NW, cap)

    cent_split = pl.pallas_call(
        split_rows,
        out_shape=like((NN, centroids.shape[0], width)),
        in_specs=[VMEM] + [ANY] * 2,
        out_specs=VMEM,
        compiler_params=PARAMS,
        name="split_rows",
    )(centroids, up[1], down[1])
    cent_tile = lax.all_to_all(cent_split, NARROW, 0, 0, tiled=True).reshape(-1, width)
    local = jnp.where(got_ids >= 0, got_ids - wi * CL_DEV, -1)
    clusters = iota((1, CL_DEV), 1)
    cent_own = choose_rows(local[:, :NN].T.reshape(-1, 1) == clusters, cent_tile)
    cent_out = choose_rows(local[:, NN:].reshape(-1, 1) == clusters, cent_tile)
    cent_in = pick(lax.all_to_all(cent_out.reshape(NW, extra, width), WIDE, 0, 0, tiled=True), hot)
    cent_pre = jnp.concatenate(
        [
            cent_own.reshape(NN, NW, width),
            cent_in.reshape(per_n, NN, width).transpose(1, 0, 2),
            jnp.broadcast_to(key_gain, (NN, 8 - per_n, width)),
        ],
        axis=1,
    )
    cents = lax.all_to_all(cent_pre, NARROW, 0, 0, tiled=True)

    own_place = ni * NW + iota((NW, 1), 0) == place[None, :]
    resid_rows = choose_rows(own_place, resid)

    block = like((NY, NX, NW, wide_cols))
    keep, send = pl.pallas_call(
        project,
        out_shape=(block, block),
        in_specs=[SMEM] + [VMEM] * 13 + [ANY] * 2,
        out_specs=(VMEM, VMEM),
        scratch_shapes=[pltpu.VMEM((wide_cols, width), BF), pltpu.VMEM((tokens, wide_cols), F32)],
        compiler_params=PARAMS,
        name="project",
    )(where_am_i, *h_parts, *up, *down[1:], *far, got_ids, cent_tile)
    pairs = pl.pallas_call(
        add_pair,
        out_shape=[like((NX, NW, wide_cols))] * NY,
        in_specs=[VMEM] * 2 + [ANY] * 2,
        out_specs=[VMEM] * NY,
        compiler_params=PARAMS,
        name="add_pair",
    )(keep, shifted(send, "c", NC, 1), cent_own, cent_out)
    sums = pl.pallas_call(
        add_four,
        out_shape=[like((NW, wide_cols))] * NX,
        in_specs=[VMEM] * NY + [ANY],
        out_specs=[VMEM] * NX,
        compiler_params=PARAMS,
        name="add_four",
    )(pairs[0], *[shifted(pairs[g], "y", NY, g) for g in (1, 2, 3)], cent_pre)
    q = iota((8, 1), 0)
    from_host = (short[None, :] & (nth[None, :] == q * NN + ni) & (q < per_n)).astype(BF)
    keys, res_extra = pl.pallas_call(
        normalize,
        out_shape=(like((NW, d)), like((8, d))),
        in_specs=[SMEM] + [VMEM] * 7,
        out_specs=(VMEM, VMEM),
        scratch_shapes=[pltpu.VMEM((NW, d), F32)],
        compiler_params=PARAMS,
        name="normalize",
    )(
        where_am_i,
        sums[0],
        *[shifted(sums[h], "x", NX, -h) for h in (1, 2, 3)],
        resid_rows,
        cents,
        from_host,
    )

    n_of = ((yi - iota((NC, NY, 1), 1)) % NY) * NC + (ci + iota((NC, NY, 1), 0)) % NC

    got = lax.all_to_all(keys.reshape(NW, NN, width), WIDE, 0, 0, tiled=True).reshape(NW, d)
    filled = (pick(got_ids, ni, 1) >= 0).astype(F32)[:, None]
    residual = pl.pallas_call(
        subtract,
        out_shape=like((NW, d)),
        in_specs=[VMEM] * 3,
        out_specs=VMEM,
        compiler_params=PARAMS,
        name="subtract",
    )(got, cents, filled)
    parts = [residual] + [shifted(residual, "y", NY, h) for h in (1, 2, 3)]
    parts = parts + [shifted(p, "c", NC, 1) for p in parts]

    same = jnp.concatenate([res_extra] + [shifted(res_extra, "y", NY, h) for h in (1, 2, 3)])
    other = shifted(same, "c", NC, 1)
    ext_j = (iota((NC, NY, 8), 2) * NN + n_of).reshape(1, -1)
    ext = pl.pallas_call(
        rotate_extra,
        out_shape=like((NZ, extra, width)),
        in_specs=[VMEM] * 4,
        out_specs=VMEM,
        compiler_params=PARAMS,
        name="rotate_extra",
    )(same, other, rotation, (ext_j == iota((extra, 1), 0)).astype(BF))
    ext = lax.all_to_all(ext, "z", 0, 0, tiled=True).reshape(1, NZ * extra, width)
    ext = lax.all_to_all(jnp.broadcast_to(ext, (NX, NZ * extra, width)), "x", 0, 0, tiled=True)

    gap = jnp.min(jnp.where(got_ids[:, :NN] < 0, iota((1, NN), 1), NN), axis=1)
    rank = iota((1, NN), 1)
    from_n = (rank + (rank >= gap[:, None]).astype(I32)).reshape(-1, 1)
    from_s = iota((NW, NN), 0).reshape(-1, 1)
    row_n = jnp.broadcast_to(n_of, (NC, NY, NW)).reshape(1, -1)
    row_s = iota((NC, NY, NW), 2).reshape(1, -1)
    chosen = ((from_n == row_n) & (from_s == row_s)).astype(BF)
    return pl.pallas_call(
        rotate,
        out_shape=like((NW * cap, width)),
        in_specs=[SMEM] + [VMEM] * 11,
        out_specs=VMEM,
        compiler_params=PARAMS,
        name="rotate",
    )(where_am_i, *parts, rotation, chosen, ext.reshape(NW * extra, width))


def solution(mesh):
    grid = Mesh(mesh.devices.reshape(NX, NZ, NY, NC), ("x", "z", "y", "c"))
    placed = (
        P(WIDE, NARROW),
        P(WIDE, None),
        P(NARROW, WIDE),
        P(NARROW),
        P(WIDE),
        P(WIDE + NARROW, None),
        P(None, NARROW),
    )
    return jax.shard_map(
        per_device, mesh=grid, in_specs=placed, out_specs=P(WIDE, NARROW), check_vma=False
    )
```

```python
import jax
import jax.numpy as jnp
from jax import lax
from jax.experimental import pallas as pl
from jax.experimental.pallas import tpu as pltpu
from jax.sharding import Mesh, PartitionSpec as P

CL_DEV = 1024
EPS = 1e-05
NX, NZ, NY, NC = 4, 8, 4, 2
WIDE = ("x", "z")
NARROW = ("y", "c")
NN = NY * NC
NW = NX * NZ
BF = jnp.bfloat16
F32 = jnp.float32
I32 = jnp.int32


def shifted(a, axis, n, h):
    return lax.ppermute(a, axis, [(i, (i + h) % n) for i in range(n)])


def pick(a, i, axis=0):
    return lax.dynamic_index_in_dim(a, i, axis, keepdims=False)


def iota(shape, dim):
    return lax.broadcasted_iota(I32, shape, dim)


def choose_rows(onehot, a):
    return jnp.dot(onehot.astype(BF), a, preferred_element_type=F32).astype(BF)


def places(ids, cap, per_owner):
    owner = ids // CL_DEV
    onehot = (owner[:, None] == iota((1, NW), 1)).astype(I32)
    rank = jnp.sum((jnp.cumsum(onehot, axis=0) - onehot) * onehot, axis=1)
    count = jnp.sum(onehot, axis=0)
    hot = jnp.argmax(count).astype(I32)
    short = count < per_owner
    nth = jnp.cumsum(short.astype(I32)) - short.astype(I32)
    gap = jnp.where(short, nth % per_owner, per_owner)
    n_of = rank + (rank >= jnp.sum(onehot * gap[None, :], axis=1)).astype(I32)
    surplus = rank >= per_owner
    j = rank - per_owner
    host = jnp.sum(
        jnp.where(short[None, :] & (nth[None, :] == j[:, None]), iota((1, NW), 1), 0), axis=1
    )
    place = jnp.where(surplus, (j % per_owner) * NW + host, n_of * NW + owner)
    cell = owner * cap + jnp.where(surplus, rank, n_of)
    return place, cell, hot, short, nth


SMEM = pl.BlockSpec(memory_space=pltpu.SMEM)
ANY = pl.BlockSpec(memory_space=pl.ANY)
PARAMS = pltpu.CompilerParams(vmem_limit_bytes=28 * 1024 * 1024)


def like(shape, dtype=BF):
    return jax.ShapeDtypeStruct(shape, dtype)


def whole(shape):
    return pl.BlockSpec(shape, lambda i: (0,) * len(shape))


def local_call(kernel, outs, args, after=(), smem=(), scratch=(), grid=(1,), specs=None):
    return pl.pallas_call(
        kernel,
        out_shape=outs,
        grid=grid,
        in_specs=[SMEM] * len(smem) + (specs or [whole(a.shape) for a in args]) + [ANY] * len(after),
        out_specs=jax.tree.map(lambda o: whole(o.shape), outs),
        scratch_shapes=list(scratch),
        compiler_params=PARAMS,
        name=kernel.__name__,
    )(*smem, *args, *after)


def at(i, size, step):
    return pl.ds(pl.multiple_of(i * size, step), size)


def project(at_ref, *refs):
    h_refs, up, down, far = refs[:4], refs[4:8], refs[8:11], refs[11:13]
    keep, send, w_all, acc = refs[13:]
    z, y, c = at_ref[1], at_ref[2], at_ref[3]
    cols = up[0].shape[0]
    for h in range(4):
        w_all[at(lax.rem(z + NZ - h, NZ), cols, 16), :] = up[h][...]
        if h:
            w_all[at(lax.rem(z + h, NZ), cols, 16), :] = down[h - 1][...]
    across = lax.rem(z + 4, NZ) * cols
    w_all[pl.ds(pl.multiple_of(across, 16), cols // 2), :] = far[0][...]
    w_all[pl.ds(pl.multiple_of(across + cols // 2, 16), cols // 2), :] = far[1][...]
    for h in range(NX):
        acc[...] = lax.dot_general(
            h_refs[h][...], w_all[...], (((1,), (1,)), ((), ())), preferred_element_type=F32
        )
        for g in range(NY):
            n = lax.rem(y + g, NY) * NC
            keep[g, h] = acc[at(n + c, NW, 32), :].astype(BF)
            send[g, h] = acc[at(n + 1 - c, NW, 32), :].astype(BF)


def add_pair(keep, other, *outs):
    for g in range(NY):
        outs[g][...] = (keep[g].astype(F32) + other[g].astype(F32)).astype(BF)


def add_four(*refs):
    outs = refs[-NX:]
    for h in range(NX):
        total = refs[0][h].astype(F32)
        for g in range(1, NY):
            total = total + refs[g][h].astype(F32)
        outs[h][...] = total.astype(BF)


def gate(ids, token, out):
    out[...] = ids[...]


def normalize(at_ref, b0, b1, b2, b3, resid, cents, from_host, keys, extra, stream):
    x = at_ref[0]
    span = b0.shape[1]
    width = cents.shape[2]
    for h, b in enumerate((b0, b1, b2, b3)):
        where = at(lax.rem(x + h, NX), span, 128)
        stream[:, where] = resid[:, where].astype(F32) + b[...].astype(F32)
    value = stream[...]
    scale = lax.rsqrt(jnp.mean(value * value, axis=1, keepdims=True) + EPS)
    for n in range(NN):
        part = slice(n * width, (n + 1) * width)
        tail = cents[n, NW:, :].astype(F32)
        key = (stream[:, part] * scale * tail[7:8]).astype(BF)
        keys[:, part] = key
        chosen = jnp.dot(from_host[...], key, preferred_element_type=F32)
        extra[:, part] = (chosen - tail).astype(BF)


def subtract(keys, cents, filled, out):
    width = cents.shape[2]
    for n in range(NN):
        part = slice(n * width, (n + 1) * width)
        diff = keys[:, part].astype(F32) - cents[n, :NW, :].astype(F32)
        out[:, part] = jnp.where(filled[...] > 0, diff, 0.0).astype(BF)


def split_rows(cent, *refs):
    out = refs[-1]
    width = out.shape[2]
    for n in range(NN):
        out[n] = cent[:, n * width : (n + 1) * width]


def cells(cell, ids, *refs):
    out = refs[-1]
    hit = cell[...] == lax.broadcasted_iota(I32, (cell.shape[0], out.shape[1]), 1)
    out[...] = jnp.sum(jnp.where(hit, ids[...] + 1, 0), axis=0, keepdims=True) - 1


def accumulate(parts, rot, acc):
    lhs = jnp.concatenate([p[...] for p in parts], axis=0)
    new = jnp.dot(lhs, rot[...], preferred_element_type=F32)

    @pl.when(pl.program_id(0) == 0)
    def _():
        acc[...] = new

    @pl.when(pl.program_id(0) > 0)
    def _():
        acc[...] += new


def rotate_extra(*refs):
    parts, (rot, chosen, out, acc) = refs[:8], refs[8:]
    accumulate(parts, rot, acc)

    @pl.when(pl.program_id(0) == pl.num_programs(0) - 1)
    def _():
        rows = acc[...].astype(BF)
        picked = jnp.dot(chosen[...], rows, preferred_element_type=F32).astype(BF)
        for g in range(NZ):
            out[g] = picked


def rotate(at_ref, *refs):
    parts, (rot, chosen), ext, (out, acc) = refs[:8], refs[8:10], refs[10:14], refs[14:]
    accumulate(parts, rot, acc)

    @pl.when(pl.program_id(0) == pl.num_programs(0) - 1)
    def _():
        x, hot = at_ref[0], at_ref[4]
        acc[...] = jnp.dot(chosen[...], acc[...].astype(BF), preferred_element_type=F32)
        extra = ext[0].shape[1]
        cap = NN + extra
        for h in range(NX):
            first = lax.rem(x + h, NX) * NZ
            for g in range(NZ):
                tail = jnp.where(hot > 0, ext[h][g].astype(F32), 0.0)
                rows = jnp.concatenate([acc[at(first + g, NN, 8), :], tail], axis=0)
                out[at(first + g, cap, 32), :] = rows.astype(BF)


def per_device(hidden, resid, w_out, key_gain, cluster_ids, centroids, rotation):
    xi, zi, yi, ci = (lax.axis_index(a) for a in ("x", "z", "y", "c"))
    ni = yi * NC + ci
    wi = xi * NZ + zi
    tokens, width = hidden.shape
    d = width * NN
    cap = 4 * tokens // NW
    cols = w_out.shape[1]
    wide_cols = NZ * cols
    extra = cap - NN
    per_n = extra // NN

    w_t = w_out.T
    up, down = [w_t], [w_t]
    for _ in range(3):
        up.append(shifted(up[-1], "z", NZ, 1))
        down.append(shifted(down[-1], "z", NZ, -1))
    far = [
        shifted(up[-1][: cols // 2], "z", NZ, 1),
        shifted(down[-1][cols // 2 :], "z", NZ, -1),
    ]

    place, cell, hot, short, nth = places(cluster_ids, cap, NN)
    where_am_i = jnp.stack([xi, zi, yi, ci, (wi == hot).astype(I32)]).astype(I32)
    hidden_p = choose_rows(iota((tokens, 1), 0) == place[None, :], hidden)
    h_parts = [hidden_p] + [shifted(hidden_p, "x", NX, h) for h in (1, 2, 3)]

    send_ids = local_call(
        cells,
        like((1, NW * cap), I32),
        (cell[:, None], cluster_ids[:, None]),
        after=(h_parts[1], h_parts[3]),
    )
    got_ids = lax.all_to_all(send_ids.reshape(NW * cap), WIDE, 0, 0, tiled=True).reshape(NW, cap)

    cent_split = local_call(
        split_rows,
        like((NN, centroids.shape[0], width)),
        (centroids,),
        after=(up[1], down[1]),
    )
    cent_tile = lax.all_to_all(cent_split, NARROW, 0, 0, tiled=True).reshape(-1, width)

    block = like((NY, NX, NW, wide_cols))
    keep, send = local_call(
        project,
        (block, block),
        (*h_parts, *up, *down[1:], *far),
        smem=(where_am_i,),
        scratch=[pltpu.VMEM((wide_cols, width), BF), pltpu.VMEM((tokens, wide_cols), F32)],
    )
    pairs = local_call(
        add_pair, [like((NX, NW, wide_cols))] * NY, (keep, shifted(send, "c", NC, 1))
    )

    local = jnp.where(got_ids >= 0, got_ids - wi * CL_DEV, -1)
    local = local_call(gate, like(local.shape, I32), (local,), after=(keep,))
    clusters = iota((1, CL_DEV), 1)
    cent_own = choose_rows(local[:, :NN].T.reshape(-1, 1) == clusters, cent_tile)
    cent_out = choose_rows(local[:, NN:].reshape(-1, 1) == clusters, cent_tile)
    cent_in = pick(lax.all_to_all(cent_out.reshape(NW, extra, width), WIDE, 0, 0, tiled=True), hot)
    cent_pre = jnp.concatenate(
        [
            cent_own.reshape(NN, NW, width),
            cent_in.reshape(per_n, NN, width).transpose(1, 0, 2),
            jnp.broadcast_to(key_gain, (NN, 8 - per_n, width)),
        ],
        axis=1,
    )
    cents = lax.all_to_all(cent_pre, NARROW, 0, 0, tiled=True)

    own_place = ni * NW + iota((NW, 1), 0) == place[None, :]
    resid_rows = choose_rows(own_place, resid)

    sums = local_call(
        add_four,
        [like((NW, wide_cols))] * NX,
        (pairs[0], *[shifted(pairs[g], "y", NY, g) for g in (1, 2, 3)]),
    )
    q = iota((8, 1), 0)
    from_host = (short[None, :] & (nth[None, :] == q * NN + ni) & (q < per_n)).astype(BF)
    keys, res_extra = local_call(
        normalize,
        (like((NW, d)), like((8, d))),
        (
            sums[0],
            *[shifted(sums[h], "x", NX, -h) for h in (1, 2, 3)],
            resid_rows,
            cents,
            from_host,
        ),
        smem=(where_am_i,),
        scratch=[pltpu.VMEM((NW, d), F32)],
    )

    n_of = ((yi - iota((NC, NY, 1), 1)) % NY) * NC + (ci + iota((NC, NY, 1), 0)) % NC

    got = lax.all_to_all(keys.reshape(NW, NN, width), WIDE, 0, 0, tiled=True).reshape(NW, d)
    filled = (pick(got_ids, ni, 1) >= 0).astype(F32)[:, None]
    residual = local_call(subtract, like((NW, d)), (got, cents, filled))
    parts = [residual] + [shifted(residual, "y", NY, h) for h in (1, 2, 3)]
    parts = parts + [shifted(p, "c", NC, 1) for p in parts]

    steps = 4
    rot_spec = pl.BlockSpec((d // steps, width), lambda k: (k, 0))

    def row_specs(rows):
        return [pl.BlockSpec((rows, d // steps), lambda k: (0, k))] * NN

    pieces = [res_extra] + [shifted(res_extra, "y", NY, h) for h in (1, 2, 3)]
    pieces = pieces + [shifted(p, "c", NC, 1) for p in pieces]
    ext_j = (iota((NC, NY, 8), 2) * NN + n_of).reshape(1, -1)
    choose_ext = (ext_j == iota((extra, 1), 0)).astype(BF)
    ext = local_call(
        rotate_extra,
        like((NZ, extra, width)),
        (*pieces, rotation, choose_ext),
        scratch=[pltpu.VMEM((NN * 8, width), F32)],
        grid=(steps,),
        specs=row_specs(8) + [rot_spec, whole(choose_ext.shape)],
    )
    ext = lax.all_to_all(ext, "z", 0, 0, tiled=True)
    ext = [ext] + [shifted(ext, "x", NX, -h) for h in range(1, NX)]

    gap = jnp.min(jnp.where(got_ids[:, :NN] < 0, iota((1, NN), 1), NN), axis=1)
    rank = iota((1, NN), 1)
    from_n = (rank + (rank >= gap[:, None]).astype(I32)).reshape(-1, 1)
    from_s = iota((NW, NN), 0).reshape(-1, 1)
    row_n = jnp.broadcast_to(n_of, (NC, NY, NW)).reshape(1, -1)
    row_s = iota((NC, NY, NW), 2).reshape(1, -1)
    chosen = ((from_n == row_n) & (from_s == row_s)).astype(BF)
    return local_call(
        rotate,
        like((NW * cap, width)),
        (*parts, rotation, chosen, *ext),
        smem=(where_am_i,),
        scratch=[pltpu.VMEM((NN * NW, width), F32)],
        grid=(steps,),
        specs=row_specs(NW) + [rot_spec, whole(chosen.shape)] + [whole(ext[0].shape)] * NX,
    )


def solution(mesh):
    grid = Mesh(mesh.devices.reshape(NX, NZ, NY, NC), ("x", "z", "y", "c"))
    placed = (
        P(WIDE, NARROW),
        P(WIDE, None),
        P(NARROW, WIDE),
        P(NARROW),
        P(WIDE),
        P(WIDE + NARROW, None),
        P(None, NARROW),
    )
    return jax.shard_map(
        per_device, mesh=grid, in_specs=placed, out_specs=P(WIDE, NARROW), check_vma=False
    )
```

```python
import jax
import jax.numpy as jnp
from jax import lax
from jax.experimental import pallas as pl
from jax.experimental.pallas import tpu as pltpu
from jax.sharding import Mesh, PartitionSpec as P

CL_DEV = 1024
EPS = 1e-05
NX, NZ, NY, NC = 4, 8, 4, 2
WIDE = ("x", "z")
NARROW = ("y", "c")
NN = NY * NC
NW = NX * NZ
BF = jnp.bfloat16
F32 = jnp.float32
I32 = jnp.int32


def shifted(a, axis, n, h):
    return lax.ppermute(a, axis, [(i, (i + h) % n) for i in range(n)])


def pick(a, i, axis=0):
    return lax.dynamic_index_in_dim(a, i, axis, keepdims=False)


def iota(shape, dim):
    return lax.broadcasted_iota(I32, shape, dim)


def choose_rows(onehot, a):
    return jnp.dot(onehot.astype(BF), a, preferred_element_type=F32).astype(BF)


def places(ids, cap, per_owner):
    owner = ids // CL_DEV
    onehot = (owner[:, None] == iota((1, NW), 1)).astype(I32)
    rank = jnp.sum((jnp.cumsum(onehot, axis=0) - onehot) * onehot, axis=1)
    count = jnp.sum(onehot, axis=0)
    hot = jnp.argmax(count).astype(I32)
    short = count < per_owner
    nth = jnp.cumsum(short.astype(I32)) - short.astype(I32)
    gap = jnp.where(short, nth % per_owner, per_owner)
    n_of = rank + (rank >= jnp.sum(onehot * gap[None, :], axis=1)).astype(I32)
    surplus = rank >= per_owner
    j = rank - per_owner
    host = jnp.sum(
        jnp.where(short[None, :] & (nth[None, :] == j[:, None]), iota((1, NW), 1), 0), axis=1
    )
    place = jnp.where(surplus, (j % per_owner) * NW + host, n_of * NW + owner)
    cell = owner * cap + jnp.where(surplus, rank, n_of)
    return place, cell, hot, short, nth


SMEM = pl.BlockSpec(memory_space=pltpu.SMEM)
ANY = pl.BlockSpec(memory_space=pl.ANY)
PARAMS = pltpu.CompilerParams(vmem_limit_bytes=56 * 1024 * 1024)


def like(shape, dtype=BF):
    return jax.ShapeDtypeStruct(shape, dtype)


def whole(shape):
    return pl.BlockSpec(shape, lambda i: (0,) * len(shape))


def local_call(kernel, outs, args, after=(), smem=(), scratch=(), grid=(1,), specs=None):
    return pl.pallas_call(
        kernel,
        out_shape=outs,
        grid=grid,
        in_specs=[SMEM] * len(smem) + (specs or [whole(a.shape) for a in args]) + [ANY] * len(after),
        out_specs=jax.tree.map(lambda o: whole(o.shape), outs),
        scratch_shapes=list(scratch),
        compiler_params=PARAMS,
        name=kernel.__name__,
    )(*smem, *args, *after)


def at(i, size, step):
    return pl.ds(pl.multiple_of(i * size, step), size)


def project(at_ref, *refs):
    h_refs, up, down, far = refs[:4], refs[4:8], refs[8:11], refs[11:13]
    keep, send, w_all, acc = refs[13:]
    z, y, c = at_ref[1], at_ref[2], at_ref[3]
    cols = up[0].shape[0]
    for h in range(4):
        w_all[at(lax.rem(z + NZ - h, NZ), cols, 16), :] = up[h][...]
        if h:
            w_all[at(lax.rem(z + h, NZ), cols, 16), :] = down[h - 1][...]
    across = lax.rem(z + 4, NZ) * cols
    w_all[pl.ds(pl.multiple_of(across, 16), cols // 2), :] = far[0][...]
    w_all[pl.ds(pl.multiple_of(across + cols // 2, 16), cols // 2), :] = far[1][...]
    for h in range(NX):
        acc[...] = lax.dot_general(
            h_refs[h][...], w_all[...], (((1,), (1,)), ((), ())), preferred_element_type=F32
        )
        for g in range(NY):
            n = lax.rem(y + g, NY) * NC
            keep[g, h] = acc[at(n + c, NW, 32), :].astype(BF)
            send[g, h] = acc[at(n + 1 - c, NW, 32), :].astype(BF)


def add_pair(keep, other, *outs):
    for g in range(NY):
        outs[g][...] = (keep[g].astype(F32) + other[g].astype(F32)).astype(BF)


def add_four(*refs):
    outs = refs[-NX:]
    for h in range(NX):
        total = refs[0][h].astype(F32)
        for g in range(1, NY):
            total = total + refs[g][h].astype(F32)
        outs[h][...] = total.astype(BF)


def gate(ids, *refs):
    refs[-1][...] = ids[...]


def normalize(at_ref, b0, b1, b2, b3, resid, cents, from_host, keys, extra, stream):
    x = at_ref[0]
    span = b0.shape[1]
    width = cents.shape[2]
    for h, b in enumerate((b0, b1, b2, b3)):
        where = at(lax.rem(x + h, NX), span, 128)
        stream[:, where] = resid[:, where].astype(F32) + b[...].astype(F32)
    value = stream[...]
    scale = lax.rsqrt(jnp.mean(value * value, axis=1, keepdims=True) + EPS)
    for n in range(NN):
        part = slice(n * width, (n + 1) * width)
        tail = cents[n, NW:, :].astype(F32)
        key = (stream[:, part] * scale * tail[7:8]).astype(BF)
        keys[:, part] = key
        chosen = jnp.dot(from_host[...], key, preferred_element_type=F32)
        extra[:, part] = (chosen - tail).astype(BF)


def spread(keys, *refs):
    out = refs[-1]
    width = out.shape[2]
    for n in range(NN):
        out[:, n, :] = keys[:, n * width : (n + 1) * width]


def subtract(keys, cents, filled, out):
    width = cents.shape[2]
    for n in range(NN):
        part = slice(n * width, (n + 1) * width)
        diff = keys[:, n, :].astype(F32) - cents[n, :NW, :].astype(F32)
        out[:, part] = jnp.where(filled[...] > 0, diff, 0.0).astype(BF)


def split_lines(at_ref, cent, *refs):
    outs = refs[-NY:]
    span = outs[0].shape[1]
    for g in range(NY):
        outs[g][...] = cent[:, at(lax.rem(at_ref[2] + g, NY), span, 128)]


def split_cores(at_ref, *refs):
    parts, (keep, send) = refs[:NY], refs[NY:]
    c, width = at_ref[3], keep.shape[2]
    for h in range(NY):
        keep[h] = parts[h][:, at(c, width, 128)]
        send[h] = parts[h][:, at(1 - c, width, 128)]


def pick_rows(at_ref, ids, keep, other, *refs):
    own, away, hits, tile = refs[-4:]
    y, c = at_ref[2], at_ref[3]
    slots, (rows, width) = ids.shape[0], keep.shape[1:]
    for k, part in enumerate((keep, other)):
        for h in range(NY):
            n = lax.rem(y + NY - h, NY) * NC + (1 - c if k else c)
            base = (k * NY + h) * rows
            tile[base : base + rows, :] = part[h]
            cluster = n * rows + lax.broadcasted_iota(I32, (slots, rows), 1)
            hits[:, base : base + rows] = (ids[...] == cluster).astype(F32).astype(BF)
    mine = own.shape[0] * own.shape[1]
    out = jnp.dot(hits[:mine, :], tile[...], preferred_element_type=F32).astype(BF)
    own[...] = out.reshape(own.shape)
    out = jnp.dot(hits[mine:, :], tile[...], preferred_element_type=F32)
    away[...] = out.reshape(away.shape).astype(BF)


def accumulate(parts, rot, acc):
    lhs = jnp.concatenate([p[...] for p in parts], axis=0)
    new = jnp.dot(lhs, rot[...], preferred_element_type=F32)

    @pl.when(pl.program_id(0) == 0)
    def _():
        acc[...] = new

    @pl.when(pl.program_id(0) > 0)
    def _():
        acc[...] += new


def rotate_extra(*refs):
    parts, (rot, chosen, out, acc) = refs[:8], refs[8:]
    accumulate(parts, rot, acc)

    @pl.when(pl.program_id(0) == pl.num_programs(0) - 1)
    def _():
        rows = acc[...].astype(BF)
        picked = jnp.dot(chosen[...], rows, preferred_element_type=F32).astype(BF)
        for g in range(NZ):
            out[g] = picked


def rotate(at_ref, *refs):
    parts, (rot, chosen), ext, (out, acc) = refs[:8], refs[8:10], refs[10:14], refs[14:]
    accumulate(parts, rot, acc)

    @pl.when(pl.program_id(0) == pl.num_programs(0) - 1)
    def _():
        x, hot = at_ref[0], at_ref[4]
        acc[...] = jnp.dot(chosen[...], acc[...].astype(BF), preferred_element_type=F32)
        extra = ext[0].shape[1]
        cap = NN + extra
        for h in range(NX):
            first = lax.rem(x + h, NX) * NZ
            for g in range(NZ):
                tail = jnp.where(hot > 0, ext[h][g].astype(F32), 0.0)
                rows = jnp.concatenate([acc[at(first + g, NN, 8), :], tail], axis=0)
                out[at(first + g, cap, 32), :] = rows.astype(BF)


def per_device(hidden, resid, w_out, key_gain, cluster_ids, centroids, rotation):
    xi, zi, yi, ci = (lax.axis_index(a) for a in ("x", "z", "y", "c"))
    ni = yi * NC + ci
    wi = xi * NZ + zi
    tokens, width = hidden.shape
    d = width * NN
    cap = 4 * tokens // NW
    cols = w_out.shape[1]
    wide_cols = NZ * cols
    extra = cap - NN
    per_n = extra // NN

    w_t = w_out.T
    up, down = [w_t], [w_t]
    for _ in range(3):
        up.append(shifted(up[-1], "z", NZ, 1))
        down.append(shifted(down[-1], "z", NZ, -1))
    far = [
        shifted(up[-1][: cols // 2], "z", NZ, 1),
        shifted(down[-1][cols // 2 :], "z", NZ, -1),
    ]

    place, cell, hot, short, nth = places(cluster_ids, cap, NN)
    where_am_i = jnp.stack([xi, zi, yi, ci, (wi == hot).astype(I32)]).astype(I32)
    hidden_p = choose_rows(iota((tokens, 1), 0) == place[None, :], hidden)
    h_parts = [hidden_p] + [shifted(hidden_p, "x", NX, h) for h in (1, 2, 3)]

    cell = local_call(
        gate, like((2, tokens // 2), I32), (cell.reshape(2, -1),), after=(up[1], down[1], h_parts[1])
    ).reshape(-1)
    cell_of = cell[:, None] == iota((1, NW * cap), 1)
    send_ids = jnp.sum(jnp.where(cell_of, cluster_ids[:, None] + 1, 0), axis=0) - 1
    got_ids = lax.all_to_all(send_ids.reshape(NW, cap), WIDE, 0, 0, tiled=True)

    lines = local_call(
        split_lines,
        [like((centroids.shape[0], NC * width))] * NY,
        (centroids,),
        smem=(where_am_i,),
        after=(up[1], down[1]),
    )
    lines = [lines[0]] + [shifted(lines[g], "y", NY, g) for g in (1, 2, 3)]
    part = like((NY, centroids.shape[0], width))
    cent_keep, cent_send = local_call(split_cores, (part, part), lines, smem=(where_am_i,))
    cent_other = shifted(cent_send, "c", NC, 1)

    block = like((NY, NX, NW, wide_cols))
    keep, send = local_call(
        project,
        (block, block),
        (*h_parts, *up, *down[1:], *far),
        smem=(where_am_i,),
        scratch=[pltpu.VMEM((wide_cols, width), BF), pltpu.VMEM((tokens, wide_cols), F32)],
    )
    pairs = local_call(
        add_pair, [like((NX, NW, wide_cols))] * NY, (keep, shifted(send, "c", NC, 1))
    )

    local = jnp.where(got_ids >= 0, got_ids - wi * CL_DEV, -1)
    local = jnp.concatenate([local[:, :NN].T.reshape(-1), local[:, NN:].reshape(-1)])
    cent_own, cent_out = local_call(
        pick_rows,
        (like((NN, NW, width)), like((NW, extra, width))),
        (local[:, None], cent_keep, cent_other),
        smem=(where_am_i,),
        after=(up[3], down[3]),
        scratch=[
            pltpu.VMEM((NW * cap, CL_DEV), BF),
            pltpu.VMEM((CL_DEV, width), BF),
        ],
    )
    cent_in = pick(lax.all_to_all(cent_out, WIDE, 0, 0, tiled=True), hot)
    cent_pre = jnp.concatenate(
        [
            cent_own,
            cent_in.reshape(per_n, NN, width).transpose(1, 0, 2),
            jnp.broadcast_to(key_gain, (NN, 8 - per_n, width)),
        ],
        axis=1,
    )
    cents = lax.all_to_all(cent_pre, NARROW, 0, 0, tiled=True)

    own_place = ni * NW + iota((NW, 1), 0) == place[None, :]
    resid_rows = choose_rows(own_place, resid)

    sums = local_call(
        add_four,
        [like((NW, wide_cols))] * NX,
        (pairs[0], *[shifted(pairs[g], "y", NY, g) for g in (1, 2, 3)]),
    )
    q = iota((8, 1), 0)
    from_host = (short[None, :] & (nth[None, :] == q * NN + ni) & (q < per_n)).astype(BF)
    keys, res_extra = local_call(
        normalize,
        (like((NW, d)), like((8, d))),
        (
            sums[0],
            *[shifted(sums[h], "x", NX, -h) for h in (1, 2, 3)],
            resid_rows,
            cents,
            from_host,
        ),
        smem=(where_am_i,),
        scratch=[pltpu.VMEM((NW, d), F32)],
    )

    n_of = ((yi - iota((NC, NY, 1), 1)) % NY) * NC + (ci + iota((NC, NY, 1), 0)) % NC

    pieces = [res_extra] + [shifted(res_extra, "y", NY, h) for h in (1, 2, 3)]

    keys = local_call(spread, like((NW, NN, width)), (keys,), after=(pieces[1],))
    got = lax.all_to_all(keys, WIDE, 0, 0, tiled=True)
    filled = (pick(got_ids, ni, 1) >= 0).astype(F32)[:, None]
    residual = local_call(subtract, like((NW, d)), (got, cents, filled))
    parts = [residual] + [shifted(residual, "y", NY, h) for h in (1, 2, 3)]
    parts = parts + [shifted(p, "c", NC, 1) for p in parts]

    steps = 4
    rot_spec = pl.BlockSpec((d // steps, width), lambda k: (k, 0))

    def row_specs(rows):
        return [pl.BlockSpec((rows, d // steps), lambda k: (0, k))] * NN

    pieces = pieces + [shifted(p, "c", NC, 1) for p in pieces]
    ext_j = (iota((NC, NY, 8), 2) * NN + n_of).reshape(1, -1)
    choose_ext = (ext_j == iota((extra, 1), 0)).astype(BF)
    ext = local_call(
        rotate_extra,
        like((NZ, extra, width)),
        (*pieces, rotation, choose_ext),
        scratch=[pltpu.VMEM((NN * 8, width), F32)],
        grid=(steps,),
        specs=row_specs(8) + [rot_spec, whole(choose_ext.shape)],
    )
    ext = lax.all_to_all(ext, "z", 0, 0, tiled=True)
    ext = [ext] + [shifted(ext, "x", NX, -h) for h in range(1, NX)]

    gap = jnp.min(jnp.where(got_ids[:, :NN] < 0, iota((1, NN), 1), NN), axis=1)
    rank = iota((1, NN), 1)
    from_n = (rank + (rank >= gap[:, None]).astype(I32)).reshape(-1, 1)
    from_s = iota((NW, NN), 0).reshape(-1, 1)
    row_n = jnp.broadcast_to(n_of, (NC, NY, NW)).reshape(1, -1)
    row_s = iota((NC, NY, NW), 2).reshape(1, -1)
    chosen = ((from_n == row_n) & (from_s == row_s)).astype(BF)
    return local_call(
        rotate,
        like((NW * cap, width)),
        (*parts, rotation, chosen, *ext),
        smem=(where_am_i,),
        scratch=[pltpu.VMEM((NN * NW, width), F32)],
        grid=(steps,),
        specs=row_specs(NW) + [rot_spec, whole(chosen.shape)] + [whole(ext[0].shape)] * NX,
    )


def solution(mesh):
    grid = Mesh(mesh.devices.reshape(NX, NZ, NY, NC), ("x", "z", "y", "c"))
    placed = (
        P(WIDE, NARROW),
        P(WIDE, None),
        P(NARROW, WIDE),
        P(NARROW),
        P(WIDE),
        P(WIDE + NARROW, None),
        P(None, NARROW),
    )
    return jax.shard_map(
        per_device, mesh=grid, in_specs=placed, out_specs=P(WIDE, NARROW), check_vma=False
    )
```

```python
import jax
import jax.numpy as jnp
from jax import lax
from jax.experimental import pallas as pl
from jax.experimental.pallas import tpu as pltpu
from jax.sharding import Mesh, PartitionSpec as P

CL_DEV = 1024
EPS = 1e-05
NX, NZ, NY, NC = 4, 8, 4, 2
WIDE = ("x", "z")
NARROW = ("y", "c")
NN = NY * NC
NW = NX * NZ
BF = jnp.bfloat16
F32 = jnp.float32
I32 = jnp.int32


def shifted(a, axis, n, h):
    return lax.ppermute(a, axis, [(i, (i + h) % n) for i in range(n)])


def pick(a, i, axis=0):
    return lax.dynamic_index_in_dim(a, i, axis, keepdims=False)


def iota(shape, dim):
    return lax.broadcasted_iota(I32, shape, dim)


def choose_rows(onehot, a):
    return jnp.dot(onehot.astype(BF), a, preferred_element_type=F32).astype(BF)


def places(ids, cap, per_owner):
    owner = ids // CL_DEV
    onehot = (owner[:, None] == iota((1, NW), 1)).astype(I32)
    rank = jnp.sum((jnp.cumsum(onehot, axis=0) - onehot) * onehot, axis=1)
    count = jnp.sum(onehot, axis=0)
    hot = jnp.argmax(count).astype(I32)
    short = count < per_owner
    nth = jnp.cumsum(short.astype(I32)) - short.astype(I32)
    gap = jnp.where(short, nth % per_owner, per_owner)
    n_of = rank + (rank >= jnp.sum(onehot * gap[None, :], axis=1)).astype(I32)
    surplus = rank >= per_owner
    j = rank - per_owner
    host = jnp.sum(
        jnp.where(short[None, :] & (nth[None, :] == j[:, None]), iota((1, NW), 1), 0), axis=1
    )
    place = jnp.where(surplus, (j % per_owner) * NW + host, n_of * NW + owner)
    cell = owner * cap + jnp.where(surplus, rank, n_of)
    return place, cell, hot, short, nth


SMEM = pl.BlockSpec(memory_space=pltpu.SMEM)
ANY = pl.BlockSpec(memory_space=pl.ANY)
PARAMS = pltpu.CompilerParams(vmem_limit_bytes=56 * 1024 * 1024)


def like(shape, dtype=BF):
    return jax.ShapeDtypeStruct(shape, dtype)


def whole(shape):
    return pl.BlockSpec(shape, lambda i: (0,) * len(shape))


def local_call(kernel, outs, args, after=(), smem=(), scratch=(), grid=(1,), specs=None):
    return pl.pallas_call(
        kernel,
        out_shape=outs,
        grid=grid,
        in_specs=[SMEM] * len(smem) + (specs or [whole(a.shape) for a in args]) + [ANY] * len(after),
        out_specs=jax.tree.map(lambda o: whole(o.shape), outs),
        scratch_shapes=list(scratch),
        compiler_params=PARAMS,
        name=kernel.__name__,
    )(*smem, *args, *after)


def at(i, size, step):
    return pl.ds(pl.multiple_of(i * size, step), size)


def project(at_ref, *refs):
    h_refs, up, down, far = refs[:4], refs[4:8], refs[8:11], refs[11:13]
    keep, send, w_all, acc = refs[13:]
    z, y, c = at_ref[1], at_ref[2], at_ref[3]
    cols = up[0].shape[0]
    for h in range(4):
        w_all[at(lax.rem(z + NZ - h, NZ), cols, 16), :] = up[h][...]
        if h:
            w_all[at(lax.rem(z + h, NZ), cols, 16), :] = down[h - 1][...]
    across = lax.rem(z + 4, NZ) * cols
    w_all[pl.ds(pl.multiple_of(across, 16), cols // 2), :] = far[0][...]
    w_all[pl.ds(pl.multiple_of(across + cols // 2, 16), cols // 2), :] = far[1][...]
    for h in range(NX):
        acc[...] = lax.dot_general(
            h_refs[h][...], w_all[...], (((1,), (1,)), ((), ())), preferred_element_type=F32
        )
        for g in range(NY):
            n = lax.rem(y + g, NY) * NC
            keep[g, h] = acc[at(n + c, NW, 32), :].astype(BF)
            send[g, h] = acc[at(n + 1 - c, NW, 32), :].astype(BF)


def add_pair(keep, other, *outs):
    for g in range(NY):
        outs[g][...] = (keep[g].astype(F32) + other[g].astype(F32)).astype(BF)


def add_four(*refs):
    outs = refs[-NX:]
    for h in range(NX):
        total = refs[0][h].astype(F32)
        for g in range(1, NY):
            total = total + refs[g][h].astype(F32)
        outs[h][...] = total.astype(BF)


def hold(*refs):
    pass


def later(a, *after):
    return pl.pallas_call(
        hold,
        out_shape=like(a.shape, a.dtype),
        in_specs=[ANY] * (1 + len(after)),
        out_specs=ANY,
        input_output_aliases={0: 0},
        compiler_params=PARAMS,
        name="later",
    )(a, *after)


def normalize(at_ref, b0, b1, b2, b3, resid, cents, from_host, keys, extra, stream):
    x = at_ref[0]
    span = b0.shape[1]
    width = cents.shape[2]
    for h, b in enumerate((b0, b1, b2, b3)):
        where = at(lax.rem(x + h, NX), span, 128)
        stream[:, where] = resid[:, where].astype(F32) + b[...].astype(F32)
    value = stream[...]
    scale = lax.rsqrt(jnp.mean(value * value, axis=1, keepdims=True) + EPS)
    for n in range(NN):
        part = slice(n * width, (n + 1) * width)
        tail = cents[n, NW:, :].astype(F32)
        key = (stream[:, part] * scale * tail[7:8]).astype(BF)
        keys[:, part] = key
        chosen = jnp.dot(from_host[...], key, preferred_element_type=F32)
        extra[:, part] = (chosen - tail).astype(BF)


def spread(keys, *refs):
    out = refs[-1]
    width = out.shape[2]
    for n in range(NN):
        out[:, n, :] = keys[:, n * width : (n + 1) * width]


def subtract(keys, cents, filled, out):
    width = cents.shape[2]
    for n in range(NN):
        part = slice(n * width, (n + 1) * width)
        diff = keys[:, n, :].astype(F32) - cents[n, :NW, :].astype(F32)
        out[:, part] = jnp.where(filled[...] > 0, diff, 0.0).astype(BF)


def split_lines(at_ref, cent, *refs):
    outs = refs[-NY:]
    span = outs[0].shape[1]
    for g in range(NY):
        outs[g][...] = cent[:, at(lax.rem(at_ref[2] + g, NY), span, 128)]


def split_cores(at_ref, *refs):
    parts, (keep, send) = refs[:NY], refs[-2:]
    c, width = at_ref[3], keep.shape[2]
    for h in range(NY):
        keep[h] = parts[h][:, at(c, width, 128)]
        send[h] = parts[h][:, at(1 - c, width, 128)]


def pick_rows(at_ref, ids, keep, other, *refs):
    own, away, hits, tile = refs[-4:]
    y, c = at_ref[2], at_ref[3]
    slots, (rows, width) = ids.shape[0], keep.shape[1:]
    for k, part in enumerate((keep, other)):
        for h in range(NY):
            n = lax.rem(y + NY - h, NY) * NC + (1 - c if k else c)
            base = (k * NY + h) * rows
            tile[base : base + rows, :] = part[h]
            cluster = n * rows + lax.broadcasted_iota(I32, (slots, rows), 1)
            hits[:, base : base + rows] = (ids[...] == cluster).astype(F32).astype(BF)
    mine = own.shape[0] * own.shape[1]
    out = jnp.dot(hits[:mine, :], tile[...], preferred_element_type=F32).astype(BF)
    own[...] = out.reshape(own.shape)
    out = jnp.dot(hits[mine:, :], tile[...], preferred_element_type=F32)
    away[...] = out.reshape(away.shape).astype(BF)


def accumulate(parts, rot, acc):
    lhs = jnp.concatenate([p[...] for p in parts], axis=0)
    new = jnp.dot(lhs, rot[...], preferred_element_type=F32)

    @pl.when(pl.program_id(0) == 0)
    def _():
        acc[...] = new

    @pl.when(pl.program_id(0) > 0)
    def _():
        acc[...] += new


def rotate_extra(*refs):
    parts, (rot, chosen, out, acc) = refs[:8], refs[8:]
    accumulate(parts, rot, acc)

    @pl.when(pl.program_id(0) == pl.num_programs(0) - 1)
    def _():
        rows = acc[...].astype(BF)
        picked = jnp.dot(chosen[...], rows, preferred_element_type=F32).astype(BF)
        for g in range(NZ):
            out[g] = picked


def rotate(at_ref, *refs):
    parts, (rot, chosen), ext, (out, acc) = refs[:8], refs[8:10], refs[10:14], refs[14:]
    accumulate(parts, rot, acc)

    @pl.when(pl.program_id(0) == pl.num_programs(0) - 1)
    def _():
        x, hot = at_ref[0], at_ref[4]
        acc[...] = jnp.dot(chosen[...], acc[...].astype(BF), preferred_element_type=F32)
        extra = ext[0].shape[1]
        cap = NN + extra
        for h in range(NX):
            first = lax.rem(x + h, NX) * NZ
            for g in range(NZ):
                tail = jnp.where(hot > 0, ext[h][g].astype(F32), 0.0)
                rows = jnp.concatenate([acc[at(first + g, NN, 8), :], tail], axis=0)
                out[at(first + g, cap, 32), :] = rows.astype(BF)


def per_device(hidden, resid, w_out, key_gain, cluster_ids, centroids, rotation):
    xi, zi, yi, ci = (lax.axis_index(a) for a in ("x", "z", "y", "c"))
    ni = yi * NC + ci
    wi = xi * NZ + zi
    tokens, width = hidden.shape
    d = width * NN
    cap = 4 * tokens // NW
    cols = w_out.shape[1]
    wide_cols = NZ * cols
    extra = cap - NN
    per_n = extra // NN

    w_t = w_out.T
    up, down = [w_t], [w_t]
    for _ in range(3):
        up.append(shifted(up[-1], "z", NZ, 1))
        down.append(shifted(down[-1], "z", NZ, -1))
    far = [
        shifted(up[-1][: cols // 2], "z", NZ, 1),
        shifted(down[-1][cols // 2 :], "z", NZ, -1),
    ]

    place, cell, hot, short, nth = places(cluster_ids, cap, NN)
    where_am_i = jnp.stack([xi, zi, yi, ci, (wi == hot).astype(I32)]).astype(I32)
    hidden_p = choose_rows(iota((tokens, 1), 0) == place[None, :], hidden)
    h_parts = [hidden_p] + [shifted(hidden_p, "x", NX, h) for h in (1, 2, 3)]

    cell_of = cell[:, None] == iota((1, NW * cap), 1)
    send_ids = jnp.sum(jnp.where(cell_of, cluster_ids[:, None] + 1, 0), axis=0) - 1
    send_ids = later(send_ids.reshape(NW, cap), up[3], down[3], *h_parts[1:])
    got_ids = lax.all_to_all(send_ids, WIDE, 0, 0, tiled=True)

    lines = local_call(
        split_lines,
        [like((centroids.shape[0], NC * width))] * NY,
        (centroids,),
        smem=(where_am_i,),
        after=(up[1], down[1]),
    )
    lines = [lines[0]] + [shifted(lines[g], "y", NY, g) for g in (1, 2, 3)]
    part = like((NY, centroids.shape[0], width))
    cent_keep, cent_send = local_call(split_cores, (part, part), lines, smem=(where_am_i,), after=(up[3], down[3]))
    cent_other = shifted(cent_send, "c", NC, 1)

    block = like((NY, NX, NW, wide_cols))
    keep, send = local_call(
        project,
        (block, block),
        (*h_parts, *up, *down[1:], *far),
        smem=(where_am_i,),
        scratch=[pltpu.VMEM((wide_cols, width), BF), pltpu.VMEM((tokens, wide_cols), F32)],
    )
    pairs = local_call(
        add_pair, [like((NX, NW, wide_cols))] * NY, (keep, shifted(send, "c", NC, 1))
    )

    local = jnp.where(got_ids >= 0, got_ids - wi * CL_DEV, -1)
    local = jnp.concatenate([local[:, :NN].T.reshape(-1), local[:, NN:].reshape(-1)])
    cent_own, cent_out = local_call(
        pick_rows,
        (like((NN, NW, width)), like((NW, extra, width))),
        (local[:, None], cent_keep, cent_other),
        smem=(where_am_i,),
        after=(send,),
        scratch=[
            pltpu.VMEM((NW * cap, CL_DEV), BF),
            pltpu.VMEM((CL_DEV, width), BF),
        ],
    )
    cent_in = pick(lax.all_to_all(later(cent_out, pairs[1]), WIDE, 0, 0, tiled=True), hot)
    cent_pre = jnp.concatenate(
        [
            cent_own,
            cent_in.reshape(per_n, NN, width).transpose(1, 0, 2),
            jnp.broadcast_to(key_gain, (NN, 8 - per_n, width)),
        ],
        axis=1,
    )
    cents = lax.all_to_all(cent_pre, NARROW, 0, 0, tiled=True)

    own_place = ni * NW + iota((NW, 1), 0) == place[None, :]
    resid_rows = choose_rows(own_place, resid)

    sums = local_call(
        add_four,
        [like((NW, wide_cols))] * NX,
        (pairs[0], *[shifted(pairs[g], "y", NY, g) for g in (1, 2, 3)]),
    )
    q = iota((8, 1), 0)
    from_host = (short[None, :] & (nth[None, :] == q * NN + ni) & (q < per_n)).astype(BF)
    keys, res_extra = local_call(
        normalize,
        (like((NW, d)), like((8, d))),
        (
            sums[0],
            *[shifted(sums[h], "x", NX, -h) for h in (1, 2, 3)],
            resid_rows,
            cents,
            from_host,
        ),
        smem=(where_am_i,),
        scratch=[pltpu.VMEM((NW, d), F32)],
    )

    n_of = ((yi - iota((NC, NY, 1), 1)) % NY) * NC + (ci + iota((NC, NY, 1), 0)) % NC

    pieces = [res_extra] + [shifted(res_extra, "y", NY, h) for h in (1, 2, 3)]

    keys = local_call(spread, like((NW, NN, width)), (keys,))
    got = lax.all_to_all(keys, WIDE, 0, 0, tiled=True)
    filled = (pick(got_ids, ni, 1) >= 0).astype(F32)[:, None]
    residual = local_call(subtract, like((NW, d)), (got, cents, filled))
    parts = [residual] + [shifted(residual, "y", NY, h) for h in (1, 2, 3)]
    parts = parts + [shifted(p, "c", NC, 1) for p in parts]

    steps = 4
    rot_spec = pl.BlockSpec((d // steps, width), lambda k: (k, 0))

    def row_specs(rows):
        return [pl.BlockSpec((rows, d // steps), lambda k: (0, k))] * NN

    pieces = pieces + [shifted(p, "c", NC, 1) for p in pieces]
    ext_j = (iota((NC, NY, 8), 2) * NN + n_of).reshape(1, -1)
    choose_ext = (ext_j == iota((extra, 1), 0)).astype(BF)
    ext = local_call(
        rotate_extra,
        like((NZ, extra, width)),
        (*pieces, rotation, choose_ext),
        scratch=[pltpu.VMEM((NN * 8, width), F32)],
        grid=(steps,),
        specs=row_specs(8) + [rot_spec, whole(choose_ext.shape)],
    )
    ext = lax.all_to_all(ext, "z", 0, 0, tiled=True)
    ext = [ext] + [shifted(ext, "x", NX, -h) for h in range(1, NX)]

    gap = jnp.min(jnp.where(got_ids[:, :NN] < 0, iota((1, NN), 1), NN), axis=1)
    rank = iota((1, NN), 1)
    from_n = (rank + (rank >= gap[:, None]).astype(I32)).reshape(-1, 1)
    from_s = iota((NW, NN), 0).reshape(-1, 1)
    row_n = jnp.broadcast_to(n_of, (NC, NY, NW)).reshape(1, -1)
    row_s = iota((NC, NY, NW), 2).reshape(1, -1)
    chosen = ((from_n == row_n) & (from_s == row_s)).astype(BF)
    return local_call(
        rotate,
        like((NW * cap, width)),
        (*parts, rotation, chosen, *ext),
        smem=(where_am_i,),
        scratch=[pltpu.VMEM((NN * NW, width), F32)],
        grid=(steps,),
        specs=row_specs(NW) + [rot_spec, whole(chosen.shape)] + [whole(ext[0].shape)] * NX,
    )


def solution(mesh):
    grid = Mesh(mesh.devices.reshape(NX, NZ, NY, NC), ("x", "z", "y", "c"))
    placed = (
        P(WIDE, NARROW),
        P(WIDE, None),
        P(NARROW, WIDE),
        P(NARROW),
        P(WIDE),
        P(WIDE + NARROW, None),
        P(None, NARROW),
    )
    return jax.shard_map(
        per_device, mesh=grid, in_specs=placed, out_specs=P(WIDE, NARROW), check_vma=False
    )
```

```python
import jax
import jax.numpy as jnp
from jax import lax
from jax.experimental import pallas as pl
from jax.experimental.pallas import tpu as pltpu
from jax.sharding import Mesh, PartitionSpec as P

CL_DEV = 1024
EPS = 1e-05
NX, NZ, NY, NC = 4, 8, 4, 2
WIDE = ("x", "z")
NARROW = ("y", "c")
NN = NY * NC
NW = NX * NZ
BF = jnp.bfloat16
F32 = jnp.float32
I32 = jnp.int32


def shifted(a, axis, n, h):
    return lax.ppermute(a, axis, [(i, (i + h) % n) for i in range(n)])


def pick(a, i, axis=0):
    return lax.dynamic_index_in_dim(a, i, axis, keepdims=False)


def iota(shape, dim):
    return lax.broadcasted_iota(I32, shape, dim)


def choose_rows(onehot, a):
    return jnp.dot(onehot.astype(BF), a, preferred_element_type=F32).astype(BF)


def places(ids, cap, per_owner):
    owner = ids // CL_DEV
    onehot = (owner[:, None] == iota((1, NW), 1)).astype(I32)
    rank = jnp.sum((jnp.cumsum(onehot, axis=0) - onehot) * onehot, axis=1)
    count = jnp.sum(onehot, axis=0)
    hot = jnp.argmax(count).astype(I32)
    short = count < per_owner
    nth = jnp.cumsum(short.astype(I32)) - short.astype(I32)
    gap = jnp.where(short, nth % per_owner, per_owner)
    n_of = rank + (rank >= jnp.sum(onehot * gap[None, :], axis=1)).astype(I32)
    surplus = rank >= per_owner
    j = rank - per_owner
    host = jnp.sum(
        jnp.where(short[None, :] & (nth[None, :] == j[:, None]), iota((1, NW), 1), 0), axis=1
    )
    place = jnp.where(surplus, (j % per_owner) * NW + host, n_of * NW + owner)
    cell = owner * cap + jnp.where(surplus, rank, n_of)
    return place, cell, hot, short, nth


SMEM = pl.BlockSpec(memory_space=pltpu.SMEM)
ANY = pl.BlockSpec(memory_space=pl.ANY)
PARAMS = pltpu.CompilerParams(vmem_limit_bytes=56 * 1024 * 1024)


def like(shape, dtype=BF):
    return jax.ShapeDtypeStruct(shape, dtype)


def whole(shape):
    return pl.BlockSpec(shape, lambda i: (0,) * len(shape))


def local_call(kernel, outs, args, after=(), smem=(), scratch=(), grid=(1,), specs=None):
    return pl.pallas_call(
        kernel,
        out_shape=outs,
        grid=grid,
        in_specs=[SMEM] * len(smem) + (specs or [whole(a.shape) for a in args]) + [ANY] * len(after),
        out_specs=jax.tree.map(lambda o: whole(o.shape), outs),
        scratch_shapes=list(scratch),
        compiler_params=PARAMS,
        name=kernel.__name__,
    )(*smem, *args, *after)


def at(i, size, step):
    return pl.ds(pl.multiple_of(i * size, step), size)


def project(at_ref, *refs):
    h_refs, up, down, far = refs[:4], refs[4:8], refs[8:11], refs[11:13]
    keep, send, w_all, acc = refs[-4:]
    z, y, c = at_ref[1], at_ref[2], at_ref[3]
    cols = up[0].shape[0]
    for h in range(4):
        w_all[at(lax.rem(z + NZ - h, NZ), cols, 16), :] = up[h][...]
        if h:
            w_all[at(lax.rem(z + h, NZ), cols, 16), :] = down[h - 1][...]
    across = lax.rem(z + 4, NZ) * cols
    w_all[pl.ds(pl.multiple_of(across, 16), cols // 2), :] = far[0][...]
    w_all[pl.ds(pl.multiple_of(across + cols // 2, 16), cols // 2), :] = far[1][...]
    for h in range(NX):
        acc[...] = lax.dot_general(
            h_refs[h][...], w_all[...], (((1,), (1,)), ((), ())), preferred_element_type=F32
        )
        for g in range(NY):
            n = lax.rem(y + g, NY) * NC
            keep[g, h] = acc[at(n + c, NW, 32), :].astype(BF)
            send[g, h] = acc[at(n + 1 - c, NW, 32), :].astype(BF)


def add_pair(keep, other, *outs):
    for g in range(NY):
        outs[g][...] = (keep[g].astype(F32) + other[g].astype(F32)).astype(BF)


def add_four(*refs):
    outs = refs[-NX:]
    for h in range(NX):
        total = refs[0][h].astype(F32)
        for g in range(1, NY):
            total = total + refs[g][h].astype(F32)
        outs[h][...] = total.astype(BF)


def hold(*refs):
    pass


def later(a, *after):
    return pl.pallas_call(
        hold,
        out_shape=like(a.shape, a.dtype),
        in_specs=[ANY] * (1 + len(after)),
        out_specs=ANY,
        input_output_aliases={0: 0},
        compiler_params=PARAMS,
        name="later",
    )(a, *after)


def normalize(at_ref, b0, b1, b2, b3, resid, from_host, gain, other, keys, extra, stream):
    x, y, c = at_ref[0], at_ref[2], at_ref[3]
    span = b0.shape[1]
    width = gain.shape[2]
    for h, b in enumerate((b0, b1, b2, b3)):
        where = at(lax.rem(x + h, NX), span, 128)
        stream[:, where] = resid[:, where].astype(F32) + b[...].astype(F32)
    value = stream[...]
    scale = lax.rsqrt(jnp.mean(value * value, axis=1, keepdims=True) + EPS)
    for k, gains in enumerate((gain, other)):
        for h in range(NY):
            n = lax.rem(y + NY - h, NY) * NC + (1 - c if k else c)
            where = at(n, width, 128)
            row = gains[h].astype(F32)[:1]
            keys[:, where] = (stream[:, where] * scale * row).astype(BF)
    chosen = jnp.dot(from_host[...], keys[...], preferred_element_type=F32)
    extra[...] = chosen.astype(BF)


def spread(keys, *refs):
    out = refs[-1]
    width = out.shape[2]
    for n in range(NN):
        out[:, n, :] = keys[:, n * width : (n + 1) * width]


def subtract(keys, cents, filled, out):
    width = cents.shape[2]
    for n in range(NN):
        part = slice(n * width, (n + 1) * width)
        diff = keys[:, n, :].astype(F32) - cents[n, :NW, :].astype(F32)
        out[:, part] = jnp.where(filled[...] > 0, diff, 0.0).astype(BF)


def split_lines(at_ref, cent, gain, *refs):
    outs = refs[-NY:]
    rows, span = cent.shape[0], outs[0].shape[1]
    for g in range(NY):
        outs[g][:rows, :] = cent[:, at(lax.rem(at_ref[2] + g, NY), span, 128)]
        outs[g][rows:, :] = jnp.broadcast_to(gain[...], (16, span))


def split_cores(at_ref, *refs):
    parts, (keep, send) = refs[:NY], refs[-2:]
    c, width = at_ref[3], keep.shape[2]
    rows = keep.shape[1] - 16
    for h in range(NY):
        keep[h, :rows] = parts[h][:rows, at(c, width, 128)]
        send[h, :rows] = parts[h][:rows, at(1 - c, width, 128)]
        keep[h, rows:] = parts[h][rows:, :width]
        send[h, rows:] = parts[h][rows:, :width]


def pick_rows(at_ref, ids, keep, other, *refs):
    own, away, hits, tile = refs[-4:]
    y, c = at_ref[2], at_ref[3]
    slots, rows = ids.shape[0], keep.shape[1] - 16
    for k, part in enumerate((keep, other)):
        for h in range(NY):
            n = lax.rem(y + NY - h, NY) * NC + (1 - c if k else c)
            base = (k * NY + h) * rows
            tile[base : base + rows, :] = part[h, :rows]
            cluster = n * rows + lax.broadcasted_iota(I32, (slots, rows), 1)
            hits[:, base : base + rows] = (ids[...] == cluster).astype(F32).astype(BF)
    mine = own.shape[0] * own.shape[1]
    out = jnp.dot(hits[:mine, :], tile[...], preferred_element_type=F32).astype(BF)
    own[...] = out.reshape(own.shape)
    out = jnp.dot(hits[mine:, :], tile[...], preferred_element_type=F32)
    away[...] = out.reshape(away.shape).astype(BF)


def accumulate(parts, rot, acc):
    lhs = jnp.concatenate([p[...] for p in parts], axis=0)
    new = jnp.dot(lhs, rot[...], preferred_element_type=F32)

    @pl.when(pl.program_id(0) == 0)
    def _():
        acc[...] = new

    @pl.when(pl.program_id(0) > 0)
    def _():
        acc[...] += new


def rotate_extra(*refs):
    parts, (rot, chosen, cents, out, acc) = refs[:8], refs[8:]
    keys = jnp.concatenate([p[...] for p in parts], axis=0)
    keys = jnp.dot(chosen[...], keys, preferred_element_type=F32)
    centre = jnp.concatenate([cents[n, NW:, :] for n in range(cents.shape[0])], axis=1)
    rows = (keys - centre.astype(F32)).astype(BF)
    new = jnp.dot(rows, rot[...], preferred_element_type=F32)

    @pl.when(pl.program_id(0) == 0)
    def _():
        acc[...] = new

    @pl.when(pl.program_id(0) > 0)
    def _():
        acc[...] += new

    @pl.when(pl.program_id(0) == pl.num_programs(0) - 1)
    def _():
        for g in range(NZ):
            out[g] = acc[...].astype(BF)


def rotate(at_ref, *refs):
    parts, (rot, chosen), ext, (out, acc) = refs[:8], refs[8:10], refs[10:14], refs[14:]
    accumulate(parts, rot, acc)

    @pl.when(pl.program_id(0) == pl.num_programs(0) - 1)
    def _():
        x, hot = at_ref[0], at_ref[4]
        acc[...] = jnp.dot(chosen[...], acc[...].astype(BF), preferred_element_type=F32)
        extra = ext[0].shape[1]
        cap = NN + extra
        for h in range(NX):
            first = lax.rem(x + h, NX) * NZ
            for g in range(NZ):
                tail = jnp.where(hot > 0, ext[h][g].astype(F32), 0.0)
                rows = jnp.concatenate([acc[at(first + g, NN, 8), :], tail], axis=0)
                out[at(first + g, cap, 32), :] = rows.astype(BF)


def per_device(hidden, resid, w_out, key_gain, cluster_ids, centroids, rotation):
    xi, zi, yi, ci = (lax.axis_index(a) for a in ("x", "z", "y", "c"))
    ni = yi * NC + ci
    wi = xi * NZ + zi
    tokens, width = hidden.shape
    d = width * NN
    cap = 4 * tokens // NW
    cols = w_out.shape[1]
    wide_cols = NZ * cols
    extra = cap - NN
    per_n = extra // NN

    w_t = w_out.T
    up, down = [w_t], [w_t]
    for _ in range(2):
        up.append(shifted(up[-1], "z", NZ, 1))
        down.append(shifted(down[-1], "z", NZ, -1))
    place, cell, hot, short, nth = places(cluster_ids, cap, NN)
    where_am_i = jnp.stack([xi, zi, yi, ci, (wi == hot).astype(I32)]).astype(I32)
    hidden_p = choose_rows(iota((tokens, 1), 0) == place[None, :], hidden)
    h_parts = [hidden_p] + [shifted(hidden_p, "x", NX, h) for h in (1, 2, 3)]

    up.append(shifted(later(up[2], h_parts[1]), "z", NZ, 1))
    down.append(shifted(down[2], "z", NZ, -1))
    near = later(up[3][: cols // 2], h_parts[2], h_parts[3])
    far = [shifted(near, "z", NZ, 1), shifted(down[3][cols // 2 :], "z", NZ, -1)]

    cell_of = cell[:, None] == iota((1, NW * cap), 1)
    send_ids = jnp.sum(jnp.where(cell_of, cluster_ids[:, None] + 1, 0), axis=0) - 1
    send_ids = later(send_ids.reshape(NW, cap), up[1], down[1])
    got_ids = lax.all_to_all(send_ids, WIDE, 0, 0, tiled=True)

    lines = local_call(
        split_lines,
        [like((centroids.shape[0] + 16, NC * width))] * NY,
        (centroids, jnp.tile(key_gain, NC)[None, :]),
        smem=(where_am_i,),
        after=(up[1], down[1]),
    )
    lines = [lines[0]] + [shifted(lines[g], "y", NY, g) for g in (1, 2, 3)]
    part = like((NY, centroids.shape[0] + 16, width))
    cent_keep, cent_send = local_call(split_cores, (part, part), lines, smem=(where_am_i,))
    cent_other = shifted(cent_send, "c", NC, 1)

    block = like((NY, NX, NW, wide_cols))
    keep, send = local_call(
        project,
        (block, block),
        (*h_parts, *up, *down[1:], *far),
        smem=(where_am_i,),
        after=(got_ids, cent_keep),
        scratch=[pltpu.VMEM((wide_cols, width), BF), pltpu.VMEM((tokens, wide_cols), F32)],
    )
    pairs = local_call(
        add_pair, [like((NX, NW, wide_cols))] * NY, (keep, shifted(send, "c", NC, 1))
    )

    local = jnp.where(got_ids >= 0, got_ids - wi * CL_DEV, -1)
    local = jnp.concatenate([local[:, :NN].T.reshape(-1), local[:, NN:].reshape(-1)])
    cent_own, cent_out = local_call(
        pick_rows,
        (like((NN, NW, width)), like((NW, extra, width))),
        (local[:, None], cent_keep, cent_other),
        smem=(where_am_i,),
        after=(send,),
        scratch=[
            pltpu.VMEM((NW * cap, CL_DEV), BF),
            pltpu.VMEM((CL_DEV, width), BF),
        ],
    )
    cent_in = pick(lax.all_to_all(cent_out, WIDE, 0, 0, tiled=True), hot)
    cent_pre = jnp.concatenate(
        [cent_own, jnp.broadcast_to(cent_in[None], (NN, extra, width))], axis=1
    )
    cents = lax.all_to_all(cent_pre, NARROW, 0, 0, tiled=True)

    own_place = ni * NW + iota((NW, 1), 0) == place[None, :]
    resid_rows = choose_rows(own_place, resid)

    sums = local_call(
        add_four,
        [like((NW, wide_cols))] * NX,
        (pairs[0], *[shifted(pairs[g], "y", NY, g) for g in (1, 2, 3)]),
    )
    q = iota((8, 1), 0)
    from_host = (short[None, :] & (nth[None, :] == q * NN + ni) & (q < per_n)).astype(BF)
    blocks = [
        sums[0],
        *[shifted(sums[h], "x", NX, -h) for h in (1, 2, 3)],
        resid_rows,
        from_host,
    ]
    gain_at = centroids.shape[0] // 16
    keys, key_extra = local_call(
        normalize,
        (like((NW, d)), like((8, d))),
        (*blocks, cent_keep, cent_other),
        smem=(where_am_i,),
        scratch=[pltpu.VMEM((NW, d), F32)],
        specs=[whole(b.shape) for b in blocks]
        + [pl.BlockSpec((NY, 16, width), lambda i: (0, gain_at, 0))] * 2,
    )

    n_of = ((yi - iota((NC, NY, 1), 1)) % NY) * NC + (ci + iota((NC, NY, 1), 0)) % NC

    pieces = [key_extra] + [shifted(key_extra, "y", NY, h) for h in (1, 2, 3)]

    keys = local_call(spread, like((NW, NN, width)), (keys,))
    got = lax.all_to_all(keys, WIDE, 0, 0, tiled=True)
    filled = (pick(got_ids, ni, 1) >= 0).astype(F32)[:, None]
    residual = local_call(subtract, like((NW, d)), (got, cents, filled))
    parts = [residual] + [shifted(residual, "y", NY, h) for h in (1, 2, 3)]
    parts = parts + [shifted(p, "c", NC, 1) for p in parts]

    steps = 4
    rot_spec = pl.BlockSpec((d // steps, width), lambda k: (k, 0))

    def row_specs(rows):
        return [pl.BlockSpec((rows, d // steps), lambda k: (0, k))] * NN

    pieces = pieces + [shifted(p, "c", NC, 1) for p in pieces]
    ext_j = (iota((NC, NY, 8), 2) * NN + n_of).reshape(1, -1)
    choose_ext = (ext_j == iota((extra, 1), 0)).astype(BF)
    ext = local_call(
        rotate_extra,
        like((NZ, extra, width)),
        (*pieces, rotation, choose_ext, cents),
        scratch=[pltpu.VMEM((extra, width), F32)],
        grid=(steps,),
        specs=row_specs(8)
        + [rot_spec, whole(choose_ext.shape)]
        + [pl.BlockSpec((NN // steps, NW + extra, width), lambda k: (k, 0, 0))],
    )
    ext = lax.all_to_all(ext, "z", 0, 0, tiled=True)
    ext = [ext] + [shifted(ext, "x", NX, -h) for h in range(1, NX)]

    gap = jnp.min(jnp.where(got_ids[:, :NN] < 0, iota((1, NN), 1), NN), axis=1)
    rank = iota((1, NN), 1)
    from_n = (rank + (rank >= gap[:, None]).astype(I32)).reshape(-1, 1)
    from_s = iota((NW, NN), 0).reshape(-1, 1)
    row_n = jnp.broadcast_to(n_of, (NC, NY, NW)).reshape(1, -1)
    row_s = iota((NC, NY, NW), 2).reshape(1, -1)
    chosen = ((from_n == row_n) & (from_s == row_s)).astype(BF)
    return local_call(
        rotate,
        like((NW * cap, width)),
        (*parts, rotation, chosen, *ext),
        smem=(where_am_i,),
        scratch=[pltpu.VMEM((NN * NW, width), F32)],
        grid=(steps,),
        specs=row_specs(NW) + [rot_spec, whole(chosen.shape)] + [whole(ext[0].shape)] * NX,
    )


def solution(mesh):
    grid = Mesh(mesh.devices.reshape(NX, NZ, NY, NC), ("x", "z", "y", "c"))
    placed = (
        P(WIDE, NARROW),
        P(WIDE, None),
        P(NARROW, WIDE),
        P(NARROW),
        P(WIDE),
        P(WIDE + NARROW, None),
        P(None, NARROW),
    )
    return jax.shard_map(
        per_device, mesh=grid, in_specs=placed, out_specs=P(WIDE, NARROW), check_vma=False
    )
```

```python
import jax
import jax.numpy as jnp
from jax import lax
from jax.experimental import pallas as pl
from jax.experimental.pallas import tpu as pltpu
from jax.sharding import Mesh, PartitionSpec as P

CL_DEV = 1024
EPS = 1e-05
NX, NZ, NY, NC = 4, 8, 4, 2
WIDE = ("x", "z")
NARROW = ("y", "c")
NN = NY * NC
NW = NX * NZ
BF = jnp.bfloat16
F32 = jnp.float32
I32 = jnp.int32


def shifted(a, axis, n, h):
    return lax.ppermute(a, axis, [(i, (i + h) % n) for i in range(n)])


def pick(a, i, axis=0):
    return lax.dynamic_index_in_dim(a, i, axis, keepdims=False)


def iota(shape, dim):
    return lax.broadcasted_iota(I32, shape, dim)


def choose_rows(onehot, a):
    return jnp.dot(onehot.astype(BF), a, preferred_element_type=F32).astype(BF)


def places(ids, cap, per_owner):
    owner = ids // CL_DEV
    onehot = (owner[:, None] == iota((1, NW), 1)).astype(I32)
    rank = jnp.sum((jnp.cumsum(onehot, axis=0) - onehot) * onehot, axis=1)
    count = jnp.sum(onehot, axis=0)
    hot = jnp.argmax(count).astype(I32)
    short = count < per_owner
    nth = jnp.cumsum(short.astype(I32)) - short.astype(I32)
    gap = jnp.where(short, nth % per_owner, per_owner)
    n_of = rank + (rank >= jnp.sum(onehot * gap[None, :], axis=1)).astype(I32)
    surplus = rank >= per_owner
    j = rank - per_owner
    host = jnp.sum(
        jnp.where(short[None, :] & (nth[None, :] == j[:, None]), iota((1, NW), 1), 0), axis=1
    )
    place = jnp.where(surplus, (j % per_owner) * NW + host, n_of * NW + owner)
    cell = owner * cap + jnp.where(surplus, rank, n_of)
    return place, cell, hot, short, nth


SMEM = pl.BlockSpec(memory_space=pltpu.SMEM)
ANY = pl.BlockSpec(memory_space=pl.ANY)
PARAMS = pltpu.CompilerParams(vmem_limit_bytes=56 * 1024 * 1024)


def like(shape, dtype=BF):
    return jax.ShapeDtypeStruct(shape, dtype)


def whole(shape):
    return pl.BlockSpec(shape, lambda i: (0,) * len(shape))


def local_call(kernel, outs, args, after=(), smem=(), scratch=(), grid=(1,), specs=None):
    return pl.pallas_call(
        kernel,
        out_shape=outs,
        grid=grid,
        in_specs=[SMEM] * len(smem) + (specs or [whole(a.shape) for a in args]) + [ANY] * len(after),
        out_specs=jax.tree.map(lambda o: whole(o.shape), outs),
        scratch_shapes=list(scratch),
        compiler_params=PARAMS,
        name=kernel.__name__,
    )(*smem, *args, *after)


def at(i, size, step):
    return pl.ds(pl.multiple_of(i * size, step), size)


def project(at_ref, *refs):
    h_refs, up, down, far = refs[:4], refs[4:8], refs[8:11], refs[11:13]
    keep, send, w_all, acc = refs[-4:]
    z, y, c = at_ref[1], at_ref[2], at_ref[3]
    cols = up[0].shape[0]
    for h in range(4):
        w_all[at(lax.rem(z + NZ - h, NZ), cols, 16), :] = up[h][...]
        if h:
            w_all[at(lax.rem(z + h, NZ), cols, 16), :] = down[h - 1][...]
    across = lax.rem(z + 4, NZ) * cols
    w_all[pl.ds(pl.multiple_of(across, 16), cols // 2), :] = far[0][...]
    w_all[pl.ds(pl.multiple_of(across + cols // 2, 16), cols // 2), :] = far[1][...]
    for h in range(NX):
        acc[...] = lax.dot_general(
            h_refs[h][...], w_all[...], (((1,), (1,)), ((), ())), preferred_element_type=F32
        )
        for g in range(NY):
            n = lax.rem(y + g, NY) * NC
            keep[g, h] = acc[at(n + c, NW, 32), :].astype(BF)
            send[g, h] = acc[at(n + 1 - c, NW, 32), :].astype(BF)


def add_pair(keep, other, *outs):
    for g in range(NY):
        outs[g][...] = (keep[g].astype(F32) + other[g].astype(F32)).astype(BF)


def add_four(*refs):
    outs = refs[-NX:]
    for h in range(NX):
        total = refs[0][h].astype(F32)
        for g in range(1, NY):
            total = total + refs[g][h].astype(F32)
        outs[h][...] = total.astype(BF)


def hold(*refs):
    pass


def later(a, *after):
    return pl.pallas_call(
        hold,
        out_shape=like(a.shape, a.dtype),
        in_specs=[ANY] * (1 + len(after)),
        out_specs=ANY,
        input_output_aliases={0: 0},
        compiler_params=PARAMS,
        name="later",
    )(a, *after)


def normalize(at_ref, b0, b1, b2, b3, resid, from_host, gain, other, keys, extra, stream):
    x, y, c = at_ref[0], at_ref[2], at_ref[3]
    span = b0.shape[1]
    width = gain.shape[2]
    for h, b in enumerate((b0, b1, b2, b3)):
        where = at(lax.rem(x + h, NX), span, 128)
        stream[:, where] = resid[:, where].astype(F32) + b[...].astype(F32)
    value = stream[...]
    scale = lax.rsqrt(jnp.mean(value * value, axis=1, keepdims=True) + EPS)
    for k, gains in enumerate((gain, other)):
        for h in range(NY):
            n = lax.rem(y + NY - h, NY) * NC + (1 - c if k else c)
            where = at(n, width, 128)
            row = gains[h].astype(F32)[:1]
            keys[:, where] = (stream[:, where] * scale * row).astype(BF)
    chosen = jnp.dot(from_host[...], keys[...], preferred_element_type=F32)
    extra[...] = chosen.astype(BF)


def spread(keys, *refs):
    out = refs[-1]
    width = out.shape[2]
    for n in range(NN):
        out[:, n, :] = keys[:, n * width : (n + 1) * width]


def subtract(keys, cents, filled, out):
    width = cents.shape[2]
    for n in range(NN):
        part = slice(n * width, (n + 1) * width)
        diff = keys[:, n, :].astype(F32) - cents[n, :NW, :].astype(F32)
        out[:, part] = jnp.where(filled[...] > 0, diff, 0.0).astype(BF)


def split_lines(at_ref, cent, gain, *refs):
    outs = refs[-NY:]
    rows, span = cent.shape[0], outs[0].shape[1]
    for g in range(NY):
        outs[g][:rows, :] = cent[:, at(lax.rem(at_ref[2] + g, NY), span, 128)]
        outs[g][rows:, :] = jnp.broadcast_to(gain[...], (16, span))


def split_cores(at_ref, *refs):
    parts, (keep, send) = refs[:NY], refs[-2:]
    c, width = at_ref[3], keep.shape[2]
    rows = keep.shape[1] - 16
    for h in range(NY):
        keep[h, :rows] = parts[h][:rows, at(c, width, 128)]
        send[h, :rows] = parts[h][:rows, at(1 - c, width, 128)]
        keep[h, rows:] = parts[h][rows:, :width]
        send[h, rows:] = parts[h][rows:, :width]


def pick_rows(at_ref, ids, keep, other, *refs):
    own, away, hits, tile = refs[-4:]
    y, c = at_ref[2], at_ref[3]
    slots, rows = ids.shape[0], keep.shape[1] - 16
    for k, part in enumerate((keep, other)):
        for h in range(NY):
            n = lax.rem(y + NY - h, NY) * NC + (1 - c if k else c)
            base = (k * NY + h) * rows
            tile[base : base + rows, :] = part[h, :rows]
            cluster = n * rows + lax.broadcasted_iota(I32, (slots, rows), 1)
            hits[:, base : base + rows] = (ids[...] == cluster).astype(F32).astype(BF)
    mine = own.shape[0] * own.shape[1]
    out = jnp.dot(hits[:mine, :], tile[...], preferred_element_type=F32).astype(BF)
    own[...] = out.reshape(own.shape)
    out = jnp.dot(hits[mine:, :], tile[...], preferred_element_type=F32)
    away[...] = out.reshape(away.shape).astype(BF)


def accumulate(parts, rot, acc):
    lhs = jnp.concatenate([p[...] for p in parts], axis=0)
    new = jnp.dot(lhs, rot[...], preferred_element_type=F32)

    @pl.when(pl.program_id(0) == 0)
    def _():
        acc[...] = new

    @pl.when(pl.program_id(0) > 0)
    def _():
        acc[...] += new


def rotate_extra(*refs):
    parts, (rot, chosen, cents, out, acc) = refs[:8], refs[8:]
    keys = jnp.concatenate([p[...] for p in parts], axis=0)
    keys = jnp.dot(chosen[...], keys, preferred_element_type=F32)
    centre = jnp.concatenate([cents[n, NW:, :] for n in range(cents.shape[0])], axis=1)
    rows = (keys - centre.astype(F32)).astype(BF)
    new = jnp.dot(rows, rot[...], preferred_element_type=F32)

    @pl.when(pl.program_id(0) == 0)
    def _():
        acc[...] = new

    @pl.when(pl.program_id(0) > 0)
    def _():
        acc[...] += new

    @pl.when(pl.program_id(0) == pl.num_programs(0) - 1)
    def _():
        for g in range(NZ):
            out[g] = acc[...].astype(BF)


def rotate(at_ref, *refs):
    parts, (rot, chosen), ext, (out, acc) = refs[:8], refs[8:10], refs[10:14], refs[14:]
    accumulate(parts, rot, acc)

    @pl.when(pl.program_id(0) == pl.num_programs(0) - 1)
    def _():
        x, hot = at_ref[0], at_ref[4]
        acc[...] = jnp.dot(chosen[...], acc[...].astype(BF), preferred_element_type=F32)
        extra = ext[0].shape[1]
        cap = NN + extra
        for h in range(NX):
            first = lax.rem(x + h, NX) * NZ
            for g in range(NZ):
                tail = jnp.where(hot > 0, ext[h][g].astype(F32), 0.0)
                rows = jnp.concatenate([acc[at(first + g, NN, 8), :], tail], axis=0)
                out[at(first + g, cap, 32), :] = rows.astype(BF)


def per_device(hidden, resid, w_out, key_gain, cluster_ids, centroids, rotation):
    xi, zi, yi, ci = (lax.axis_index(a) for a in ("x", "z", "y", "c"))
    ni = yi * NC + ci
    wi = xi * NZ + zi
    tokens, width = hidden.shape
    d = width * NN
    cap = 4 * tokens // NW
    cols = w_out.shape[1]
    wide_cols = NZ * cols
    extra = cap - NN
    per_n = extra // NN

    w_t = w_out.T
    up, down = [w_t, shifted(w_t, "z", NZ, 1)], [w_t, shifted(w_t, "z", NZ, -1)]
    place, cell, hot, short, nth = places(cluster_ids, cap, NN)
    where_am_i = jnp.stack([xi, zi, yi, ci, (wi == hot).astype(I32)]).astype(I32)
    hidden_p = choose_rows(iota((tokens, 1), 0) == place[None, :], hidden)
    h_parts = [hidden_p] + [shifted(hidden_p, "x", NX, h) for h in (1, 2, 3)]

    lines = local_call(
        split_lines,
        [like((centroids.shape[0] + 16, NC * width))] * NY,
        (centroids, jnp.tile(key_gain, NC)[None, :]),
        smem=(where_am_i,),
        after=(hidden_p,),
    )
    lines = [lines[0]] + [shifted(lines[g], "y", NY, g) for g in (1, 2, 3)]
    up.append(shifted(later(up[1], hidden_p), "z", NZ, 1))
    down.append(shifted(down[1], "z", NZ, -1))
    up.append(shifted(later(up[2], h_parts[1], lines[0]), "z", NZ, 1))
    down.append(shifted(down[2], "z", NZ, -1))
    near = later(up[3][: cols // 2], h_parts[2], h_parts[3], *lines[1:])
    far = [shifted(near, "z", NZ, 1), shifted(down[3][cols // 2 :], "z", NZ, -1)]

    cell_of = cell[:, None] == iota((1, NW * cap), 1)
    send_ids = jnp.sum(jnp.where(cell_of, cluster_ids[:, None] + 1, 0), axis=0) - 1
    send_ids = later(send_ids.reshape(NW, cap), up[2], down[2])
    got_ids = lax.all_to_all(send_ids, WIDE, 0, 0, tiled=True)

    part = like((NY, centroids.shape[0] + 16, width))
    cent_keep, cent_send = local_call(split_cores, (part, part), lines, smem=(where_am_i,))
    cent_other = shifted(cent_send, "c", NC, 1)

    block = like((NY, NX, NW, wide_cols))
    keep, send = local_call(
        project,
        (block, block),
        (*h_parts, *up, *down[1:], *far),
        smem=(where_am_i,),
        after=(got_ids,),
        scratch=[pltpu.VMEM((wide_cols, width), BF), pltpu.VMEM((tokens, wide_cols), F32)],
    )
    pairs = local_call(
        add_pair, [like((NX, NW, wide_cols))] * NY, (keep, shifted(send, "c", NC, 1))
    )

    y_parts = [shifted(pairs[g], "y", NY, g) for g in (1, 2, 3)]

    local = jnp.where(got_ids >= 0, got_ids - wi * CL_DEV, -1)
    local = jnp.concatenate([local[:, :NN].T.reshape(-1), local[:, NN:].reshape(-1)])
    cent_own, cent_out = local_call(
        pick_rows,
        (like((NN, NW, width)), like((NW, extra, width))),
        (local[:, None], cent_keep, cent_other),
        smem=(where_am_i,),
        after=(send,),
        scratch=[
            pltpu.VMEM((NW * cap, CL_DEV), BF),
            pltpu.VMEM((CL_DEV, width), BF),
        ],
    )
    cent_in = pick(lax.all_to_all(later(cent_out, y_parts[0]), WIDE, 0, 0, tiled=True), hot)
    cent_pre = jnp.concatenate(
        [cent_own, jnp.broadcast_to(cent_in[None], (NN, extra, width))], axis=1
    )
    cents = lax.all_to_all(cent_pre, NARROW, 0, 0, tiled=True)

    own_place = ni * NW + iota((NW, 1), 0) == place[None, :]
    resid_rows = choose_rows(own_place, resid)

    n_of = ((yi - iota((NC, NY, 1), 1)) % NY) * NC + (ci + iota((NC, NY, 1), 0)) % NC
    filled = (pick(got_ids, ni, 1) >= 0).astype(F32)[:, None]
    ext_j = (iota((NC, NY, 8), 2) * NN + n_of).reshape(1, -1)
    choose_ext = (ext_j == iota((extra, 1), 0)).astype(BF)
    gap = jnp.min(jnp.where(got_ids[:, :NN] < 0, iota((1, NN), 1), NN), axis=1)
    rank = iota((1, NN), 1)
    from_n = (rank + (rank >= gap[:, None]).astype(I32)).reshape(-1, 1)
    from_s = iota((NW, NN), 0).reshape(-1, 1)
    row_n = jnp.broadcast_to(n_of, (NC, NY, NW)).reshape(1, -1)
    row_s = iota((NC, NY, NW), 2).reshape(1, -1)
    chosen = ((from_n == row_n) & (from_s == row_s)).astype(BF)

    sums = local_call(
        add_four,
        [like((NW, wide_cols))] * NX,
        (pairs[0], *y_parts),
        after=(chosen, choose_ext, filled),
    )
    q = iota((8, 1), 0)
    from_host = (short[None, :] & (nth[None, :] == q * NN + ni) & (q < per_n)).astype(BF)
    blocks = [
        sums[0],
        *[shifted(sums[h], "x", NX, -h) for h in (1, 2, 3)],
        resid_rows,
        from_host,
    ]
    gain_at = centroids.shape[0] // 16
    keys, key_extra = local_call(
        normalize,
        (like((NW, d)), like((8, d))),
        (*blocks, cent_keep, cent_other),
        smem=(where_am_i,),
        scratch=[pltpu.VMEM((NW, d), F32)],
        specs=[whole(b.shape) for b in blocks]
        + [pl.BlockSpec((NY, 16, width), lambda i: (0, gain_at, 0))] * 2,
    )

    pieces = [key_extra] + [shifted(key_extra, "y", NY, h) for h in (1, 2, 3)]

    keys = local_call(spread, like((NW, NN, width)), (keys,), after=(cents,))
    got = lax.all_to_all(keys, WIDE, 0, 0, tiled=True)
    residual = local_call(subtract, like((NW, d)), (got, cents, filled))
    parts = [residual] + [shifted(residual, "y", NY, h) for h in (1, 2, 3)]
    parts = parts + [shifted(p, "c", NC, 1) for p in parts]

    steps = 4
    rot_spec = pl.BlockSpec((d // steps, width), lambda k: (k, 0))

    def row_specs(rows):
        return [pl.BlockSpec((rows, d // steps), lambda k: (0, k))] * NN

    pieces = pieces + [shifted(p, "c", NC, 1) for p in pieces]
    ext = local_call(
        rotate_extra,
        like((NZ, extra, width)),
        (*pieces, rotation, choose_ext, cents),
        scratch=[pltpu.VMEM((extra, width), F32)],
        grid=(steps,),
        specs=row_specs(8)
        + [rot_spec, whole(choose_ext.shape)]
        + [pl.BlockSpec((NN // steps, NW + extra, width), lambda k: (k, 0, 0))],
    )
    ext = lax.all_to_all(ext, "z", 0, 0, tiled=True)
    ext = [ext] + [shifted(ext, "x", NX, -h) for h in range(1, NX)]

    return local_call(
        rotate,
        like((NW * cap, width)),
        (*parts, rotation, chosen, *ext),
        smem=(where_am_i,),
        scratch=[pltpu.VMEM((NN * NW, width), F32)],
        grid=(steps,),
        specs=row_specs(NW) + [rot_spec, whole(chosen.shape)] + [whole(ext[0].shape)] * NX,
    )


def solution(mesh):
    grid = Mesh(mesh.devices.reshape(NX, NZ, NY, NC), ("x", "z", "y", "c"))
    placed = (
        P(WIDE, NARROW),
        P(WIDE, None),
        P(NARROW, WIDE),
        P(NARROW),
        P(WIDE),
        P(WIDE + NARROW, None),
        P(None, NARROW),
    )
    return jax.shard_map(
        per_device, mesh=grid, in_specs=placed, out_specs=P(WIDE, NARROW), check_vma=False
    )
```

```python
import jax
import jax.numpy as jnp
from jax import lax
from jax.experimental import pallas as pl
from jax.experimental.pallas import tpu as pltpu
from jax.sharding import Mesh, PartitionSpec as P

CL_DEV = 1024
EPS = 1e-05
NX, NZ, NY, NC = 4, 8, 4, 2
WIDE = ("x", "z")
NARROW = ("y", "c")
NN = NY * NC
NW = NX * NZ
BF = jnp.bfloat16
F32 = jnp.float32
I32 = jnp.int32


def shifted(a, axis, n, h):
    return lax.ppermute(a, axis, [(i, (i + h) % n) for i in range(n)])


def pick(a, i, axis=0):
    return lax.dynamic_index_in_dim(a, i, axis, keepdims=False)


def iota(shape, dim):
    return lax.broadcasted_iota(I32, shape, dim)


def choose_rows(onehot, a):
    return jnp.dot(onehot.astype(BF), a, preferred_element_type=F32).astype(BF)


def places(ids, cap, per_owner):
    owner = ids // CL_DEV
    onehot = (owner[:, None] == iota((1, NW), 1)).astype(I32)
    rank = jnp.sum((jnp.cumsum(onehot, axis=0) - onehot) * onehot, axis=1)
    count = jnp.sum(onehot, axis=0)
    hot = jnp.argmax(count).astype(I32)
    short = count < per_owner
    nth = jnp.cumsum(short.astype(I32)) - short.astype(I32)
    gap = jnp.where(short, nth % per_owner, per_owner)
    n_of = rank + (rank >= jnp.sum(onehot * gap[None, :], axis=1)).astype(I32)
    surplus = rank >= per_owner
    j = rank - per_owner
    host = jnp.sum(
        jnp.where(short[None, :] & (nth[None, :] == j[:, None]), iota((1, NW), 1), 0), axis=1
    )
    place = jnp.where(surplus, (j % per_owner) * NW + host, n_of * NW + owner)
    cell = owner * cap + jnp.where(surplus, rank, n_of)
    return place, cell, hot, short, nth


SMEM = pl.BlockSpec(memory_space=pltpu.SMEM)
ANY = pl.BlockSpec(memory_space=pl.ANY)
PARAMS = pltpu.CompilerParams(vmem_limit_bytes=56 * 1024 * 1024)


def like(shape, dtype=BF):
    return jax.ShapeDtypeStruct(shape, dtype)


def whole(shape):
    return pl.BlockSpec(shape, lambda i: (0,) * len(shape))


def local_call(kernel, outs, args, after=(), smem=(), scratch=(), grid=(1,), specs=None):
    return pl.pallas_call(
        kernel,
        out_shape=outs,
        grid=grid,
        in_specs=[SMEM] * len(smem) + (specs or [whole(a.shape) for a in args]) + [ANY] * len(after),
        out_specs=jax.tree.map(lambda o: whole(o.shape), outs),
        scratch_shapes=list(scratch),
        compiler_params=PARAMS,
        name=kernel.__name__,
    )(*smem, *args, *after)


def at(i, size, step):
    return pl.ds(pl.multiple_of(i * size, step), size)


def project(at_ref, *refs):
    h_refs, up, down, far = refs[:4], refs[4:8], refs[8:11], refs[11:13]
    keep, send, w_all, acc = refs[-4:]
    z, y, c = at_ref[1], at_ref[2], at_ref[3]
    cols = up[0].shape[0]
    for h in range(4):
        w_all[at(lax.rem(z + NZ - h, NZ), cols, 16), :] = up[h][...]
        if h:
            w_all[at(lax.rem(z + h, NZ), cols, 16), :] = down[h - 1][...]
    across = lax.rem(z + 4, NZ) * cols
    w_all[pl.ds(pl.multiple_of(across, 16), cols // 2), :] = far[0][...]
    w_all[pl.ds(pl.multiple_of(across + cols // 2, 16), cols // 2), :] = far[1][...]
    for h in range(NX):
        acc[...] = lax.dot_general(
            h_refs[h][...], w_all[...], (((1,), (1,)), ((), ())), preferred_element_type=F32
        )
        for g in range(NY):
            n = lax.rem(y + g, NY) * NC
            keep[g, h] = acc[at(n + c, NW, 32), :].astype(BF)
            send[g, h] = acc[at(n + 1 - c, NW, 32), :].astype(BF)


def add_pair(keep, other, *outs):
    for g in range(NY):
        outs[g][...] = (keep[g].astype(F32) + other[g].astype(F32)).astype(BF)


def add_four(*refs):
    outs = refs[-NX:]
    for h in range(NX):
        total = refs[0][h].astype(F32)
        for g in range(1, NY):
            total = total + refs[g][h].astype(F32)
        outs[h][...] = total.astype(BF)


def hold(*refs):
    pass


def later(a, *after):
    return pl.pallas_call(
        hold,
        out_shape=like(a.shape, a.dtype),
        in_specs=[ANY] * (1 + len(after)),
        out_specs=ANY,
        input_output_aliases={0: 0},
        compiler_params=PARAMS,
        name="later",
    )(a, *after)


def normalize(at_ref, b0, b1, b2, b3, resid, from_host, gain, other, keys, extra, stream):
    x, y, c = at_ref[0], at_ref[2], at_ref[3]
    span = b0.shape[1]
    width = gain.shape[2]
    for h, b in enumerate((b0, b1, b2, b3)):
        where = at(lax.rem(x + h, NX), span, 128)
        stream[:, where] = resid[:, where].astype(F32) + b[...].astype(F32)
    value = stream[...]
    scale = lax.rsqrt(jnp.mean(value * value, axis=1, keepdims=True) + EPS)
    for k, gains in enumerate((gain, other)):
        for h in range(NY):
            n = lax.rem(y + NY - h, NY) * NC + (1 - c if k else c)
            where = at(n, width, 128)
            row = gains[h].astype(F32)[:1]
            keys[:, where] = (stream[:, where] * scale * row).astype(BF)
    chosen = jnp.dot(from_host[...], keys[...], preferred_element_type=F32)
    extra[...] = chosen.astype(BF)


def spread(keys, *refs):
    out = refs[-1]
    width = out.shape[2]
    for n in range(NN):
        out[:, n, :] = keys[:, n * width : (n + 1) * width]


def subtract(keys, cents, filled, out):
    width = cents.shape[2]
    for n in range(NN):
        part = slice(n * width, (n + 1) * width)
        diff = keys[:, n, :].astype(F32) - cents[n, :NW, :].astype(F32)
        out[:, part] = jnp.where(filled[...] > 0, diff, 0.0).astype(BF)


def split_lines(at_ref, cent, gain, *refs):
    outs = refs[-NY:]
    rows, span = cent.shape[0], outs[0].shape[1]
    for g in range(NY):
        outs[g][:rows, :] = cent[:, at(lax.rem(at_ref[2] + g, NY), span, 128)]
        outs[g][rows:, :] = jnp.broadcast_to(gain[...], (16, span))


def split_cores(at_ref, *refs):
    parts, (keep, send) = refs[:NY], refs[-2:]
    c, width = at_ref[3], keep.shape[2]
    rows = keep.shape[1] - 16
    for h in range(NY):
        keep[h, :rows] = parts[h][:rows, at(c, width, 128)]
        send[h, :rows] = parts[h][:rows, at(1 - c, width, 128)]
        keep[h, rows:] = parts[h][rows:, :width]
        send[h, rows:] = parts[h][rows:, :width]


def pick_rows(at_ref, ids, keep, other, *refs):
    own, away, hits, tile = refs[-4:]
    y, c = at_ref[2], at_ref[3]
    slots, rows = ids.shape[0], keep.shape[1] - 16
    for k, part in enumerate((keep, other)):
        for h in range(NY):
            n = lax.rem(y + NY - h, NY) * NC + (1 - c if k else c)
            base = (k * NY + h) * rows
            tile[base : base + rows, :] = part[h, :rows]
            cluster = n * rows + lax.broadcasted_iota(I32, (slots, rows), 1)
            hits[:, base : base + rows] = (ids[...] == cluster).astype(F32).astype(BF)
    mine = own.shape[0] * own.shape[1]
    out = jnp.dot(hits[:mine, :], tile[...], preferred_element_type=F32).astype(BF)
    own[...] = out.reshape(own.shape)
    out = jnp.dot(hits[mine:, :], tile[...], preferred_element_type=F32)
    away[...] = out.reshape(away.shape).astype(BF)


def accumulate(parts, rot, acc):
    lhs = jnp.concatenate([p[...] for p in parts], axis=0)
    new = jnp.dot(lhs, rot[...], preferred_element_type=F32)

    @pl.when(pl.program_id(0) == 0)
    def _():
        acc[...] = new

    @pl.when(pl.program_id(0) > 0)
    def _():
        acc[...] += new


def rotate_extra(*refs):
    parts, (rot, chosen, cents, out, acc) = refs[:8], refs[8:]
    keys = jnp.concatenate([p[...] for p in parts], axis=0)
    keys = jnp.dot(chosen[...], keys, preferred_element_type=F32)
    centre = jnp.concatenate([cents[n, NW:, :] for n in range(cents.shape[0])], axis=1)
    rows = (keys - centre.astype(F32)).astype(BF)
    new = jnp.dot(rows, rot[...], preferred_element_type=F32)

    @pl.when(pl.program_id(0) == 0)
    def _():
        acc[...] = new

    @pl.when(pl.program_id(0) > 0)
    def _():
        acc[...] += new

    @pl.when(pl.program_id(0) == pl.num_programs(0) - 1)
    def _():
        for g in range(NZ):
            out[g] = acc[...].astype(BF)


def rotate(at_ref, *refs):
    parts, (rot, chosen), ext, (out, acc) = refs[:8], refs[8:10], refs[10:14], refs[14:]
    accumulate(parts, rot, acc)

    @pl.when(pl.program_id(0) == pl.num_programs(0) - 1)
    def _():
        x, hot = at_ref[0], at_ref[4]
        acc[...] = jnp.dot(chosen[...], acc[...].astype(BF), preferred_element_type=F32)
        extra = ext[0].shape[1]
        cap = NN + extra
        for h in range(NX):
            first = lax.rem(x + h, NX) * NZ
            for g in range(NZ):
                tail = jnp.where(hot > 0, ext[h][g].astype(F32), 0.0)
                rows = jnp.concatenate([acc[at(first + g, NN, 8), :], tail], axis=0)
                out[at(first + g, cap, 32), :] = rows.astype(BF)


def per_device(hidden, resid, w_out, key_gain, cluster_ids, centroids, rotation):
    xi, zi, yi, ci = (lax.axis_index(a) for a in ("x", "z", "y", "c"))
    ni = yi * NC + ci
    wi = xi * NZ + zi
    tokens, width = hidden.shape
    d = width * NN
    cap = 4 * tokens // NW
    cols = w_out.shape[1]
    wide_cols = NZ * cols
    extra = cap - NN
    per_n = extra // NN

    w_t = w_out.T
    up, down = [w_t, shifted(w_t, "z", NZ, 1)], [w_t, shifted(w_t, "z", NZ, -1)]
    place, cell, hot, short, nth = places(cluster_ids, cap, NN)
    where_am_i = jnp.stack([xi, zi, yi, ci, (wi == hot).astype(I32)]).astype(I32)
    hidden_p = choose_rows(iota((tokens, 1), 0) == place[None, :], hidden)
    h_parts = [hidden_p] + [shifted(hidden_p, "x", NX, h) for h in (1, 2, 3)]

    lines = local_call(
        split_lines,
        [like((centroids.shape[0] + 16, NC * width))] * NY,
        (centroids, jnp.tile(key_gain, NC)[None, :]),
        smem=(where_am_i,),
        after=(hidden_p,),
    )
    lines = [lines[0]] + [shifted(lines[g], "y", NY, g) for g in (1, 2, 3)]
    cell_of = cell[:, None] == iota((1, NW * cap), 1)
    send_ids = jnp.sum(jnp.where(cell_of, cluster_ids[:, None] + 1, 0), axis=0) - 1
    send_ids = later(send_ids.reshape(NW, cap), up[1], down[1])
    got_ids = lax.all_to_all(send_ids, WIDE, 0, 0, tiled=True)
    up.append(shifted(later(up[1], hidden_p), "z", NZ, 1))
    down.append(shifted(down[1], "z", NZ, -1))
    up.append(shifted(later(up[2], h_parts[1], lines[0]), "z", NZ, 1))
    down.append(shifted(down[2], "z", NZ, -1))
    near = later(up[3][: cols // 2], h_parts[2], h_parts[3], *lines[1:], got_ids)
    far = [shifted(near, "z", NZ, 1), shifted(down[3][cols // 2 :], "z", NZ, -1)]

    part = like((NY, centroids.shape[0] + 16, width))
    cent_keep, cent_send = local_call(split_cores, (part, part), lines, smem=(where_am_i,))
    cent_other = shifted(cent_send, "c", NC, 1)

    block = like((NY, NX, NW, wide_cols))
    keep, send = local_call(
        project,
        (block, block),
        (*h_parts, *up, *down[1:], *far),
        smem=(where_am_i,),
        scratch=[pltpu.VMEM((wide_cols, width), BF), pltpu.VMEM((tokens, wide_cols), F32)],
    )
    pairs = local_call(
        add_pair, [like((NX, NW, wide_cols))] * NY, (keep, shifted(send, "c", NC, 1))
    )

    y_parts = [shifted(pairs[g], "y", NY, g) for g in (1, 2, 3)]

    local = jnp.where(got_ids >= 0, got_ids - wi * CL_DEV, -1)
    local = jnp.concatenate([local[:, :NN].T.reshape(-1), local[:, NN:].reshape(-1)])
    cent_own, cent_out = local_call(
        pick_rows,
        (like((NN, NW, width)), like((NW, extra, width))),
        (local[:, None], cent_keep, cent_other),
        smem=(where_am_i,),
        after=(send,),
        scratch=[
            pltpu.VMEM((NW * cap, CL_DEV), BF),
            pltpu.VMEM((CL_DEV, width), BF),
        ],
    )
    cent_in = pick(lax.all_to_all(cent_out, WIDE, 0, 0, tiled=True), hot)
    cent_pre = jnp.concatenate(
        [cent_own, jnp.broadcast_to(cent_in[None], (NN, extra, width))], axis=1
    )
    own_place = ni * NW + iota((NW, 1), 0) == place[None, :]
    resid_rows = choose_rows(own_place, resid)

    n_of = ((yi - iota((NC, NY, 1), 1)) % NY) * NC + (ci + iota((NC, NY, 1), 0)) % NC
    filled = (pick(got_ids, ni, 1) >= 0).astype(F32)[:, None]
    ext_j = (iota((NC, NY, 8), 2) * NN + n_of).reshape(1, -1)
    choose_ext = (ext_j == iota((extra, 1), 0)).astype(BF)
    gap = jnp.min(jnp.where(got_ids[:, :NN] < 0, iota((1, NN), 1), NN), axis=1)
    rank = iota((1, NN), 1)
    from_n = (rank + (rank >= gap[:, None]).astype(I32)).reshape(-1, 1)
    from_s = iota((NW, NN), 0).reshape(-1, 1)
    row_n = jnp.broadcast_to(n_of, (NC, NY, NW)).reshape(1, -1)
    row_s = iota((NC, NY, NW), 2).reshape(1, -1)
    chosen = ((from_n == row_n) & (from_s == row_s)).astype(BF)

    sums = local_call(
        add_four,
        [like((NW, wide_cols))] * NX,
        (pairs[0], *y_parts),
        after=(chosen, choose_ext, filled),
    )
    q = iota((8, 1), 0)
    from_host = (short[None, :] & (nth[None, :] == q * NN + ni) & (q < per_n)).astype(BF)
    blocks = [
        sums[0],
        *[shifted(sums[h], "x", NX, -h) for h in (1, 2, 3)],
        resid_rows,
        from_host,
    ]
    gain_at = centroids.shape[0] // 16
    keys, key_extra = local_call(
        normalize,
        (like((NW, d)), like((8, d))),
        (*blocks, cent_keep, cent_other),
        smem=(where_am_i,),
        scratch=[pltpu.VMEM((NW, d), F32)],
        specs=[whole(b.shape) for b in blocks]
        + [pl.BlockSpec((NY, 16, width), lambda i: (0, gain_at, 0))] * 2,
    )

    cents = lax.all_to_all(later(cent_pre, keys), NARROW, 0, 0, tiled=True)
    pieces = [key_extra] + [shifted(key_extra, "y", NY, h) for h in (1, 2, 3)]

    keys = local_call(spread, like((NW, NN, width)), (keys,), after=(cents,))
    got = lax.all_to_all(keys, WIDE, 0, 0, tiled=True)
    residual = local_call(subtract, like((NW, d)), (got, cents, filled))
    parts = [residual] + [shifted(residual, "y", NY, h) for h in (1, 2, 3)]
    parts = parts + [shifted(p, "c", NC, 1) for p in parts]

    steps = 4
    rot_spec = pl.BlockSpec((d // steps, width), lambda k: (k, 0))

    def row_specs(rows):
        return [pl.BlockSpec((rows, d // steps), lambda k: (0, k))] * NN

    pieces = pieces + [shifted(p, "c", NC, 1) for p in pieces]
    ext = local_call(
        rotate_extra,
        like((NZ, extra, width)),
        (*pieces, rotation, choose_ext, cents),
        scratch=[pltpu.VMEM((extra, width), F32)],
        grid=(steps,),
        specs=row_specs(8)
        + [rot_spec, whole(choose_ext.shape)]
        + [pl.BlockSpec((NN // steps, NW + extra, width), lambda k: (k, 0, 0))],
    )
    ext = lax.all_to_all(later(ext, residual), "z", 0, 0, tiled=True)
    ext = [ext] + [shifted(ext, "x", NX, -h) for h in range(1, NX)]

    return local_call(
        rotate,
        like((NW * cap, width)),
        (*parts, rotation, chosen, *ext),
        smem=(where_am_i,),
        scratch=[pltpu.VMEM((NN * NW, width), F32)],
        grid=(steps,),
        specs=row_specs(NW) + [rot_spec, whole(chosen.shape)] + [whole(ext[0].shape)] * NX,
    )


def solution(mesh):
    grid = Mesh(mesh.devices.reshape(NX, NZ, NY, NC), ("x", "z", "y", "c"))
    placed = (
        P(WIDE, NARROW),
        P(WIDE, None),
        P(NARROW, WIDE),
        P(NARROW),
        P(WIDE),
        P(WIDE + NARROW, None),
        P(None, NARROW),
    )
    return jax.shard_map(
        per_device, mesh=grid, in_specs=placed, out_specs=P(WIDE, NARROW), check_vma=False
    )
```

```python
import jax
import jax.numpy as jnp
from jax import lax
from jax.experimental import pallas as pl
from jax.experimental.pallas import tpu as pltpu
from jax.sharding import Mesh, PartitionSpec as P

CL_DEV = 1024
EPS = 1e-05
NX, NZ, NY, NC = 4, 8, 4, 2
WIDE = ("x", "z")
NARROW = ("y", "c")
NN = NY * NC
NW = NX * NZ
BF = jnp.bfloat16
F32 = jnp.float32
I32 = jnp.int32


def shifted(a, axis, n, h):
    return lax.ppermute(a, axis, [(i, (i + h) % n) for i in range(n)])


def pick(a, i, axis=0):
    return lax.dynamic_index_in_dim(a, i, axis, keepdims=False)


def iota(shape, dim):
    return lax.broadcasted_iota(I32, shape, dim)


def choose_rows(onehot, a):
    return jnp.dot(onehot.astype(BF), a, preferred_element_type=F32).astype(BF)


def places(ids, cap, per_owner):
    owner = ids // CL_DEV
    onehot = (owner[:, None] == iota((1, NW), 1)).astype(I32)
    rank = jnp.sum((jnp.cumsum(onehot, axis=0) - onehot) * onehot, axis=1)
    count = jnp.sum(onehot, axis=0)
    hot = jnp.argmax(count).astype(I32)
    short = count < per_owner
    nth = jnp.cumsum(short.astype(I32)) - short.astype(I32)
    gap = jnp.where(short, nth % per_owner, per_owner)
    n_of = rank + (rank >= jnp.sum(onehot * gap[None, :], axis=1)).astype(I32)
    surplus = rank >= per_owner
    j = rank - per_owner
    host = jnp.sum(
        jnp.where(short[None, :] & (nth[None, :] == j[:, None]), iota((1, NW), 1), 0), axis=1
    )
    place = jnp.where(surplus, (j % per_owner) * NW + host, n_of * NW + owner)
    cell = owner * cap + jnp.where(surplus, rank, n_of)
    return place, cell, hot, short, nth


SMEM = pl.BlockSpec(memory_space=pltpu.SMEM)
ANY = pl.BlockSpec(memory_space=pl.ANY)


def like(shape, dtype=BF):
    return jax.ShapeDtypeStruct(shape, dtype)


def whole(shape):
    return pl.BlockSpec(shape, lambda i: (0,) * len(shape))


def local_call(
    kernel, outs, args, after=(), smem=(), scratch=(), grid=(1,), specs=None, grant=28
):
    return pl.pallas_call(
        kernel,
        out_shape=outs,
        grid=grid,
        in_specs=[SMEM] * len(smem) + (specs or [whole(a.shape) for a in args]) + [ANY] * len(after),
        out_specs=jax.tree.map(lambda o: whole(o.shape), outs),
        scratch_shapes=list(scratch),
        compiler_params=pltpu.CompilerParams(vmem_limit_bytes=grant * 1024 * 1024),
        name=kernel.__name__,
    )(*smem, *args, *after)


def at(i, size, step):
    return pl.ds(pl.multiple_of(i * size, step), size)


def project(at_ref, *refs):
    h_refs, up, down, far = refs[:4], refs[4:8], refs[8:11], refs[11:13]
    keep, send, w_all, acc = refs[13:]
    z, y, c = at_ref[1], at_ref[2], at_ref[3]
    cols = up[0].shape[0]
    for h in range(4):
        w_all[at(lax.rem(z + NZ - h, NZ), cols, 16), :] = up[h][...]
        if h:
            w_all[at(lax.rem(z + h, NZ), cols, 16), :] = down[h - 1][...]
    across = lax.rem(z + 4, NZ) * cols
    w_all[pl.ds(pl.multiple_of(across, 16), cols // 2), :] = far[0][...]
    w_all[pl.ds(pl.multiple_of(across + cols // 2, 16), cols // 2), :] = far[1][...]
    for h in range(NX):
        acc[...] = lax.dot_general(
            h_refs[h][...], w_all[...], (((1,), (1,)), ((), ())), preferred_element_type=F32
        )
        for g in range(NY):
            n = lax.rem(y + g, NY) * NC
            keep[g, h] = acc[at(n + c, NW, 32), :].astype(BF)
            send[g, h] = acc[at(n + 1 - c, NW, 32), :].astype(BF)


def add_pair(keep, other, *outs):
    for g in range(NY):
        outs[g][...] = (keep[g].astype(F32) + other[g].astype(F32)).astype(BF)


def add_four(*refs):
    outs = refs[-NX:]
    for h in range(NX):
        total = refs[0][h].astype(F32)
        for g in range(1, NY):
            total = total + refs[g][h].astype(F32)
        outs[h][...] = total.astype(BF)


def gate(ids, token, out):
    out[...] = ids[...]


def normalize(at_ref, b0, b1, b2, b3, resid, cents, from_host, keys, extra, stream):
    x = at_ref[0]
    span = b0.shape[1]
    width = cents.shape[2]
    for h, b in enumerate((b0, b1, b2, b3)):
        where = at(lax.rem(x + h, NX), span, 128)
        stream[:, where] = resid[:, where].astype(F32) + b[...].astype(F32)
    value = stream[...]
    scale = lax.rsqrt(jnp.mean(value * value, axis=1, keepdims=True) + EPS)
    for n in range(NN):
        part = slice(n * width, (n + 1) * width)
        tail = cents[n, NW:, :].astype(F32)
        key = (stream[:, part] * scale * tail[7:8]).astype(BF)
        keys[:, part] = key
        chosen = jnp.dot(from_host[...], key, preferred_element_type=F32)
        extra[:, part] = (chosen - tail).astype(BF)


def subtract(keys, cents, filled, out):
    width = cents.shape[2]
    for n in range(NN):
        part = slice(n * width, (n + 1) * width)
        diff = keys[:, part].astype(F32) - cents[n, :NW, :].astype(F32)
        out[:, part] = jnp.where(filled[...] > 0, diff, 0.0).astype(BF)


def split_rows(cent, *refs):
    out = refs[-1]
    width = out.shape[2]
    for n in range(NN):
        out[n] = cent[:, n * width : (n + 1) * width]


def cells(cell, ids, *refs):
    out = refs[-1]
    hit = cell[...] == lax.broadcasted_iota(I32, (cell.shape[0], out.shape[1]), 1)
    out[...] = jnp.sum(jnp.where(hit, ids[...] + 1, 0), axis=0, keepdims=True) - 1


def accumulate(parts, rot, acc):
    lhs = jnp.concatenate([p[...] for p in parts], axis=0)
    new = jnp.dot(lhs, rot[...], preferred_element_type=F32)

    @pl.when(pl.program_id(0) == 0)
    def _():
        acc[...] = new

    @pl.when(pl.program_id(0) > 0)
    def _():
        acc[...] += new


def rotate_extra(*refs):
    parts, (rot, chosen, out, acc) = refs[:8], refs[8:]
    accumulate(parts, rot, acc)

    @pl.when(pl.program_id(0) == pl.num_programs(0) - 1)
    def _():
        rows = acc[...].astype(BF)
        picked = jnp.dot(chosen[...], rows, preferred_element_type=F32).astype(BF)
        for g in range(NZ):
            out[g] = picked


def rotate(*refs):
    parts, (rot, chosen, out, acc) = refs[:8], refs[8:]
    accumulate(parts, rot, acc)

    @pl.when(pl.program_id(0) == pl.num_programs(0) - 1)
    def _():
        rows = acc[...].astype(BF)
        out[...] = jnp.dot(chosen[...], rows, preferred_element_type=F32)


def lay_out(at_ref, rows, *refs):
    ext, out = refs[:NX], refs[-1]
    x, hot = at_ref[0], at_ref[4]
    extra = ext[0].shape[1]
    cap = NN + extra
    for h in range(NX):
        first = lax.rem(x + h, NX) * NZ
        for g in range(NZ):
            tail = jnp.where(hot > 0, ext[h][g].astype(F32), 0.0)
            both = jnp.concatenate([rows[at(first + g, NN, 8), :], tail], axis=0)
            out[at(first + g, cap, 32), :] = both.astype(BF)


def per_device(hidden, resid, w_out, key_gain, cluster_ids, centroids, rotation):
    xi, zi, yi, ci = (lax.axis_index(a) for a in ("x", "z", "y", "c"))
    ni = yi * NC + ci
    wi = xi * NZ + zi
    tokens, width = hidden.shape
    d = width * NN
    cap = 4 * tokens // NW
    cols = w_out.shape[1]
    wide_cols = NZ * cols
    extra = cap - NN
    per_n = extra // NN

    w_t = w_out.T
    up, down = [w_t], [w_t]
    for _ in range(3):
        up.append(shifted(up[-1], "z", NZ, 1))
        down.append(shifted(down[-1], "z", NZ, -1))
    far = [
        shifted(up[-1][: cols // 2], "z", NZ, 1),
        shifted(down[-1][cols // 2 :], "z", NZ, -1),
    ]

    place, cell, hot, short, nth = places(cluster_ids, cap, NN)
    where_am_i = jnp.stack([xi, zi, yi, ci, (wi == hot).astype(I32)]).astype(I32)
    hidden_p = choose_rows(iota((tokens, 1), 0) == place[None, :], hidden)
    h_parts = [hidden_p] + [shifted(hidden_p, "x", NX, h) for h in (1, 2, 3)]

    send_ids = local_call(
        cells,
        like((1, NW * cap), I32),
        (cell[:, None], cluster_ids[:, None]),
        after=(up[2], down[2], *h_parts[1:]),
    )
    got_ids = lax.all_to_all(send_ids.reshape(NW * cap), WIDE, 0, 0, tiled=True).reshape(NW, cap)

    cent_split = local_call(
        split_rows,
        like((NN, centroids.shape[0], width)),
        (centroids,),
        after=(up[1], down[1]),
    )
    cent_tile = lax.all_to_all(cent_split, NARROW, 0, 0, tiled=True).reshape(-1, width)

    block = like((NY, NX, NW, wide_cols))
    keep, send = local_call(
        project,
        (block, block),
        (*h_parts, *up, *down[1:], *far),
        smem=(where_am_i,),
        scratch=[pltpu.VMEM((wide_cols, width), BF), pltpu.VMEM((tokens, wide_cols), F32)],
    )
    pairs = local_call(
        add_pair, [like((NX, NW, wide_cols))] * NY, (keep, shifted(send, "c", NC, 1))
    )

    local = jnp.where(got_ids >= 0, got_ids - wi * CL_DEV, -1)
    local = local_call(gate, like(local.shape, I32), (local,), after=(keep,))
    clusters = iota((1, CL_DEV), 1)
    cent_own = choose_rows(local[:, :NN].T.reshape(-1, 1) == clusters, cent_tile)
    cent_out = choose_rows(local[:, NN:].reshape(-1, 1) == clusters, cent_tile)
    cent_in = pick(lax.all_to_all(cent_out.reshape(NW, extra, width), WIDE, 0, 0, tiled=True), hot)
    cent_pre = jnp.concatenate(
        [
            cent_own.reshape(NN, NW, width),
            cent_in.reshape(per_n, NN, width).transpose(1, 0, 2),
            jnp.broadcast_to(key_gain, (NN, 8 - per_n, width)),
        ],
        axis=1,
    )
    cents = lax.all_to_all(cent_pre, NARROW, 0, 0, tiled=True)

    own_place = ni * NW + iota((NW, 1), 0) == place[None, :]
    resid_rows = choose_rows(own_place, resid)

    sums = local_call(
        add_four,
        [like((NW, wide_cols))] * NX,
        (pairs[0], *[shifted(pairs[g], "y", NY, g) for g in (1, 2, 3)]),
    )
    q = iota((8, 1), 0)
    from_host = (short[None, :] & (nth[None, :] == q * NN + ni) & (q < per_n)).astype(BF)
    keys, res_extra = local_call(
        normalize,
        (like((NW, d)), like((8, d))),
        (
            sums[0],
            *[shifted(sums[h], "x", NX, -h) for h in (1, 2, 3)],
            resid_rows,
            cents,
            from_host,
        ),
        smem=(where_am_i,),
        scratch=[pltpu.VMEM((NW, d), F32)],
        grant=58,
    )

    n_of = ((yi - iota((NC, NY, 1), 1)) % NY) * NC + (ci + iota((NC, NY, 1), 0)) % NC

    got = lax.all_to_all(keys.reshape(NW, NN, width), WIDE, 0, 0, tiled=True).reshape(NW, d)
    filled = (pick(got_ids, ni, 1) >= 0).astype(F32)[:, None]
    residual = local_call(subtract, like((NW, d)), (got, cents, filled))
    parts = [residual] + [shifted(residual, "y", NY, h) for h in (1, 2, 3)]
    parts = parts + [shifted(p, "c", NC, 1) for p in parts]

    steps = 4
    rot_spec = pl.BlockSpec((d // steps, width), lambda k: (k, 0))

    def row_specs(rows):
        return [pl.BlockSpec((rows, d // steps), lambda k: (0, k))] * NN

    pieces = [res_extra] + [shifted(res_extra, "y", NY, h) for h in (1, 2, 3)]
    pieces = pieces + [shifted(p, "c", NC, 1) for p in pieces]
    ext_j = (iota((NC, NY, 8), 2) * NN + n_of).reshape(1, -1)
    choose_ext = (ext_j == iota((extra, 1), 0)).astype(BF)
    ext = local_call(
        rotate_extra,
        like((NZ, extra, width)),
        (*pieces, rotation, choose_ext),
        scratch=[pltpu.VMEM((NN * 8, width), F32)],
        grid=(steps,),
        specs=row_specs(8) + [rot_spec, whole(choose_ext.shape)],
    )
    ext = lax.all_to_all(ext, "z", 0, 0, tiled=True)
    ext = [ext] + [shifted(ext, "x", NX, -h) for h in range(1, NX)]

    gap = jnp.min(jnp.where(got_ids[:, :NN] < 0, iota((1, NN), 1), NN), axis=1)
    rank = iota((1, NN), 1)
    from_n = (rank + (rank >= gap[:, None]).astype(I32)).reshape(-1, 1)
    from_s = iota((NW, NN), 0).reshape(-1, 1)
    row_n = jnp.broadcast_to(n_of, (NC, NY, NW)).reshape(1, -1)
    row_s = iota((NC, NY, NW), 2).reshape(1, -1)
    chosen = ((from_n == row_n) & (from_s == row_s)).astype(BF)
    rotated = local_call(
        rotate,
        like((NN * NW, width), F32),
        (*parts, rotation, chosen),
        scratch=[pltpu.VMEM((NN * NW, width), F32)],
        grid=(steps,),
        specs=row_specs(NW) + [rot_spec, whole(chosen.shape)],
    )
    return local_call(
        lay_out, like((NW * cap, width)), (rotated, *ext), smem=(where_am_i,), grant=58
    )


def solution(mesh):
    grid = Mesh(mesh.devices.reshape(NX, NZ, NY, NC), ("x", "z", "y", "c"))
    placed = (
        P(WIDE, NARROW),
        P(WIDE, None),
        P(NARROW, WIDE),
        P(NARROW),
        P(WIDE),
        P(WIDE + NARROW, None),
        P(None, NARROW),
    )
    return jax.shard_map(
        per_device, mesh=grid, in_specs=placed, out_specs=P(WIDE, NARROW), check_vma=False
    )
```

```python
import jax
import jax.numpy as jnp
from jax import lax
from jax.experimental import pallas as pl
from jax.experimental.pallas import tpu as pltpu
from jax.sharding import Mesh, PartitionSpec as P

CL_DEV = 1024
EPS = 1e-05
NX, NZ, NY, NC = 4, 8, 4, 2
WIDE = ("x", "z")
NARROW = ("y", "c")
NN = NY * NC
NW = NX * NZ
BF = jnp.bfloat16
F32 = jnp.float32
I32 = jnp.int32


def shifted(a, axis, n, h):
    return lax.ppermute(a, axis, [(i, (i + h) % n) for i in range(n)])


def pick(a, i, axis=0):
    return lax.dynamic_index_in_dim(a, i, axis, keepdims=False)


def iota(shape, dim):
    return lax.broadcasted_iota(I32, shape, dim)


def choose_rows(onehot, a):
    return jnp.dot(onehot.astype(BF), a, preferred_element_type=F32).astype(BF)


def places(ids, cap, per_owner):
    owner = ids // CL_DEV
    onehot = (owner[:, None] == iota((1, NW), 1)).astype(I32)
    rank = jnp.sum((jnp.cumsum(onehot, axis=0) - onehot) * onehot, axis=1)
    count = jnp.sum(onehot, axis=0)
    hot = jnp.argmax(count).astype(I32)
    short = count < per_owner
    nth = jnp.cumsum(short.astype(I32)) - short.astype(I32)
    gap = jnp.where(short, nth % per_owner, per_owner)
    n_of = rank + (rank >= jnp.sum(onehot * gap[None, :], axis=1)).astype(I32)
    surplus = rank >= per_owner
    j = rank - per_owner
    host = jnp.sum(
        jnp.where(short[None, :] & (nth[None, :] == j[:, None]), iota((1, NW), 1), 0), axis=1
    )
    place = jnp.where(surplus, (j % per_owner) * NW + host, n_of * NW + owner)
    cell = owner * cap + jnp.where(surplus, rank, n_of)
    return place, cell, hot, short, nth


SMEM = pl.BlockSpec(memory_space=pltpu.SMEM)
ANY = pl.BlockSpec(memory_space=pl.ANY)


def like(shape, dtype=BF):
    return jax.ShapeDtypeStruct(shape, dtype)


def whole(shape):
    return pl.BlockSpec(shape, lambda i: (0,) * len(shape))


def local_call(
    kernel, outs, args, after=(), smem=(), scratch=(), grid=(1,), specs=None, grant=28
):
    return pl.pallas_call(
        kernel,
        out_shape=outs,
        grid=grid,
        in_specs=[SMEM] * len(smem) + (specs or [whole(a.shape) for a in args]) + [ANY] * len(after),
        out_specs=jax.tree.map(lambda o: whole(o.shape), outs),
        scratch_shapes=list(scratch),
        compiler_params=pltpu.CompilerParams(vmem_limit_bytes=grant * 1024 * 1024),
        name=kernel.__name__,
    )(*smem, *args, *after)


def at(i, size, step):
    return pl.ds(pl.multiple_of(i * size, step), size)


def project(at_ref, *refs):
    h_refs, up, down, far = refs[:4], refs[4:8], refs[8:11], refs[11:13]
    keep, send, w_all, acc = refs[13:]
    z, y, c = at_ref[1], at_ref[2], at_ref[3]
    cols = up[0].shape[0]
    for h in range(4):
        w_all[at(lax.rem(z + NZ - h, NZ), cols, 16), :] = up[h][...]
        if h:
            w_all[at(lax.rem(z + h, NZ), cols, 16), :] = down[h - 1][...]
    across = lax.rem(z + 4, NZ) * cols
    w_all[pl.ds(pl.multiple_of(across, 16), cols // 2), :] = far[0][...]
    w_all[pl.ds(pl.multiple_of(across + cols // 2, 16), cols // 2), :] = far[1][...]
    for h in range(NX):
        acc[...] = lax.dot_general(
            h_refs[h][...], w_all[...], (((1,), (1,)), ((), ())), preferred_element_type=F32
        )
        for g in range(NY):
            n = lax.rem(y + g, NY) * NC
            keep[g, h] = acc[at(n + c, NW, 32), :].astype(BF)
            send[g, h] = acc[at(n + 1 - c, NW, 32), :].astype(BF)


def add_pair(keep, other, *outs):
    for g in range(NY):
        outs[g][...] = (keep[g].astype(F32) + other[g].astype(F32)).astype(BF)


def add_four(*refs):
    outs = refs[-NX:]
    for h in range(NX):
        total = refs[0][h].astype(F32)
        for g in range(1, NY):
            total = total + refs[g][h].astype(F32)
        outs[h][...] = total.astype(BF)


def gate(ids, token, out):
    out[...] = ids[...]


def normalize(at_ref, b0, b1, b2, b3, resid, cents, from_host, keys, extra, stream):
    x = at_ref[0]
    span = b0.shape[1]
    width = cents.shape[2]
    for h, b in enumerate((b0, b1, b2, b3)):
        where = at(lax.rem(x + h, NX), span, 128)
        stream[:, where] = resid[:, where].astype(F32) + b[...].astype(F32)
    value = stream[...]
    scale = lax.rsqrt(jnp.mean(value * value, axis=1, keepdims=True) + EPS)
    for n in range(NN):
        part = slice(n * width, (n + 1) * width)
        tail = cents[n, NW:, :].astype(F32)
        key = (stream[:, part] * scale * tail[7:8]).astype(BF)
        keys[:, part] = key
        chosen = jnp.dot(from_host[...], key, preferred_element_type=F32)
        extra[:, part] = (chosen - tail).astype(BF)


def subtract(keys, cents, filled, token, out):
    width = cents.shape[2]
    for n in range(NN):
        part = slice(n * width, (n + 1) * width)
        diff = keys[:, part].astype(F32) - cents[n, :NW, :].astype(F32)
        out[:, part] = jnp.where(filled[...] > 0, diff, 0.0).astype(BF)


def split_rows(cent, *refs):
    out = refs[-1]
    width = out.shape[2]
    for n in range(NN):
        out[n] = cent[:, n * width : (n + 1) * width]


def hold(*refs):
    pass


def later(a, *after):
    return pl.pallas_call(
        hold,
        out_shape=like(a.shape, a.dtype),
        in_specs=[ANY] * (1 + len(after)),
        out_specs=ANY,
        input_output_aliases={0: 0},
        name="later",
    )(a, *after)


def accumulate(parts, rot, acc):
    lhs = jnp.concatenate([p[...] for p in parts], axis=0)
    new = jnp.dot(lhs, rot[...], preferred_element_type=F32)

    @pl.when(pl.program_id(0) == 0)
    def _():
        acc[...] = new

    @pl.when(pl.program_id(0) > 0)
    def _():
        acc[...] += new


def rotate_extra(*refs):
    parts, (rot, chosen, out, acc) = refs[:8], refs[8:]
    accumulate(parts, rot, acc)

    @pl.when(pl.program_id(0) == pl.num_programs(0) - 1)
    def _():
        rows = acc[...].astype(BF)
        picked = jnp.dot(chosen[...], rows, preferred_element_type=F32).astype(BF)
        for g in range(NZ):
            out[g] = picked


def rotate(*refs):
    parts, (rot, chosen, out, acc) = refs[:8], refs[8:]
    accumulate(parts, rot, acc)

    @pl.when(pl.program_id(0) == pl.num_programs(0) - 1)
    def _():
        rows = acc[...].astype(BF)
        out[...] = jnp.dot(chosen[...], rows, preferred_element_type=F32)


def lay_out(at_ref, rows, *refs):
    ext, out = refs[:NX], refs[-1]
    x, hot = at_ref[0], at_ref[4]
    extra = ext[0].shape[1]
    cap = NN + extra
    for h in range(NX):
        first = lax.rem(x + h, NX) * NZ
        for g in range(NZ):
            tail = jnp.where(hot > 0, ext[h][g].astype(F32), 0.0)
            both = jnp.concatenate([rows[at(first + g, NN, 8), :], tail], axis=0)
            out[at(first + g, cap, 32), :] = both.astype(BF)


def per_device(hidden, resid, w_out, key_gain, cluster_ids, centroids, rotation):
    xi, zi, yi, ci = (lax.axis_index(a) for a in ("x", "z", "y", "c"))
    ni = yi * NC + ci
    wi = xi * NZ + zi
    tokens, width = hidden.shape
    d = width * NN
    cap = 4 * tokens // NW
    cols = w_out.shape[1]
    wide_cols = NZ * cols
    extra = cap - NN
    per_n = extra // NN

    w_t = w_out.T
    up, down = [w_t], [w_t]
    for _ in range(3):
        up.append(shifted(up[-1], "z", NZ, 1))
        down.append(shifted(down[-1], "z", NZ, -1))
    far = [
        shifted(up[-1][: cols // 2], "z", NZ, 1),
        shifted(down[-1][cols // 2 :], "z", NZ, -1),
    ]

    place, cell, hot, short, nth = places(cluster_ids, cap, NN)
    where_am_i = jnp.stack([xi, zi, yi, ci, (wi == hot).astype(I32)]).astype(I32)
    hidden_p = choose_rows(iota((tokens, 1), 0) == place[None, :], hidden)
    h_parts = [hidden_p] + [shifted(hidden_p, "x", NX, h) for h in (1, 2, 3)]

    cent_split = local_call(
        split_rows,
        like((NN, centroids.shape[0], width)),
        (centroids,),
        after=(up[1], down[1]),
    )
    cent_tile = lax.all_to_all(cent_split, NARROW, 0, 0, tiled=True).reshape(-1, width)

    cell_of = cell[:, None] == iota((1, NW * cap), 1)
    send_ids = jnp.sum(jnp.where(cell_of, cluster_ids[:, None] + 1, 0), axis=0) - 1
    send_ids = later(send_ids.reshape(NW, cap), cent_tile, *far, h_parts[2], h_parts[1])
    got_ids = lax.all_to_all(send_ids, WIDE, 0, 0, tiled=True)

    block = like((NY, NX, NW, wide_cols))
    keep, send = local_call(
        project,
        (block, block),
        (*h_parts, *up, *down[1:], *far),
        smem=(where_am_i,),
        scratch=[pltpu.VMEM((wide_cols, width), BF), pltpu.VMEM((tokens, wide_cols), F32)],
    )
    pairs = local_call(
        add_pair, [like((NX, NW, wide_cols))] * NY, (keep, shifted(send, "c", NC, 1))
    )

    local = jnp.where(got_ids >= 0, got_ids - wi * CL_DEV, -1)
    local = local_call(gate, like(local.shape, I32), (local,), after=(keep,))
    clusters = iota((1, CL_DEV), 1)
    cent_own = choose_rows(local[:, :NN].T.reshape(-1, 1) == clusters, cent_tile)
    cent_out = choose_rows(local[:, NN:].reshape(-1, 1) == clusters, cent_tile)
    cent_in = pick(lax.all_to_all(cent_out.reshape(NW, extra, width), WIDE, 0, 0, tiled=True), hot)
    cent_pre = jnp.concatenate(
        [
            cent_own.reshape(NN, NW, width),
            cent_in.reshape(per_n, NN, width).transpose(1, 0, 2),
            jnp.broadcast_to(key_gain, (NN, 8 - per_n, width)),
        ],
        axis=1,
    )
    cents = lax.all_to_all(cent_pre, NARROW, 0, 0, tiled=True)

    own_place = ni * NW + iota((NW, 1), 0) == place[None, :]
    resid_rows = choose_rows(own_place, resid)

    sums = local_call(
        add_four,
        [like((NW, wide_cols))] * NX,
        (pairs[0], *[shifted(pairs[g], "y", NY, g) for g in (1, 2, 3)]),
    )
    q = iota((8, 1), 0)
    from_host = (short[None, :] & (nth[None, :] == q * NN + ni) & (q < per_n)).astype(BF)
    keys, res_extra = local_call(
        normalize,
        (like((NW, d)), like((8, d))),
        (
            sums[0],
            *[shifted(sums[h], "x", NX, -h) for h in (1, 2, 3)],
            resid_rows,
            cents,
            from_host,
        ),
        smem=(where_am_i,),
        scratch=[pltpu.VMEM((NW, d), F32)],
        grant=58,
    )

    n_of = ((yi - iota((NC, NY, 1), 1)) % NY) * NC + (ci + iota((NC, NY, 1), 0)) % NC

    got = lax.all_to_all(keys.reshape(NW, NN, width), WIDE, 0, 0, tiled=True).reshape(NW, d)
    filled = (pick(got_ids, ni, 1) >= 0).astype(F32)[:, None]
    steps = 4
    rot_spec = pl.BlockSpec((d // steps, width), lambda k: (k, 0))

    def row_specs(rows):
        return [pl.BlockSpec((rows, d // steps), lambda k: (0, k))] * NN

    pieces = [res_extra] + [shifted(res_extra, "y", NY, h) for h in (1, 2, 3)]
    pieces = pieces + [shifted(p, "c", NC, 1) for p in pieces]
    ext_j = (iota((NC, NY, 8), 2) * NN + n_of).reshape(1, -1)
    choose_ext = (ext_j == iota((extra, 1), 0)).astype(BF)
    ext = local_call(
        rotate_extra,
        like((NZ, extra, width)),
        (*pieces, rotation, choose_ext),
        scratch=[pltpu.VMEM((NN * 8, width), F32)],
        grid=(steps,),
        specs=row_specs(8) + [rot_spec, whole(choose_ext.shape)],
    )
    residual = local_call(subtract, like((NW, d)), (got, cents, filled), after=(ext,))
    parts = [residual] + [shifted(residual, "y", NY, h) for h in (1, 2, 3)]
    parts = parts + [shifted(p, "c", NC, 1) for p in parts]
    ext = lax.all_to_all(ext, "z", 0, 0, tiled=True)
    ext = [ext] + [shifted(ext, "x", NX, -h) for h in range(1, NX)]

    gap = jnp.min(jnp.where(got_ids[:, :NN] < 0, iota((1, NN), 1), NN), axis=1)
    rank = iota((1, NN), 1)
    from_n = (rank + (rank >= gap[:, None]).astype(I32)).reshape(-1, 1)
    from_s = iota((NW, NN), 0).reshape(-1, 1)
    row_n = jnp.broadcast_to(n_of, (NC, NY, NW)).reshape(1, -1)
    row_s = iota((NC, NY, NW), 2).reshape(1, -1)
    chosen = ((from_n == row_n) & (from_s == row_s)).astype(BF)
    rotated = local_call(
        rotate,
        like((NN * NW, width), F32),
        (*parts, rotation, chosen),
        scratch=[pltpu.VMEM((NN * NW, width), F32)],
        grid=(steps,),
        specs=row_specs(NW) + [rot_spec, whole(chosen.shape)],
    )
    return local_call(
        lay_out, like((NW * cap, width)), (rotated, *ext), smem=(where_am_i,), grant=58
    )


def solution(mesh):
    grid = Mesh(mesh.devices.reshape(NX, NZ, NY, NC), ("x", "z", "y", "c"))
    placed = (
        P(WIDE, NARROW),
        P(WIDE, None),
        P(NARROW, WIDE),
        P(NARROW),
        P(WIDE),
        P(WIDE + NARROW, None),
        P(None, NARROW),
    )
    return jax.shard_map(
        per_device, mesh=grid, in_specs=placed, out_specs=P(WIDE, NARROW), check_vma=False
    )
```

```python
import jax
import jax.numpy as jnp
from jax import lax
from jax.experimental import pallas as pl
from jax.experimental.pallas import tpu as pltpu
from jax.sharding import Mesh, PartitionSpec as P

CL_DEV = 1024
EPS = 1e-05
NX, NZ, NY, NC = 4, 8, 4, 2
WIDE = ("x", "z")
NARROW = ("y", "c")
NN = NY * NC
NW = NX * NZ
BF = jnp.bfloat16
F32 = jnp.float32
I32 = jnp.int32


def shifted(a, axis, n, h):
    return lax.ppermute(a, axis, [(i, (i + h) % n) for i in range(n)])


def pick(a, i, axis=0):
    return lax.dynamic_index_in_dim(a, i, axis, keepdims=False)


def iota(shape, dim):
    return lax.broadcasted_iota(I32, shape, dim)


def choose_rows(onehot, a):
    return jnp.dot(onehot.astype(BF), a, preferred_element_type=F32).astype(BF)


def places(ids, cap, per_owner):
    owner = ids // CL_DEV
    onehot = (owner[:, None] == iota((1, NW), 1)).astype(I32)
    rank = jnp.sum((jnp.cumsum(onehot, axis=0) - onehot) * onehot, axis=1)
    count = jnp.sum(onehot, axis=0)
    hot = jnp.argmax(count).astype(I32)
    short = count < per_owner
    nth = jnp.cumsum(short.astype(I32)) - short.astype(I32)
    gap = jnp.where(short, nth % per_owner, per_owner)
    n_of = rank + (rank >= jnp.sum(onehot * gap[None, :], axis=1)).astype(I32)
    surplus = rank >= per_owner
    j = rank - per_owner
    host = jnp.sum(
        jnp.where(short[None, :] & (nth[None, :] == j[:, None]), iota((1, NW), 1), 0), axis=1
    )
    place = jnp.where(surplus, (j % per_owner) * NW + host, n_of * NW + owner)
    cell = owner * cap + jnp.where(surplus, rank, n_of)
    return place, cell, hot, short, nth


SMEM = pl.BlockSpec(memory_space=pltpu.SMEM)
ANY = pl.BlockSpec(memory_space=pl.ANY)


def like(shape, dtype=BF):
    return jax.ShapeDtypeStruct(shape, dtype)


def whole(shape):
    return pl.BlockSpec(shape, lambda i: (0,) * len(shape))


def local_call(
    kernel, outs, args, after=(), smem=(), scratch=(), grid=(1,), specs=None, grant=28
):
    return pl.pallas_call(
        kernel,
        out_shape=outs,
        grid=grid,
        in_specs=[SMEM] * len(smem) + (specs or [whole(a.shape) for a in args]) + [ANY] * len(after),
        out_specs=jax.tree.map(lambda o: whole(o.shape), outs),
        scratch_shapes=list(scratch),
        compiler_params=pltpu.CompilerParams(vmem_limit_bytes=grant * 1024 * 1024),
        name=kernel.__name__,
    )(*smem, *args, *after)


def at(i, size, step):
    return pl.ds(pl.multiple_of(i * size, step), size)


def project(at_ref, *refs):
    h_refs, up, down, far = refs[:4], refs[4:8], refs[8:11], refs[11:13]
    keep, send, w_all, acc = refs[13:]
    z, y, c = at_ref[1], at_ref[2], at_ref[3]
    cols = up[0].shape[0]
    for h in range(4):
        w_all[at(lax.rem(z + NZ - h, NZ), cols, 16), :] = up[h][...]
        if h:
            w_all[at(lax.rem(z + h, NZ), cols, 16), :] = down[h - 1][...]
    across = lax.rem(z + 4, NZ) * cols
    w_all[pl.ds(pl.multiple_of(across, 16), cols // 2), :] = far[0][...]
    w_all[pl.ds(pl.multiple_of(across + cols // 2, 16), cols // 2), :] = far[1][...]
    for h in range(NX):
        acc[...] = lax.dot_general(
            h_refs[h][...], w_all[...], (((1,), (1,)), ((), ())), preferred_element_type=F32
        )
        for g in range(NY):
            n = lax.rem(y + g, NY) * NC
            keep[g, h] = acc[at(n + c, NW, 32), :].astype(BF)
            send[g, h] = acc[at(n + 1 - c, NW, 32), :].astype(BF)


def add_pair(keep, other, *outs):
    for g in range(NY):
        outs[g][...] = (keep[g].astype(F32) + other[g].astype(F32)).astype(BF)


def add_four(*refs):
    outs = refs[-NX:]
    for h in range(NX):
        total = refs[0][h].astype(F32)
        for g in range(1, NY):
            total = total + refs[g][h].astype(F32)
        outs[h][...] = total.astype(BF)


def gate(ids, token, out):
    out[...] = ids[...]


def normalize(at_ref, b0, b1, b2, b3, resid, cents, from_host, keys, extra, stream):
    x = at_ref[0]
    span = b0.shape[1]
    width = cents.shape[2]
    for h, b in enumerate((b0, b1, b2, b3)):
        where = at(lax.rem(x + h, NX), span, 128)
        stream[:, where] = resid[:, where].astype(F32) + b[...].astype(F32)
    value = stream[...]
    scale = lax.rsqrt(jnp.mean(value * value, axis=1, keepdims=True) + EPS)
    for n in range(NN):
        part = slice(n * width, (n + 1) * width)
        tail = cents[n, NW:, :].astype(F32)
        key = (stream[:, part] * scale * tail[7:8]).astype(BF)
        keys[:, part] = key
        chosen = jnp.dot(from_host[...], key, preferred_element_type=F32)
        extra[:, part] = (chosen - tail).astype(BF)


def subtract(keys, cents, filled, token, out):
    width = cents.shape[2]
    for n in range(NN):
        part = slice(n * width, (n + 1) * width)
        diff = keys[:, part].astype(F32) - cents[n, :NW, :].astype(F32)
        out[:, part] = jnp.where(filled[...] > 0, diff, 0.0).astype(BF)


def split_rows(cent, *refs):
    out = refs[-1]
    width = out.shape[2]
    for n in range(NN):
        out[n] = cent[:, n * width : (n + 1) * width]


def hold(*refs):
    pass


def later(a, *after):
    return pl.pallas_call(
        hold,
        out_shape=like(a.shape, a.dtype),
        in_specs=[ANY] * (1 + len(after)),
        out_specs=ANY,
        input_output_aliases={0: 0},
        name="later",
    )(a, *after)


def accumulate(parts, rot, acc):
    lhs = jnp.concatenate([p[...] for p in parts], axis=0)
    new = jnp.dot(lhs, rot[...], preferred_element_type=F32)

    @pl.when(pl.program_id(0) == 0)
    def _():
        acc[...] = new

    @pl.when(pl.program_id(0) > 0)
    def _():
        acc[...] += new


def rotate_extra(*refs):
    parts, (rot, chosen, out, acc) = refs[:8], refs[8:]
    accumulate(parts, rot, acc)

    @pl.when(pl.program_id(0) == pl.num_programs(0) - 1)
    def _():
        rows = acc[...].astype(BF)
        picked = jnp.dot(chosen[...], rows, preferred_element_type=F32).astype(BF)
        for g in range(NZ):
            out[g] = picked


def rotate(*refs):
    parts, (rot, chosen, out, acc) = refs[:8], refs[8:]
    accumulate(parts, rot, acc)

    @pl.when(pl.program_id(0) == pl.num_programs(0) - 1)
    def _():
        rows = acc[...].astype(BF)
        out[...] = jnp.dot(chosen[...], rows, preferred_element_type=F32)


def lay_out(at_ref, rows, *refs):
    ext, out = refs[:NX], refs[-1]
    x, hot = at_ref[0], at_ref[4]
    extra = ext[0].shape[1]
    cap = NN + extra
    for h in range(NX):
        first = lax.rem(x + h, NX) * NZ
        for g in range(NZ):
            tail = jnp.where(hot > 0, ext[h][g].astype(F32), 0.0)
            both = jnp.concatenate([rows[at(first + g, NN, 8), :], tail], axis=0)
            out[at(first + g, cap, 32), :] = both.astype(BF)


def per_device(hidden, resid, w_out, key_gain, cluster_ids, centroids, rotation):
    xi, zi, yi, ci = (lax.axis_index(a) for a in ("x", "z", "y", "c"))
    ni = yi * NC + ci
    wi = xi * NZ + zi
    tokens, width = hidden.shape
    d = width * NN
    cap = 4 * tokens // NW
    cols = w_out.shape[1]
    wide_cols = NZ * cols
    extra = cap - NN
    per_n = extra // NN

    w_t = w_out.T
    up, down = [w_t], [w_t]
    for _ in range(2):
        up.append(shifted(up[-1], "z", NZ, 1))
        down.append(shifted(down[-1], "z", NZ, -1))

    place, cell, hot, short, nth = places(cluster_ids, cap, NN)
    where_am_i = jnp.stack([xi, zi, yi, ci, (wi == hot).astype(I32)]).astype(I32)
    hidden_p = choose_rows(iota((tokens, 1), 0) == place[None, :], hidden)
    h_parts = [hidden_p] + [shifted(hidden_p, "x", NX, h) for h in (1, 2, 3)]
    up.append(shifted(later(up[2], h_parts[1]), "z", NZ, 1))
    down.append(shifted(down[2], "z", NZ, -1))
    far = [
        shifted(up[3][: cols // 2], "z", NZ, 1),
        shifted(down[3][cols // 2 :], "z", NZ, -1),
    ]

    cent_split = local_call(
        split_rows,
        like((NN, centroids.shape[0], width)),
        (centroids,),
        after=(up[1], down[1]),
    )
    cent_tile = lax.all_to_all(cent_split, NARROW, 0, 0, tiled=True).reshape(-1, width)

    cell_of = cell[:, None] == iota((1, NW * cap), 1)
    send_ids = jnp.sum(jnp.where(cell_of, cluster_ids[:, None] + 1, 0), axis=0) - 1
    send_ids = later(send_ids.reshape(NW, cap), cent_tile, *far, h_parts[2], h_parts[1])
    got_ids = lax.all_to_all(send_ids, WIDE, 0, 0, tiled=True)

    block = like((NY, NX, NW, wide_cols))
    keep, send = local_call(
        project,
        (block, block),
        (*h_parts, *up, *down[1:], *far),
        smem=(where_am_i,),
        scratch=[pltpu.VMEM((wide_cols, width), BF), pltpu.VMEM((tokens, wide_cols), F32)],
        grant=58,
    )
    pairs = local_call(
        add_pair, [like((NX, NW, wide_cols))] * NY, (keep, shifted(send, "c", NC, 1)), grant=58
    )

    n_of = ((yi - iota((NC, NY, 1), 1)) % NY) * NC + (ci + iota((NC, NY, 1), 0)) % NC
    filled = (pick(got_ids, ni, 1) >= 0).astype(F32)[:, None]
    ext_j = (iota((NC, NY, 8), 2) * NN + n_of).reshape(1, -1)
    choose_ext = (ext_j == iota((extra, 1), 0)).astype(BF)
    gap = jnp.min(jnp.where(got_ids[:, :NN] < 0, iota((1, NN), 1), NN), axis=1)
    rank = iota((1, NN), 1)
    from_n = (rank + (rank >= gap[:, None]).astype(I32)).reshape(-1, 1)
    from_s = iota((NW, NN), 0).reshape(-1, 1)
    row_n = jnp.broadcast_to(n_of, (NC, NY, NW)).reshape(1, -1)
    row_s = iota((NC, NY, NW), 2).reshape(1, -1)
    chosen = ((from_n == row_n) & (from_s == row_s)).astype(BF)

    sums = local_call(
        add_four,
        [like((NW, wide_cols))] * NX,
        (pairs[0], *[shifted(pairs[g], "y", NY, g) for g in (1, 2, 3)]),
        after=(chosen, choose_ext, filled),
    )

    local = jnp.where(got_ids >= 0, got_ids - wi * CL_DEV, -1)
    local = local_call(gate, like(local.shape, I32), (local,), after=(keep,))
    clusters = iota((1, CL_DEV), 1)
    cent_own = choose_rows(local[:, :NN].T.reshape(-1, 1) == clusters, cent_tile)
    cent_out = choose_rows(local[:, NN:].reshape(-1, 1) == clusters, cent_tile)
    cent_in = lax.all_to_all(cent_out.reshape(NW, extra, width), WIDE, 0, 0, tiled=True)
    cent_in = pick(later(cent_in, sums[1]), hot)
    cent_pre = jnp.concatenate(
        [
            cent_own.reshape(NN, NW, width),
            cent_in.reshape(per_n, NN, width).transpose(1, 0, 2),
            jnp.broadcast_to(key_gain, (NN, 8 - per_n, width)),
        ],
        axis=1,
    )
    cents = lax.all_to_all(cent_pre, NARROW, 0, 0, tiled=True)

    own_place = ni * NW + iota((NW, 1), 0) == place[None, :]
    resid_rows = choose_rows(own_place, resid)

    q = iota((8, 1), 0)
    from_host = (short[None, :] & (nth[None, :] == q * NN + ni) & (q < per_n)).astype(BF)
    keys, res_extra = local_call(
        normalize,
        (like((NW, d)), like((8, d))),
        (
            sums[0],
            *[shifted(sums[h], "x", NX, -h) for h in (1, 2, 3)],
            resid_rows,
            cents,
            from_host,
        ),
        smem=(where_am_i,),
        scratch=[pltpu.VMEM((NW, d), F32)],
        grant=58,
    )

    got = lax.all_to_all(keys.reshape(NW, NN, width), WIDE, 0, 0, tiled=True).reshape(NW, d)
    steps = 4
    rot_spec = pl.BlockSpec((d // steps, width), lambda k: (k, 0))

    def row_specs(rows):
        return [pl.BlockSpec((rows, d // steps), lambda k: (0, k))] * NN

    pieces = [res_extra] + [shifted(res_extra, "y", NY, h) for h in (1, 2, 3)]
    pieces = pieces + [shifted(p, "c", NC, 1) for p in pieces]
    ext = local_call(
        rotate_extra,
        like((NZ, extra, width)),
        (*pieces, rotation, choose_ext),
        scratch=[pltpu.VMEM((NN * 8, width), F32)],
        grid=(steps,),
        specs=row_specs(8) + [rot_spec, whole(choose_ext.shape)],
    )
    residual = local_call(subtract, like((NW, d)), (got, cents, filled), after=(ext,))
    parts = [residual] + [shifted(residual, "y", NY, h) for h in (1, 2, 3)]
    parts = parts + [shifted(p, "c", NC, 1) for p in parts]
    ext = lax.all_to_all(ext, "z", 0, 0, tiled=True)
    ext = [ext] + [shifted(ext, "x", NX, -h) for h in range(1, NX)]

    rotated = local_call(
        rotate,
        like((NN * NW, width), F32),
        (*parts, rotation, chosen),
        scratch=[pltpu.VMEM((NN * NW, width), F32)],
        grid=(steps,),
        specs=row_specs(NW) + [rot_spec, whole(chosen.shape)],
    )
    return local_call(
        lay_out, like((NW * cap, width)), (rotated, *ext), smem=(where_am_i,), grant=58
    )


def solution(mesh):
    grid = Mesh(mesh.devices.reshape(NX, NZ, NY, NC), ("x", "z", "y", "c"))
    placed = (
        P(WIDE, NARROW),
        P(WIDE, None),
        P(NARROW, WIDE),
        P(NARROW),
        P(WIDE),
        P(WIDE + NARROW, None),
        P(None, NARROW),
    )
    return jax.shard_map(
        per_device, mesh=grid, in_specs=placed, out_specs=P(WIDE, NARROW), check_vma=False
    )
```

```python
import jax
import jax.numpy as jnp
from jax import lax
from jax.experimental import pallas as pl
from jax.experimental.pallas import tpu as pltpu
from jax.sharding import Mesh, PartitionSpec as P

CL_DEV = 1024
EPS = 1e-05
NX, NZ, NY, NC = 4, 8, 4, 2
WIDE = ("x", "z")
NARROW = ("y", "c")
NN = NY * NC
NW = NX * NZ
BF = jnp.bfloat16
F32 = jnp.float32
I32 = jnp.int32


def shifted(a, axis, n, h):
    return lax.ppermute(a, axis, [(i, (i + h) % n) for i in range(n)])


def pick(a, i, axis=0):
    return lax.dynamic_index_in_dim(a, i, axis, keepdims=False)


def iota(shape, dim):
    return lax.broadcasted_iota(I32, shape, dim)


def choose_rows(onehot, a):
    return jnp.dot(onehot.astype(BF), a, preferred_element_type=F32).astype(BF)


def places(ids, cap, per_owner):
    owner = ids // CL_DEV
    onehot = (owner[:, None] == iota((1, NW), 1)).astype(I32)
    rank = jnp.sum((jnp.cumsum(onehot, axis=0) - onehot) * onehot, axis=1)
    count = jnp.sum(onehot, axis=0)
    hot = jnp.argmax(count).astype(I32)
    short = count < per_owner
    nth = jnp.cumsum(short.astype(I32)) - short.astype(I32)
    gap = jnp.where(short, nth % per_owner, per_owner)
    n_of = rank + (rank >= jnp.sum(onehot * gap[None, :], axis=1)).astype(I32)
    surplus = rank >= per_owner
    j = rank - per_owner
    host = jnp.sum(
        jnp.where(short[None, :] & (nth[None, :] == j[:, None]), iota((1, NW), 1), 0), axis=1
    )
    place = jnp.where(surplus, (j % per_owner) * NW + host, n_of * NW + owner)
    cell = owner * cap + jnp.where(surplus, rank, n_of)
    return place, cell, hot, short, nth


SMEM = pl.BlockSpec(memory_space=pltpu.SMEM)
ANY = pl.BlockSpec(memory_space=pl.ANY)


def like(shape, dtype=BF):
    return jax.ShapeDtypeStruct(shape, dtype)


def whole(shape):
    return pl.BlockSpec(shape, lambda i: (0,) * len(shape))


def local_call(
    kernel, outs, args, after=(), smem=(), scratch=(), grid=(1,), specs=None, grant=28
):
    return pl.pallas_call(
        kernel,
        out_shape=outs,
        grid=grid,
        in_specs=[SMEM] * len(smem) + (specs or [whole(a.shape) for a in args]) + [ANY] * len(after),
        out_specs=jax.tree.map(lambda o: whole(o.shape), outs),
        scratch_shapes=list(scratch),
        compiler_params=pltpu.CompilerParams(vmem_limit_bytes=grant * 1024 * 1024),
        name=kernel.__name__,
    )(*smem, *args, *after)


def at(i, size, step):
    return pl.ds(pl.multiple_of(i * size, step), size)


def project(at_ref, *refs):
    h_refs, up, down, far = refs[:4], refs[4:8], refs[8:11], refs[11:13]
    keep, send, w_all, acc = refs[13:]
    z, y, c = at_ref[1], at_ref[2], at_ref[3]
    cols = up[0].shape[0]
    for h in range(4):
        w_all[at(lax.rem(z + NZ - h, NZ), cols, 16), :] = up[h][...]
        if h:
            w_all[at(lax.rem(z + h, NZ), cols, 16), :] = down[h - 1][...]
    across = lax.rem(z + 4, NZ) * cols
    w_all[pl.ds(pl.multiple_of(across, 16), cols // 2), :] = far[0][...]
    w_all[pl.ds(pl.multiple_of(across + cols // 2, 16), cols // 2), :] = far[1][...]
    for h in range(NX):
        acc[...] = lax.dot_general(
            h_refs[h][...], w_all[...], (((1,), (1,)), ((), ())), preferred_element_type=F32
        )
        for g in range(NY):
            n = lax.rem(y + g, NY) * NC
            keep[g, h] = acc[at(n + c, NW, 32), :].astype(BF)
            send[g, h] = acc[at(n + 1 - c, NW, 32), :].astype(BF)


def add_pair(keep, other, *outs):
    for g in range(NY):
        outs[g][...] = (keep[g].astype(F32) + other[g].astype(F32)).astype(BF)


def add_four(*refs):
    outs = refs[-NX:]
    for h in range(NX):
        total = refs[0][h].astype(F32)
        for g in range(1, NY):
            total = total + refs[g][h].astype(F32)
        outs[h][...] = total.astype(BF)


def gate(ids, token, out):
    out[...] = ids[...]


def normalize(at_ref, b0, b1, b2, b3, resid, cents, from_host, keys, extra, stream):
    x = at_ref[0]
    span = b0.shape[1]
    width = cents.shape[2]
    for h, b in enumerate((b0, b1, b2, b3)):
        where = at(lax.rem(x + h, NX), span, 128)
        stream[:, where] = resid[:, where].astype(F32) + b[...].astype(F32)
    value = stream[...]
    scale = lax.rsqrt(jnp.mean(value * value, axis=1, keepdims=True) + EPS)
    for n in range(NN):
        part = slice(n * width, (n + 1) * width)
        tail = cents[n, NW:, :].astype(F32)
        key = (stream[:, part] * scale * tail[7:8]).astype(BF)
        keys[:, part] = key
        chosen = jnp.dot(from_host[...], key, preferred_element_type=F32)
        extra[:, part] = (chosen - tail).astype(BF)


def subtract(keys, cents, filled, token, out):
    width = cents.shape[2]
    for n in range(NN):
        part = slice(n * width, (n + 1) * width)
        diff = keys[:, part].astype(F32) - cents[n, :NW, :].astype(F32)
        out[:, part] = jnp.where(filled[...] > 0, diff, 0.0).astype(BF)


def split_rows(cent, *refs):
    out = refs[-1]
    width = out.shape[2]
    for n in range(NN):
        out[n] = cent[:, n * width : (n + 1) * width]


def hold(*refs):
    pass


def later(a, *after):
    return pl.pallas_call(
        hold,
        out_shape=like(a.shape, a.dtype),
        in_specs=[ANY] * (1 + len(after)),
        out_specs=ANY,
        input_output_aliases={0: 0},
        name="later",
    )(a, *after)


def accumulate(parts, rot, acc):
    lhs = jnp.concatenate([p[...] for p in parts], axis=0)
    new = jnp.dot(lhs, rot[...], preferred_element_type=F32)

    @pl.when(pl.program_id(0) == 0)
    def _():
        acc[...] = new

    @pl.when(pl.program_id(0) > 0)
    def _():
        acc[...] += new


def rotate_extra(*refs):
    parts, (rot, chosen, out, acc) = refs[:8], refs[8:]
    accumulate(parts, rot, acc)

    @pl.when(pl.program_id(0) == pl.num_programs(0) - 1)
    def _():
        rows = acc[...].astype(BF)
        picked = jnp.dot(chosen[...], rows, preferred_element_type=F32).astype(BF)
        for g in range(NZ):
            out[g] = picked


def rotate(*refs):
    parts, (rot, chosen, out, acc) = refs[:8], refs[8:]
    accumulate(parts, rot, acc)

    @pl.when(pl.program_id(0) == pl.num_programs(0) - 1)
    def _():
        rows = acc[...].astype(BF)
        out[...] = jnp.dot(chosen[...], rows, preferred_element_type=F32)


def lay_out(at_ref, rows, *refs):
    ext, out = refs[:NX], refs[-1]
    x, hot = at_ref[0], at_ref[4]
    extra = ext[0].shape[1]
    cap = NN + extra
    for h in range(NX):
        first = lax.rem(x + h, NX) * NZ
        for g in range(NZ):
            tail = jnp.where(hot > 0, ext[h][g].astype(F32), 0.0)
            both = jnp.concatenate([rows[at(first + g, NN, 8), :], tail], axis=0)
            out[at(first + g, cap, 32), :] = both.astype(BF)


def per_device(hidden, resid, w_out, key_gain, cluster_ids, centroids, rotation):
    xi, zi, yi, ci = (lax.axis_index(a) for a in ("x", "z", "y", "c"))
    ni = yi * NC + ci
    wi = xi * NZ + zi
    tokens, width = hidden.shape
    d = width * NN
    cap = 4 * tokens // NW
    cols = w_out.shape[1]
    wide_cols = NZ * cols
    extra = cap - NN
    per_n = extra // NN

    w_t = w_out.T
    up, down = [w_t], [w_t]
    for _ in range(2):
        up.append(shifted(up[-1], "z", NZ, 1))
        down.append(shifted(down[-1], "z", NZ, -1))

    place, cell, hot, short, nth = places(cluster_ids, cap, NN)
    where_am_i = jnp.stack([xi, zi, yi, ci, (wi == hot).astype(I32)]).astype(I32)
    hidden_p = choose_rows(iota((tokens, 1), 0) == place[None, :], hidden)
    h_parts = [hidden_p] + [shifted(hidden_p, "x", NX, h) for h in (1, 2, 3)]
    up.append(shifted(later(up[2], h_parts[1]), "z", NZ, 1))
    down.append(shifted(down[2], "z", NZ, -1))
    far = [
        shifted(up[3][: cols // 2], "z", NZ, 1),
        shifted(down[3][cols // 2 :], "z", NZ, -1),
    ]

    cent_split = local_call(
        split_rows,
        like((NN, centroids.shape[0], width)),
        (centroids,),
        after=(up[1], down[1]),
    )
    cent_tile = lax.all_to_all(cent_split, NARROW, 0, 0, tiled=True).reshape(-1, width)

    cell_of = cell[:, None] == iota((1, NW * cap), 1)
    send_ids = jnp.sum(jnp.where(cell_of, cluster_ids[:, None] + 1, 0), axis=0) - 1
    send_ids = later(send_ids.reshape(NW, cap), cent_tile, *far, h_parts[2], h_parts[1])
    got_ids = lax.all_to_all(send_ids, WIDE, 0, 0, tiled=True)

    block = like((NY, NX, NW, wide_cols))
    keep, send = local_call(
        project,
        (block, block),
        (*h_parts, *up, *down[1:], *far),
        smem=(where_am_i,),
        scratch=[pltpu.VMEM((wide_cols, width), BF), pltpu.VMEM((tokens, wide_cols), F32)],
        grant=58,
    )
    pairs = local_call(
        add_pair, [like((NX, NW, wide_cols))] * NY, (keep, shifted(send, "c", NC, 1)), grant=58
    )

    n_of = ((yi - iota((NC, NY, 1), 1)) % NY) * NC + (ci + iota((NC, NY, 1), 0)) % NC
    filled = (pick(got_ids, ni, 1) >= 0).astype(F32)[:, None]
    ext_j = (iota((NC, NY, 8), 2) * NN + n_of).reshape(1, -1)
    choose_ext = (ext_j == iota((extra, 1), 0)).astype(BF)
    gap = jnp.min(jnp.where(got_ids[:, :NN] < 0, iota((1, NN), 1), NN), axis=1)
    rank = iota((1, NN), 1)
    from_n = (rank + (rank >= gap[:, None]).astype(I32)).reshape(-1, 1)
    from_s = iota((NW, NN), 0).reshape(-1, 1)
    row_n = jnp.broadcast_to(n_of, (NC, NY, NW)).reshape(1, -1)
    row_s = iota((NC, NY, NW), 2).reshape(1, -1)
    chosen = ((from_n == row_n) & (from_s == row_s)).astype(BF)

    sums = local_call(
        add_four,
        [like((NW, wide_cols))] * NX,
        (pairs[0], *[shifted(pairs[g], "y", NY, g) for g in (1, 2, 3)]),
        after=(chosen, choose_ext, filled),
    )

    local = jnp.where(got_ids >= 0, got_ids - wi * CL_DEV, -1)
    local = local_call(gate, like(local.shape, I32), (local,), after=(keep,))
    clusters = iota((1, CL_DEV), 1)
    cent_own = choose_rows(local[:, :NN].T.reshape(-1, 1) == clusters, cent_tile)
    cent_out = choose_rows(local[:, NN:].reshape(-1, 1) == clusters, cent_tile)
    cent_in = lax.all_to_all(cent_out.reshape(NW, extra, width), WIDE, 0, 0, tiled=True)
    cent_in = pick(later(cent_in, sums[1]), hot)
    cent_pre = jnp.concatenate(
        [
            cent_own.reshape(NN, NW, width),
            cent_in.reshape(per_n, NN, width).transpose(1, 0, 2),
            jnp.broadcast_to(key_gain, (NN, 8 - per_n, width)),
        ],
        axis=1,
    )
    cents = lax.all_to_all(cent_pre, NARROW, 0, 0, tiled=True)

    own_place = ni * NW + iota((NW, 1), 0) == place[None, :]
    resid_rows = choose_rows(own_place, resid)

    q = iota((8, 1), 0)
    from_host = (short[None, :] & (nth[None, :] == q * NN + ni) & (q < per_n)).astype(BF)
    keys, res_extra = local_call(
        normalize,
        (like((NW, d)), like((8, d))),
        (
            sums[0],
            *[shifted(sums[h], "x", NX, -h) for h in (1, 2, 3)],
            resid_rows,
            cents,
            from_host,
        ),
        smem=(where_am_i,),
        scratch=[pltpu.VMEM((NW, d), F32)],
        grant=58,
    )

    got = lax.all_to_all(keys.reshape(NW, NN, width), WIDE, 0, 0, tiled=True).reshape(NW, d)
    steps = 4
    rot_spec = pl.BlockSpec((d // steps, width), lambda k: (k, 0))

    def row_specs(rows):
        return [pl.BlockSpec((rows, d // steps), lambda k: (0, k))] * NN

    pieces = [res_extra] + [shifted(res_extra, "y", NY, h) for h in (1, 2, 3)]
    pieces = pieces + [shifted(p, "c", NC, 1) for p in pieces]
    ext = local_call(
        rotate_extra,
        like((NZ, extra, width)),
        (*pieces, rotation, choose_ext),
        scratch=[pltpu.VMEM((NN * 8, width), F32)],
        grid=(steps,),
        specs=row_specs(8) + [rot_spec, whole(choose_ext.shape)],
    )
    residual = local_call(subtract, like((NW, d)), (got, cents, filled), after=(ext,))
    parts = [residual] + [shifted(residual, "y", NY, h) for h in (1, 2, 3)]
    ext = lax.all_to_all(ext, "z", 0, 0, tiled=True)
    parts = parts[:2] + [later(p, ext) for p in parts[2:]]
    parts = parts + [shifted(p, "c", NC, 1) for p in parts]
    ext = [ext] + [shifted(ext, "x", NX, -h) for h in range(1, NX)]

    rotated = local_call(
        rotate,
        like((NN * NW, width), F32),
        (*parts, rotation, chosen),
        scratch=[pltpu.VMEM((NN * NW, width), F32)],
        grid=(steps,),
        specs=row_specs(NW) + [rot_spec, whole(chosen.shape)],
    )
    return local_call(
        lay_out, like((NW * cap, width)), (rotated, *ext), smem=(where_am_i,), grant=58
    )


def solution(mesh):
    grid = Mesh(mesh.devices.reshape(NX, NZ, NY, NC), ("x", "z", "y", "c"))
    placed = (
        P(WIDE, NARROW),
        P(WIDE, None),
        P(NARROW, WIDE),
        P(NARROW),
        P(WIDE),
        P(WIDE + NARROW, None),
        P(None, NARROW),
    )
    return jax.shard_map(
        per_device, mesh=grid, in_specs=placed, out_specs=P(WIDE, NARROW), check_vma=False
    )
```

```python
import jax
import jax.numpy as jnp
from jax import lax
from jax.experimental import pallas as pl
from jax.experimental.pallas import tpu as pltpu
from jax.sharding import Mesh, PartitionSpec as P

CL_DEV = 1024
EPS = 1e-05
NX, NZ, NY, NC = 4, 8, 4, 2
WIDE = ("x", "z")
NARROW = ("y", "c")
NN = NY * NC
NW = NX * NZ
BF = jnp.bfloat16
F32 = jnp.float32
I32 = jnp.int32


def shifted(a, axis, n, h):
    return lax.ppermute(a, axis, [(i, (i + h) % n) for i in range(n)])


def pick(a, i, axis=0):
    return lax.dynamic_index_in_dim(a, i, axis, keepdims=False)


def iota(shape, dim):
    return lax.broadcasted_iota(I32, shape, dim)


def choose_rows(onehot, a):
    return jnp.dot(onehot.astype(BF), a, preferred_element_type=F32).astype(BF)


def places(ids, cap, per_owner):
    owner = ids // CL_DEV
    onehot = (owner[:, None] == iota((1, NW), 1)).astype(I32)
    rank = jnp.sum((jnp.cumsum(onehot, axis=0) - onehot) * onehot, axis=1)
    count = jnp.sum(onehot, axis=0)
    hot = jnp.argmax(count).astype(I32)
    short = count < per_owner
    nth = jnp.cumsum(short.astype(I32)) - short.astype(I32)
    gap = jnp.where(short, nth % per_owner, per_owner)
    n_of = rank + (rank >= jnp.sum(onehot * gap[None, :], axis=1)).astype(I32)
    surplus = rank >= per_owner
    j = rank - per_owner
    host = jnp.sum(
        jnp.where(short[None, :] & (nth[None, :] == j[:, None]), iota((1, NW), 1), 0), axis=1
    )
    place = jnp.where(surplus, (j % per_owner) * NW + host, n_of * NW + owner)
    cell = owner * cap + jnp.where(surplus, rank, n_of)
    return place, cell, hot, short, nth


SMEM = pl.BlockSpec(memory_space=pltpu.SMEM)
ANY = pl.BlockSpec(memory_space=pl.ANY)


def like(shape, dtype=BF):
    return jax.ShapeDtypeStruct(shape, dtype)


def whole(shape):
    return pl.BlockSpec(shape, lambda i: (0,) * len(shape))


def local_call(
    kernel, outs, args, after=(), smem=(), scratch=(), grid=(1,), specs=None, grant=28
):
    return pl.pallas_call(
        kernel,
        out_shape=outs,
        grid=grid,
        in_specs=[SMEM] * len(smem) + (specs or [whole(a.shape) for a in args]) + [ANY] * len(after),
        out_specs=jax.tree.map(lambda o: whole(o.shape), outs),
        scratch_shapes=list(scratch),
        compiler_params=pltpu.CompilerParams(vmem_limit_bytes=grant * 1024 * 1024),
        name=kernel.__name__,
    )(*smem, *args, *after)


def at(i, size, step):
    return pl.ds(pl.multiple_of(i * size, step), size)


def project(at_ref, *refs):
    h_refs, up, down, far = refs[:4], refs[4:8], refs[8:11], refs[11:13]
    keep, send, w_all, acc = refs[13:]
    z, y, c = at_ref[1], at_ref[2], at_ref[3]
    cols = up[0].shape[0]
    for h in range(4):
        w_all[at(lax.rem(z + NZ - h, NZ), cols, 16), :] = up[h][...]
        if h:
            w_all[at(lax.rem(z + h, NZ), cols, 16), :] = down[h - 1][...]
    across = lax.rem(z + 4, NZ) * cols
    w_all[pl.ds(pl.multiple_of(across, 16), cols // 2), :] = far[0][...]
    w_all[pl.ds(pl.multiple_of(across + cols // 2, 16), cols // 2), :] = far[1][...]
    for h in range(NX):
        acc[...] = lax.dot_general(
            h_refs[h][...], w_all[...], (((1,), (1,)), ((), ())), preferred_element_type=F32
        )
        for g in range(NY):
            n = lax.rem(y + g, NY) * NC
            keep[g, h] = acc[at(n + c, NW, 32), :].astype(BF)
            send[g, h] = acc[at(n + 1 - c, NW, 32), :].astype(BF)


def add_pair(keep, other, *outs):
    for g in range(NY):
        outs[g][...] = (keep[g].astype(F32) + other[g].astype(F32)).astype(BF)


def add_four(*refs):
    outs = refs[-NX:]
    for h in range(NX):
        total = refs[0][h].astype(F32)
        for g in range(1, NY):
            total = total + refs[g][h].astype(F32)
        outs[h][...] = total.astype(BF)


def gate(ids, token, out):
    out[...] = ids[...]


def normalize(at_ref, b0, b1, b2, b3, resid, cents, from_host, keys, extra, stream):
    x = at_ref[0]
    span = b0.shape[1]
    width = cents.shape[2]
    for h, b in enumerate((b0, b1, b2, b3)):
        where = at(lax.rem(x + h, NX), span, 128)
        stream[:, where] = resid[:, where].astype(F32) + b[...].astype(F32)
    value = stream[...]
    scale = lax.rsqrt(jnp.mean(value * value, axis=1, keepdims=True) + EPS)
    for n in range(NN):
        part = slice(n * width, (n + 1) * width)
        tail = cents[n, NW:, :].astype(F32)
        key = (stream[:, part] * scale * tail[7:8]).astype(BF)
        keys[:, part] = key
        chosen = jnp.dot(from_host[...], key, preferred_element_type=F32)
        extra[:, part] = (chosen - tail).astype(BF)


def subtract(keys, cents, filled, token, out):
    width = cents.shape[2]
    for n in range(NN):
        part = slice(n * width, (n + 1) * width)
        diff = keys[:, part].astype(F32) - cents[n, :NW, :].astype(F32)
        out[:, part] = jnp.where(filled[...] > 0, diff, 0.0).astype(BF)


def split_rows(cent, *refs):
    out = refs[-1]
    width = out.shape[2]
    for n in range(NN):
        out[n] = cent[:, n * width : (n + 1) * width]


def hold(*refs):
    pass


def later(a, *after):
    return pl.pallas_call(
        hold,
        out_shape=like(a.shape, a.dtype),
        in_specs=[ANY] * (1 + len(after)),
        out_specs=ANY,
        input_output_aliases={0: 0},
        name="later",
    )(a, *after)


def accumulate(parts, rot, acc):
    lhs = jnp.concatenate([p[...] for p in parts], axis=0)
    new = jnp.dot(lhs, rot[...], preferred_element_type=F32)

    @pl.when(pl.program_id(0) == 0)
    def _():
        acc[...] = new

    @pl.when(pl.program_id(0) > 0)
    def _():
        acc[...] += new


def rotate_extra(*refs):
    parts, (rot, chosen, out, acc) = refs[:8], refs[8:]
    accumulate(parts, rot, acc)

    @pl.when(pl.program_id(0) == pl.num_programs(0) - 1)
    def _():
        rows = acc[...].astype(BF)
        picked = jnp.dot(chosen[...], rows, preferred_element_type=F32).astype(BF)
        for g in range(NZ):
            out[g] = picked


def rotate(*refs):
    parts, (rot, chosen, out, acc) = refs[:8], refs[8:]
    accumulate(parts, rot, acc)

    @pl.when(pl.program_id(0) == pl.num_programs(0) - 1)
    def _():
        rows = acc[...].astype(BF)
        out[...] = jnp.dot(chosen[...], rows, preferred_element_type=F32)


def lay_out(at_ref, rows, *refs):
    ext, out = refs[:NX], refs[-1]
    x, hot = at_ref[0], at_ref[4]
    extra = ext[0].shape[1]
    cap = NN + extra
    for h in range(NX):
        first = lax.rem(x + h, NX) * NZ
        for g in range(NZ):
            tail = jnp.where(hot > 0, ext[h][g].astype(F32), 0.0)
            both = jnp.concatenate([rows[at(first + g, NN, 8), :], tail], axis=0)
            out[at(first + g, cap, 32), :] = both.astype(BF)


def per_device(hidden, resid, w_out, key_gain, cluster_ids, centroids, rotation):
    xi, zi, yi, ci = (lax.axis_index(a) for a in ("x", "z", "y", "c"))
    ni = yi * NC + ci
    wi = xi * NZ + zi
    tokens, width = hidden.shape
    d = width * NN
    cap = 4 * tokens // NW
    cols = w_out.shape[1]
    wide_cols = NZ * cols
    extra = cap - NN
    per_n = extra // NN

    w_t = w_out.T
    up, down = [w_t], [w_t]
    for _ in range(2):
        up.append(shifted(up[-1], "z", NZ, 1))
        down.append(shifted(down[-1], "z", NZ, -1))

    place, cell, hot, short, nth = places(cluster_ids, cap, NN)
    where_am_i = jnp.stack([xi, zi, yi, ci, (wi == hot).astype(I32)]).astype(I32)
    hidden_p = choose_rows(iota((tokens, 1), 0) == place[None, :], hidden)
    h_parts = [hidden_p] + [shifted(hidden_p, "x", NX, h) for h in (1, 2, 3)]
    up.append(shifted(later(up[2], h_parts[1]), "z", NZ, 1))
    down.append(shifted(down[2], "z", NZ, -1))
    far = [
        shifted(up[3][: cols // 2], "z", NZ, 1),
        shifted(down[3][cols // 2 :], "z", NZ, -1),
    ]

    cent_split = local_call(
        split_rows,
        like((NN, centroids.shape[0], width)),
        (centroids,),
        after=(up[1], down[1]),
    )
    cent_tile = lax.all_to_all(cent_split, NARROW, 0, 0, tiled=True).reshape(-1, width)

    cell_of = cell[:, None] == iota((1, NW * cap), 1)
    send_ids = jnp.sum(jnp.where(cell_of, cluster_ids[:, None] + 1, 0), axis=0) - 1
    send_ids = later(send_ids.reshape(NW, cap), cent_tile, *far, h_parts[2], h_parts[1])
    got_ids = lax.all_to_all(send_ids, WIDE, 0, 0, tiled=True)

    block = like((NY, NX, NW, wide_cols))
    keep, send = local_call(
        project,
        (block, block),
        (*h_parts, *up, *down[1:], *far),
        smem=(where_am_i,),
        scratch=[pltpu.VMEM((wide_cols, width), BF), pltpu.VMEM((tokens, wide_cols), F32)],
        grant=58,
    )
    pairs = local_call(
        add_pair, [like((NX, NW, wide_cols))] * NY, (keep, shifted(send, "c", NC, 1)), grant=58
    )

    n_of = ((yi - iota((NC, NY, 1), 1)) % NY) * NC + (ci + iota((NC, NY, 1), 0)) % NC
    filled = (pick(got_ids, ni, 1) >= 0).astype(F32)[:, None]
    ext_j = (iota((NC, NY, 8), 2) * NN + n_of).reshape(1, -1)
    choose_ext = (ext_j == iota((extra, 1), 0)).astype(BF)
    gap = jnp.min(jnp.where(got_ids[:, :NN] < 0, iota((1, NN), 1), NN), axis=1)
    rank = iota((1, NN), 1)
    from_n = (rank + (rank >= gap[:, None]).astype(I32)).reshape(-1, 1)
    from_s = iota((NW, NN), 0).reshape(-1, 1)
    row_n = jnp.broadcast_to(n_of, (NC, NY, NW)).reshape(1, -1)
    row_s = iota((NC, NY, NW), 2).reshape(1, -1)
    chosen = ((from_n == row_n) & (from_s == row_s)).astype(BF)

    sums = local_call(
        add_four,
        [like((NW, wide_cols))] * NX,
        (pairs[0], *[shifted(pairs[g], "y", NY, g) for g in (1, 2, 3)]),
    )

    local = jnp.where(got_ids >= 0, got_ids - wi * CL_DEV, -1)
    local = local_call(gate, like(local.shape, I32), (local,), after=(keep,))
    clusters = iota((1, CL_DEV), 1)
    cent_own = choose_rows(local[:, :NN].T.reshape(-1, 1) == clusters, cent_tile)
    cent_out = choose_rows(local[:, NN:].reshape(-1, 1) == clusters, cent_tile)
    cent_in = lax.all_to_all(cent_out.reshape(NW, extra, width), WIDE, 0, 0, tiled=True)
    cent_in = pick(later(cent_in, sums[1]), hot)
    cent_pre = jnp.concatenate(
        [
            cent_own.reshape(NN, NW, width),
            cent_in.reshape(per_n, NN, width).transpose(1, 0, 2),
            jnp.broadcast_to(key_gain, (NN, 8 - per_n, width)),
        ],
        axis=1,
    )
    cents = lax.all_to_all(cent_pre, NARROW, 0, 0, tiled=True)

    own_place = ni * NW + iota((NW, 1), 0) == place[None, :]
    resid_rows = choose_rows(own_place, resid)

    q = iota((8, 1), 0)
    from_host = (short[None, :] & (nth[None, :] == q * NN + ni) & (q < per_n)).astype(BF)
    keys, res_extra = local_call(
        normalize,
        (like((NW, d)), like((8, d))),
        (
            sums[0],
            *[shifted(sums[h], "x", NX, -h) for h in (1, 2, 3)],
            resid_rows,
            cents,
            from_host,
        ),
        smem=(where_am_i,),
        scratch=[pltpu.VMEM((NW, d), F32)],
        grant=58,
    )

    got = lax.all_to_all(keys.reshape(NW, NN, width), WIDE, 0, 0, tiled=True).reshape(NW, d)
    steps = 4
    rot_spec = pl.BlockSpec((d // steps, width), lambda k: (k, 0))

    def row_specs(rows):
        return [pl.BlockSpec((rows, d // steps), lambda k: (0, k))] * NN

    pieces = [res_extra] + [shifted(res_extra, "y", NY, h) for h in (1, 2, 3)]
    pieces = pieces + [shifted(p, "c", NC, 1) for p in pieces]
    ext = local_call(
        rotate_extra,
        like((NZ, extra, width)),
        (*pieces, rotation, choose_ext),
        scratch=[pltpu.VMEM((NN * 8, width), F32)],
        grid=(steps,),
        specs=row_specs(8) + [rot_spec, whole(choose_ext.shape)],
    )
    residual = local_call(subtract, like((NW, d)), (got, cents, filled), after=(ext,))
    parts = [residual] + [shifted(residual, "y", NY, h) for h in (1, 2, 3)]
    parts = parts + [shifted(p, "c", NC, 1) for p in parts]
    ext = lax.all_to_all(ext, "z", 0, 0, tiled=True)
    ext = [ext] + [shifted(ext, "x", NX, -h) for h in range(1, NX)]

    rotated = local_call(
        rotate,
        like((NN * NW, width), F32),
        (*parts, rotation, chosen),
        scratch=[pltpu.VMEM((NN * NW, width), F32)],
        grid=(steps,),
        specs=row_specs(NW) + [rot_spec, whole(chosen.shape)],
    )
    return local_call(
        lay_out, like((NW * cap, width)), (rotated, *ext), smem=(where_am_i,), grant=58
    )


def solution(mesh):
    grid = Mesh(mesh.devices.reshape(NX, NZ, NY, NC), ("x", "z", "y", "c"))
    placed = (
        P(WIDE, NARROW),
        P(WIDE, None),
        P(NARROW, WIDE),
        P(NARROW),
        P(WIDE),
        P(WIDE + NARROW, None),
        P(None, NARROW),
    )
    return jax.shard_map(
        per_device, mesh=grid, in_specs=placed, out_specs=P(WIDE, NARROW), check_vma=False
    )
```
